32 devices in a mesh: dp: 16 (over z, y, core), mp: 2 (over x).
Axes of the slice: x: 2, y: 2, z: 4, core: 2. Of those that a mesh axis runs over, the one named last changes fastest.
Arguments:
- inputs: bfloat16 [3, 1024, 2560], P(None, 'dp'), may hold values from -6 to 6
- gain_attn: float32 [2560], replicated, may hold values from 0.5 to 1.5
- w_query: bfloat16 [2560, 2560], P('dp', 'mp'), may hold values from -0.125 to 0.125
- w_keyval: bfloat16 [2560, 512], P('dp'), may hold values from -0.125 to 0.125
- w_output: bfloat16 [2560, 2560], P('mp', 'dp'), may hold values from -0.3125 to 0.3125
- gain_mlp: float32 [2560], replicated, may hold values from 0.5 to 1.5
- w_gate: bfloat16 [2560, 7680], P('dp', 'mp'), may hold values from -0.125 to 0.125
- b_gate: float32 [7680], P('mp'), may hold values from -3 to 3
- w_up: bfloat16 [2560, 7680], P('dp', 'mp'), may hold values from -0.125 to 0.125
- b_up: float32 [7680], P('mp'), may hold values from -3 to 3
- w_down: bfloat16 [7680, 2560], P('mp', 'dp'), may hold values from -0.125 to 0.125
- b_down: float32 [2560], replicated, may hold values from -3 to 3
- segment_ids: int32 [3, 16, 64], P(None, 'dp'), may hold values from 0 to 7, never falling along the last dimension, each value on 1 to 32 neighbouring positions
- cotangent: bfloat16 [3, 1024, 2560], P(None, 'dp'), may hold values from -12 to 12
Outputs:
- outputs: bfloat16 [3, 1024, 2560], P(None, 'dp')
- inputs_grad: bfloat16 [3, 1024, 2560], P(None, 'dp')
- gain_attn_grad: float32 [2560], replicated
- w_query_grad: float32 [2560, 2560], P('dp', 'mp')
- w_keyval_grad: float32 [2560, 512], P('dp')
- w_output_grad: float32 [2560, 2560], P('mp', 'dp')
- gain_mlp_grad: float32 [2560], replicated
- w_gate_grad: float32 [2560, 7680], P('dp', 'mp')
- b_gate_grad: float32 [7680], P('mp')
- w_up_grad: float32 [2560, 7680], P('dp', 'mp')
- b_up_grad: float32 [7680], P('mp')
- w_down_grad: float32 [7680, 2560], P('mp', 'dp')
- b_down_grad: float32 [2560], replicated
The draws below stay inside these ranges and needn't reach their ends.
Inputs may be any that keep to these rules, and one draw needn't show every extreme that they name: `segment_ids`: ids never fall within a block of 64 tokens; a sequence holds 1 to 32 tokens and some sequence holds 32.
All inputs are finite; a program needn't handle non-finite values.
Results may differ from the reference program's by a relative error of at most 0.014.
Values may be sent and summed in bfloat16 or wider, within the bound.
No kernel may reach another device: no remote copies, remote signals or barrier semaphores. Data moves between devices by JAX's collectives and lax.ppermute only.
A program may use at most 384 MiB of HBM per device.

```python
import math
import jax
import jax.numpy as jnp
import numpy as np
from jax import lax

D = 2560
HEADS = 10
HD = 256
FF = 7680
TOK_MB = 64
MB = 3
SEGS = 8
SEG_MOST = 32
TOKENS = 1024
N_DP = 16


def draw_cotangent(key, part):
    row_index = jnp.arange(TOKENS, dtype=jnp.float32)
    ramp_scale = (1.0 + 2.0 * row_index / max(TOKENS - 1, 1))[None, :, None]
    base_draw = jnp.clip(jax.random.normal(key, (MB, TOKENS, D), jnp.float32), -4.0, 4.0)
    return (base_draw * ramp_scale).astype(jnp.bfloat16)


def steps_of(own_key, dims, split, least, largest):
    def one(position, shards_of):
        draws = jax.random.uniform(jax.random.fold_in(jax.random.fold_in(own_key, 6), position), (shards_of,), jnp.float32, least / len(split), largest / len(split))
        return jnp.repeat(jnp.exp(draws), dims[position] // shards_of).reshape((-1,) + (1,) * (len(dims) - position - 1))

    level = one(*split[0])
    for cut in split[1:]:
        level = level * one(*cut)
    return level


def length_profile(number_of, total, reach, slope):
    weights = [(1 << 20) // math.isqrt(standing ** slope) + 1 for standing in range(2, number_of + 1)]
    rest, given = total - reach - (number_of - 1), [1] * (number_of - 1)
    while rest > 0:
        candidates = [i for i in range(number_of - 1) if given[i] < reach]
        mass, left = sum([weights[i] for i in candidates]), rest
        for i in candidates:
            addition = min(reach - given[i], max(1, left * weights[i] // mass), rest)
            given[i] = given[i] + addition
            rest = rest - addition
    return np.array([reach] + given)


def ragged(own_key, amount, total, bound, lean):
    if amount == 2:
        one = jax.random.randint(own_key, (), max(1, total - bound), min(bound, total - 1) + 1)
        return jnp.stack([one, total - one])
    tallies = jnp.asarray(length_profile(amount, total, bound, lean), jnp.int32)
    couples = (amount - 1) // 2
    source_of, taker = tallies[1:1 + 2 * couples:2], tallies[2:2 + 2 * couples:2]
    slack = jnp.minimum(source_of - 1, bound - taker)
    moved = jax.random.randint(jax.random.fold_in(own_key, 1), (couples,), 0, 1 << 20) % (slack + 1)
    tallies = tallies.at[1:1 + 2 * couples:2].set(source_of - moved).at[2:2 + 2 * couples:2].set(taker + moved)
    return tallies[jax.random.permutation(jax.random.fold_in(own_key, 2), amount)]


def noise(own_key, shape, width, most, shards=(), kind=jnp.bfloat16):
    array = jax.random.normal(own_key, shape, jnp.float32) * width
    if len(shards) > 0:
        array = steps_of(own_key, shape, shards, -0.22, 0.18) * array
    return jnp.clip(array, min=-most, max=most).astype(kind)


def setup_inputs(seed: int = 0) -> dict:
    key_list = jax.random.split(jax.random.key(seed), 15)
    return {
        "inputs": noise(key_list[0], (MB, TOKENS, D), 1.0, 6.0, ((1, 16),)),
        "gain_attn": jnp.clip(1.0 + 0.1 * jax.random.normal(key_list[1], (D,), jnp.float32), 0.5, 1.5),
        "w_query": noise(key_list[2], (D, HEADS * HD), D ** -0.5, 0.125, ((0, 16), (1, 2))),
        "w_keyval": noise(key_list[3], (D, 2 * HD), D ** -0.5, 0.125, ((0, 16),)),
        "w_output": noise(key_list[4], (HEADS * HD, D), (HEADS * HD // 8) ** -0.5, 0.3125, ((0, 2), (1, 16))),
        "gain_mlp": jnp.clip(1.0 + 0.1 * jax.random.normal(key_list[5], (D,), jnp.float32), 0.5, 1.5),
        "w_gate": noise(key_list[6], (D, FF), D ** -0.5, 0.125, ((0, 16), (1, 2))),
        "b_gate": noise(key_list[7], (FF,), 0.5, 3.0, ((0, 2),), jnp.float32),
        "w_up": noise(key_list[8], (D, FF), D ** -0.5, 0.125, ((0, 16), (1, 2))),
        "b_up": noise(key_list[9], (FF,), 0.5, 3.0, ((0, 2),), jnp.float32),
        "w_down": noise(key_list[10], (FF, D), (FF // 4) ** -0.5, 0.125, ((0, 2), (1, 16))),
        "b_down": noise(key_list[11], (D,), 0.5, 3.0, (), jnp.float32),
        "segment_ids": jax.vmap(lambda own: jnp.searchsorted(jnp.cumsum(ragged(own, SEGS, TOK_MB, SEG_MOST, 2)), jnp.arange(TOK_MB), side="right"))(jax.random.split(key_list[12], MB * N_DP)).reshape((MB, N_DP, TOK_MB)).astype(jnp.int32),
        "cotangent": draw_cotangent(jax.random.fold_in(key_list[14], 71), 0),
    }


EPS = 1e-06
HIGH = lax.Precision.HIGHEST

@jax.custom_vjp
def low(v):
    return lax.optimization_barrier(v.astype(jnp.bfloat16)).astype(jnp.float32)

@jax.custom_vjp
def low_back(v):
    return v

def low_keep(v):
    return (low(v), None)

def low_pass(kept, grad):
    return (grad,)

def back_keep(v):
    return (v, None)

def back_low(kept, grad):
    return (low(grad),)
low.defvjp(low_keep, low_pass)
low_back.defvjp(back_keep, back_low)

def matmul(left, right):
    return jnp.dot(left, right, precision=HIGH, preferred_element_type=jnp.float32)

def positions(segment):
    count = segment.shape[0]
    index = jnp.arange(count, dtype=jnp.int32)
    fresh = jnp.concatenate([jnp.ones((1,), jnp.bool_), segment[1:] != segment[:-1]])
    starts = lax.cummax(jnp.where(fresh, index, 0), axis=0)
    return (index - starts).astype(jnp.float32)

def rotate(tensor, offsets, direction):
    quarter = tensor.shape[-1] // 4
    freqs = 10000.0 ** (-jnp.arange(quarter, dtype=jnp.float32) / quarter)
    angle = offsets[:, None] * freqs[None, :]
    cosine = jnp.cos(angle)[:, None, :]
    sine = direction * jnp.sin(angle)[:, None, :]
    front_half = tensor[..., :quarter]
    back_half = tensor[..., quarter:2 * quarter]
    return jnp.concatenate([front_half * cosine - back_half * sine, back_half * cosine + front_half * sine, tensor[..., 2 * quarter:]], axis=-1)

def normalize(values, gain):
    factor = lax.rsqrt(lax.optimization_barrier(jnp.mean(values * values, axis=-1, keepdims=True)) + EPS)
    return values * factor * gain

def forward(params, hidden_in, segment):
    gain_attn, w_query, w_keyval, w_output, gain_mlp, w_gate, b_gate, w_up, b_up, w_down, b_down = params
    length = hidden_in.shape[0]
    offsets = positions(segment)
    normed = low(normalize(hidden_in, gain_attn))
    queries = low_back(matmul(normed, w_query))
    keyval = matmul(normed, w_keyval)
    keys_in = low_back(keyval[:, :HD])
    values_in = low(low_back(keyval[:, HD:]))
    rot_query = low(rotate(queries.reshape(length, HEADS, HD), offsets, 1.0) * HD ** (-0.5))
    rot_key = low(rotate(keys_in[:, None, :], offsets, 1.0)[:, 0, :])
    scores = low_back(jnp.einsum('thd,sd->hts', rot_query, rot_key, precision=HIGH))
    index = jnp.arange(length, dtype=jnp.int32)
    allowed = (segment[:, None] == segment[None, :]) & (index[None, :] <= index[:, None])
    scores = jnp.where(allowed[None], scores, -1e+30)
    probs = low(jax.nn.softmax(scores, axis=-1))
    mixed = jnp.einsum('hts,sd->thd', probs, values_in, precision=HIGH).reshape(length, HEADS * HD)
    mixed = low(low_back(mixed))
    attended = low_back(matmul(mixed, w_output))
    residual = hidden_in + attended
    normed_two = low(normalize(residual, gain_mlp))
    gate_pre = low_back(matmul(normed_two, w_gate) + b_gate)
    up_pre = low_back(matmul(normed_two, w_up) + b_up)
    inner = low(jax.nn.gelu(gate_pre, approximate=True) * up_pre)
    branch = low_back(matmul(inner, w_down) + b_down)
    return residual + branch

def reference(inputs, gain_attn, w_query, w_keyval, w_output, gain_mlp, w_gate, b_gate, w_up, b_up, w_down, b_down, segment_ids, cotangent):
    params = tuple((item.astype(jnp.float32) for item in (gain_attn, w_query, w_keyval, w_output, gain_mlp, w_gate, b_gate, w_up, b_up, w_down, b_down)))
    blocks = MB * N_DP
    hidden_all = inputs.astype(jnp.float32).reshape(blocks, TOK_MB, D)
    segment_all = segment_ids.reshape(blocks, TOK_MB)
    cot_all = cotangent.astype(jnp.float32).reshape(blocks, TOK_MB, D)

    def one_block(totals, item):
        hidden_in, segment, cot_block = item
        output, pullback = jax.vjp(lambda prm, hin: forward(prm, hin, segment), params, hidden_in)
        grads_p, grad_in = pullback(cot_block)
        return (jax.tree.map(jnp.add, totals, grads_p), (output, grad_in))
    zeros = jax.tree.map(jnp.zeros_like, params)
    totals, (outputs, grads_in) = lax.scan(one_block, zeros, (hidden_all, segment_all, cot_all))
    outputs = outputs.reshape(MB, TOKENS, D).astype(jnp.bfloat16)
    grads_in = grads_in.reshape(MB, TOKENS, D).astype(jnp.bfloat16)
    return (outputs, grads_in, totals[0], totals[1], totals[2], totals[3], totals[4], totals[5], totals[6], totals[7], totals[8], totals[9], totals[10])
```

```python
from functools import partial

import jax
import jax.numpy as jnp
from jax import lax
from jax.sharding import PartitionSpec as P

EPS = 1e-06
F32 = jnp.float32
BF16 = jnp.bfloat16


def positions(segment):
    count = segment.shape[0]
    index = jnp.arange(count, dtype=jnp.int32)
    fresh = jnp.concatenate([jnp.ones((1,), jnp.bool_), segment[1:] != segment[:-1]])
    starts = lax.cummax(jnp.where(fresh, index, 0), axis=0)
    return (index - starts).astype(F32)


def rotate(tensor, cosine, sine):
    quarter = cosine.shape[-1]
    front_half = tensor[..., :quarter]
    back_half = tensor[..., quarter : 2 * quarter]
    return jnp.concatenate(
        [
            front_half * cosine - back_half * sine,
            back_half * cosine + front_half * sine,
            tensor[..., 2 * quarter :],
        ],
        axis=-1,
    )


def inv_root(values):
    return lax.rsqrt(jnp.mean(values * values, axis=-1, keepdims=True) + EPS)


def norm_back(values, factor, gain, grad_norm):
    scaled = gain * grad_norm
    return factor * scaled - values * factor**3 * jnp.mean(scaled * values, axis=-1, keepdims=True)


def mm(left, right):
    return jnp.dot(left, right, preferred_element_type=F32)


def mm_nt(left, right):
    return lax.dot_general(left, right, (((1,), (1,)), ((), ())), preferred_element_type=F32)


def mm_tn(left, right):
    return lax.dot_general(left, right, (((0,), (0,)), ((), ())), preferred_element_type=F32)


class Grid:
    def __init__(self, total):
        self.z_count = total // 4
        spots = [(z, y, c) for z in range(self.z_count) for y in range(2) for c in range(2)]
        at = lambda z, y, c: (z * 2 + y) * 2 + c
        self.swap_y = [(at(z, y, c), at(z, 1 - y, c)) for z, y, c in spots]
        self.swap_c = [(at(z, y, c), at(z, y, 1 - c)) for z, y, c in spots]
        self.ring = [(at(z, y, c), at((z + 1) % self.z_count, y, c)) for z, y, c in spots]
        self.flips = []
        step = 1
        while step < self.z_count:
            self.flips.append([(at(z, y, c), at(z ^ step, y, c)) for z, y, c in spots])
            step *= 2
        self.lines = [
            [at(z, y, c) for z in range(self.z_count)] for y in range(2) for c in range(2)
        ]
        self.sheets = [
            [at(z, y, c) for z in range(self.z_count) for c in range(2)] for y in range(2)
        ]
        index = lax.axis_index("dp")
        self.c = index % 2
        self.y = (index // 2) % 2
        self.z = index // 4
        self.x = lax.axis_index("mp")

    def over_y(self, value):
        return lax.ppermute(value, "dp", self.swap_y)

    def over_c(self, value):
        return lax.ppermute(value, "dp", self.swap_c)

    def over_x(self, value):
        return lax.ppermute(value, "mp", [(0, 1), (1, 0)])

    def next_z(self, value):
        return lax.ppermute(value, "dp", self.ring)

    def sum_dp(self, value):
        value = value + self.over_c(value)
        value = value + self.over_y(value)
        for flip in self.flips:
            value = value + lax.ppermute(value, "dp", flip)
        return value


def pair(index, mine, other, axis):
    return jnp.where(
        index == 0, jnp.stack([mine, other], axis=axis), jnp.stack([other, mine], axis=axis)
    )


def take(value, index, axis):
    return lax.dynamic_index_in_dim(value, index, axis, keepdims=False)


def gather_rows(grid, shard):
    rows, width = shard.shape
    count = grid.z_count
    whole = jnp.zeros((count, 4 * rows, width), shard.dtype)
    slot = shard
    for step in range(count):
        across = grid.over_y(slot)
        coming = grid.next_z(slot) if step + 1 < count else None
        lines = pair(grid.y, slot, across, 0)
        beside = grid.over_c(lines)
        block = pair(grid.c, lines, beside, 1).reshape(1, 4 * rows, width)
        place = lax.rem(grid.z - step + count, count)
        whole = lax.dynamic_update_slice(whole, block, (place, 0, 0))
        slot = coming
    return whole.reshape(count * 4 * rows, width)


def scatter_rows(grid, whole):
    count = grid.z_count
    rows = whole.shape[0] // (4 * count)
    width = whole.shape[1]
    parts = whole.reshape(count, 2, 2, rows, width)
    got = grid.over_c(take(parts, 1 - grid.c, 2).astype(BF16))
    parts = take(parts, grid.c, 2).astype(F32) + got.astype(F32)
    got = grid.over_y(take(parts, 1 - grid.y, 1).astype(BF16))
    parts = (take(parts, grid.y, 1) + got.astype(F32)).astype(BF16)
    got = lax.all_to_all(parts, "dp", 0, 0, axis_index_groups=grid.lines, tiled=True)
    return jnp.sum(got.astype(F32), axis=0)


def spread_columns(grid, shard):
    rows, width = shard.shape
    count = grid.z_count
    mine = lax.all_to_all(shard, "dp", 1, 0, axis_index_groups=grid.sheets, tiled=True)
    mine = mine.reshape(count, 2 * rows, width // (2 * count))
    other = grid.over_y(mine)
    return pair(grid.y, mine, other, 1).reshape(4 * count * rows, width // (2 * count))


def collect_columns(grid, whole):
    count = grid.z_count
    rows = whole.shape[0] // (4 * count)
    width = whole.shape[1]
    parts = whole.reshape(count, 2, 2 * rows, width)
    got = grid.over_y(take(parts, 1 - grid.y, 1).astype(BF16))
    parts = (take(parts, grid.y, 1).astype(F32) + got.astype(F32)).astype(BF16)
    parts = parts.reshape(2 * count * rows, width)
    return lax.all_to_all(parts, "dp", 0, 1, axis_index_groups=grid.sheets, tiled=True).astype(F32)


def gather_tokens(grid, half):
    count = grid.z_count
    whole = jnp.zeros((count, 2, 2) + half.shape, half.dtype)
    slot = half
    for step in range(count):
        across = grid.over_x(slot)
        coming = grid.next_z(slot) if step + 1 < count else None
        both = pair(grid.x, slot, across, 0)
        beside = grid.over_c(both)
        block = pair(grid.c, both, beside, 0)[None]
        place = lax.rem(grid.z - step + count, count)
        whole = lax.dynamic_update_slice(whole, block, (place,) + (0,) * (block.ndim - 1))
        slot = coming
    return whole.reshape(-1, half.shape[-1])


def scatter_tokens(grid, whole, tokens):
    count = grid.z_count
    parts = whole.reshape(count, 2, 2, tokens, whole.shape[-1])
    got = grid.over_c(take(parts, 1 - grid.c, 1))
    parts = take(parts, grid.c, 1).astype(F32) + got.astype(F32)
    got = grid.over_x(take(parts, 1 - grid.x, 1).astype(BF16))
    parts = (take(parts, grid.x, 1) + got.astype(F32)).astype(BF16)
    got = lax.all_to_all(parts, "dp", 0, 0, axis_index_groups=grid.lines, tiled=True)
    return jnp.sum(got.astype(F32), axis=0)


def shards(
    inputs,
    gain_attn,
    w_query,
    w_keyval,
    w_output,
    gain_mlp,
    w_gate,
    b_gate,
    w_up,
    b_up,
    w_down,
    b_down,
    segment_ids,
    cotangent,
    total,
):
    grid = Grid(total)
    count = grid.z_count
    micro, length, width = inputs.shape
    tokens = micro * length
    head_dim = w_keyval.shape[1] // 2
    heads = w_query.shape[1] // head_dim
    scale = head_dim ** (-0.5)

    def halves(value):
        value = value.reshape(micro, 2, length // 2, value.shape[-1])
        return tuple(take(value, i, 1).reshape(tokens // 2, -1) for i in (grid.x, 1 - grid.x))

    def join(mine, other):
        shape = (micro, length // 2, mine.shape[-1])
        return pair(grid.x, mine.reshape(shape), other.reshape(shape), 1).reshape(tokens, -1)

    keyval_half = lax.dynamic_slice_in_dim(w_keyval, grid.x * head_dim, head_dim, 1)
    w_qkv = gather_rows(grid, jnp.concatenate([w_query, keyval_half], axis=1))
    w_out = gather_rows(grid, w_output.T)
    wq, wkv = w_qkv[:, : heads * head_dim], w_qkv[:, heads * head_dim :]

    wg = spread_columns(grid, w_gate)
    wu = spread_columns(grid, w_up)
    wd = spread_columns(grid, w_down.T)
    hidden = wg.shape[1]
    place = (2 * grid.z + grid.c) * hidden
    bg = lax.dynamic_slice_in_dim(b_gate, place, hidden, 0)
    bu = lax.dynamic_slice_in_dim(b_up, place, hidden, 0)

    segment = segment_ids.reshape(micro, length)
    offsets = jax.vmap(positions)(segment).reshape(tokens)
    quarter = head_dim // 4
    freqs = 10000.0 ** (-jnp.arange(quarter, dtype=F32) / quarter)
    angle = offsets[:, None] * freqs[None, :]
    cosine, sine = jnp.cos(angle), jnp.sin(angle)
    index = jnp.arange(tokens, dtype=jnp.int32)
    seg = segment.reshape(tokens)
    allowed = (
        (seg[:, None] == seg[None, :])
        & (index[:, None] // length == index[None, :] // length)
        & (index[None, :] <= index[:, None])
    )
    hidden_x = inputs.reshape(tokens, width).astype(F32)
    factor_one = inv_root(hidden_x)
    normed = (hidden_x * factor_one * gain_attn).astype(BF16)
    queries = mm(normed, wq).reshape(tokens, heads, head_dim).transpose(1, 0, 2)
    rot_query = (rotate(queries, cosine, sine) * scale).astype(BF16)
    rot_query = rot_query.reshape(heads * tokens, head_dim)
    keyval = mm(normed, wkv)
    keyval = jnp.where(grid.x == 0, rotate(keyval, cosine, sine), keyval).astype(BF16)
    keyval_other = grid.over_x(keyval)
    rot_key = jnp.where(grid.x == 0, keyval, keyval_other)
    values_in = jnp.where(grid.x == 0, keyval_other, keyval)
    scores = mm_nt(rot_query, rot_key).reshape(heads, tokens, tokens)
    scores = jnp.where(allowed[None], scores, -1e30)
    row_max = jnp.max(scores, axis=-1, keepdims=True)
    expon = jnp.exp(scores - row_max)
    row_total = jnp.sum(expon, axis=-1, keepdims=True)
    probs = expon / row_total
    probs_b = probs.astype(BF16).reshape(heads * tokens, tokens)
    mixed = mm(probs_b, values_in).reshape(heads, tokens, head_dim)
    mixed_b = mixed.astype(BF16).transpose(1, 0, 2).reshape(tokens, heads * head_dim)
    attended = mm_nt(mixed_b, w_out)
    mine, other = halves(attended)
    attended = mine + grid.over_x(other.astype(BF16)).astype(F32)
    x_half = halves(hidden_x)[0]
    residual = x_half + attended
    factor_two = inv_root(residual)
    normed_two = (residual * factor_two * gain_mlp).astype(BF16)

    dy_half = halves(cotangent.reshape(tokens, width))[0]
    dy_all = gather_tokens(grid, dy_half)
    normed_all = gather_tokens(grid, normed_two)
    gate_pre = mm(normed_all, wg) + bg
    up_pre = mm(normed_all, wu) + bu
    gelu_out, gelu_pull = jax.vjp(partial(jax.nn.gelu, approximate=True), gate_pre)
    inner_b = (gelu_out * up_pre).astype(BF16)
    branch_all = mm_nt(inner_b, wd).astype(BF16)
    grad_inner = mm(dy_all, wd)
    grad_gate = gelu_pull(grad_inner * up_pre)[0].astype(BF16)
    grad_up = (grad_inner * gelu_out).astype(BF16)
    grad_norm_all = (mm_nt(grad_gate, wg) + mm_nt(grad_up, wu)).astype(BF16)
    grad_norm_two = scatter_tokens(grid, grad_norm_all, tokens // 2)
    branch = scatter_tokens(grid, branch_all, tokens // 2) + b_down
    outputs = (residual + branch).astype(BF16)
    outputs = join(outputs, grid.over_x(outputs))
    down_grad = collect_columns(grid, mm_tn(dy_all, inner_b)).T
    gate_grad = collect_columns(grid, mm_tn(normed_all, grad_gate))
    up_grad = collect_columns(grid, mm_tn(normed_all, grad_up))

    grad_out = dy_half.astype(F32)
    gain_mlp_term = jnp.sum(grad_norm_two * residual * factor_two, axis=0)
    grad_resid = grad_out + norm_back(residual, factor_two, gain_mlp, grad_norm_two)
    grad_resid_b = grad_resid.astype(BF16)
    grad_resid_b = join(grad_resid_b, grid.over_x(grad_resid_b))
    out_grad = scatter_rows(grid, mm_tn(grad_resid_b, mixed_b)).T
    grad_mixed = mm(grad_resid_b, w_out).astype(BF16)
    grad_mixed = grad_mixed.reshape(tokens, heads, head_dim).transpose(1, 0, 2)
    grad_mixed = grad_mixed.reshape(heads * tokens, head_dim)
    grad_values = mm_tn(probs_b, grad_mixed)
    grad_probs = mm_nt(grad_mixed, values_in).reshape(heads, tokens, tokens)
    row_delta = jnp.sum(probs * grad_probs, axis=-1, keepdims=True)
    grad_scores = (probs * (grad_probs - row_delta)).astype(BF16)
    grad_scores = grad_scores.reshape(heads * tokens, tokens)
    grad_rq = mm(grad_scores, rot_key).reshape(heads, tokens, head_dim) * scale
    grad_query = rotate(grad_rq, cosine, -sine).astype(BF16)
    grad_query = grad_query.transpose(1, 0, 2).reshape(tokens, heads * head_dim)
    grad_key = rotate(mm_tn(grad_scores, rot_query), cosine, -sine)
    grad_own = jnp.where(grid.x == 0, grad_key, grad_values)
    grad_other = jnp.where(grid.x == 0, grad_values, grad_key)
    grad_keyval = (grad_own + grid.over_x(grad_other)).astype(BF16)
    grad_qkv = jnp.concatenate([grad_query, grad_keyval], axis=1)
    qkv_grad = scatter_rows(grid, mm_tn(normed, grad_qkv))
    mine, other = halves(mm_nt(grad_qkv, w_qkv))
    grad_normed = mine + grid.over_x(other.astype(BF16)).astype(F32)
    factor_half = halves(factor_one)[0]
    gain_attn_term = jnp.sum(grad_normed * x_half * factor_half, axis=0)
    grad_input = grad_resid + norm_back(x_half, factor_half, gain_attn, grad_normed)
    grad_input = grad_input.astype(BF16)
    grad_input = join(grad_input, grid.over_x(grad_input))
    query_grad = qkv_grad[:, : heads * head_dim]
    keyval_grad = qkv_grad[:, heads * head_dim :]
    keyval_grad = pair(grid.x, keyval_grad, grid.over_x(keyval_grad), 1)
    keyval_grad = keyval_grad.reshape(keyval_grad.shape[0], 2 * head_dim)

    wide = jnp.zeros((2, b_gate.shape[0]), F32)
    bias = jnp.stack(
        [jnp.sum(grad_gate.astype(F32), axis=0), jnp.sum(grad_up.astype(F32), axis=0)]
    )
    wide = lax.dynamic_update_slice(wide, bias, (0, place)).reshape(-1)
    bias_down_term = jnp.sum(grad_out, axis=0)
    early = jnp.concatenate([gain_mlp_term, bias_down_term])
    early = jnp.concatenate([early + grid.over_x(early), wide])
    early = grid.sum_dp(early)
    gain_attn_grad = gain_attn_term + grid.over_x(gain_attn_term)
    gain_attn_grad = grid.sum_dp(gain_attn_grad)
    ffn = b_gate.shape[0]
    return (
        outputs.reshape(inputs.shape),
        grad_input.reshape(inputs.shape),
        gain_attn_grad,
        query_grad,
        keyval_grad,
        out_grad,
        early[:width],
        gate_grad,
        early[2 * width : 2 * width + ffn],
        up_grad,
        early[2 * width + ffn :],
        down_grad,
        early[width : 2 * width],
    )


def solution(mesh):
    in_specs = (
        P(None, "dp", None),
        P(),
        P("dp", "mp"),
        P("dp", None),
        P("mp", "dp"),
        P(),
        P("dp", "mp"),
        P("mp"),
        P("dp", "mp"),
        P("mp"),
        P("mp", "dp"),
        P(),
        P(None, "dp", None),
        P(None, "dp", None),
    )
    out_specs = (
        P(None, "dp", None),
        P(None, "dp", None),
        P(),
        P("dp", "mp"),
        P("dp", None),
        P("mp", "dp"),
        P(),
        P("dp", "mp"),
        P("mp"),
        P("dp", "mp"),
        P("mp"),
        P("mp", "dp"),
        P(),
    )
    body = partial(shards, total=mesh.shape["dp"])
    return jax.shard_map(body, mesh=mesh, in_specs=in_specs, out_specs=out_specs, check_vma=False)
```

```python
import math
from functools import partial

import jax
import jax.numpy as jnp
from jax import lax
from jax.experimental import pallas as pl
from jax.experimental.pallas import tpu as pltpu
from jax.sharding import PartitionSpec as P

EPS = 1e-06
F32 = jnp.float32
BF16 = jnp.bfloat16
DEPTH = {"x": 1, "y": 1, "z": 2}
VMEM = 48 * 2**20
GELU_A, GELU_B = math.sqrt(2.0 / math.pi), 0.044715


def positions(segment):
    count = segment.shape[0]
    index = jnp.arange(count, dtype=jnp.int32)
    fresh = jnp.concatenate([jnp.ones((1,), jnp.bool_), segment[1:] != segment[:-1]])
    starts = lax.cummax(jnp.where(fresh, index, 0), axis=0)
    return (index - starts).astype(F32)


def inv_root(values):
    return lax.rsqrt(jnp.mean(values * values, axis=-1, keepdims=True) + EPS)


def norm_back(values, factor, gain, grad_norm):
    scaled = gain * grad_norm
    return factor * scaled - values * factor**3 * jnp.mean(scaled * values, axis=-1, keepdims=True)


def mm(left, right):
    return jnp.dot(left, right, preferred_element_type=F32)


def mm_nt(left, right):
    return lax.dot_general(left, right, (((1,), (1,)), ((), ())), preferred_element_type=F32)


def mm_tn(left, right):
    return lax.dot_general(left, right, (((0,), (0,)), ((), ())), preferred_element_type=F32)


def after(value, *earlier):
    return lax.optimization_barrier((value,) + earlier)[0]


class Grid:
    def __init__(self, total):
        self.z_count = total // 4
        spots = [(z, y, c) for z in range(self.z_count) for y in range(2) for c in range(2)]
        at = lambda z, y, c: (z * 2 + y) * 2 + c
        self.swap_y = [(at(z, y, c), at(z, 1 - y, c)) for z, y, c in spots]
        self.swap_c = [(at(z, y, c), at(z, y, 1 - c)) for z, y, c in spots]
        self.ring = [(at(z, y, c), at((z + 1) % self.z_count, y, c)) for z, y, c in spots]
        self.flips = []
        step = 1
        while step < self.z_count:
            self.flips.append([(at(z, y, c), at(z ^ step, y, c)) for z, y, c in spots])
            step *= 2
        self.lines = [
            [at(z, y, c) for z in range(self.z_count)] for y in range(2) for c in range(2)
        ]
        index = lax.axis_index("dp")
        self.c = index % 2
        self.y = (index // 2) % 2
        self.z = index // 4
        self.x = lax.axis_index("mp")
        self.sent = {"x": [], "y": [], "z": []}

    def queue(self, link, value, send):
        ahead = self.sent[link][-DEPTH[link] :]
        if len(ahead) == DEPTH[link]:
            value = after(value, ahead[0])
        self.sent[link].append(send(value))
        return self.sent[link][-1]

    def over_y(self, value):
        return self.queue("y", value, lambda v: lax.ppermute(v, "dp", self.swap_y))

    def over_c(self, value):
        return lax.ppermute(value, "dp", self.swap_c)

    def over_x(self, value):
        return self.queue("x", value, lambda v: lax.ppermute(v, "mp", [(0, 1), (1, 0)]))

    def next_z(self, value):
        return self.queue("z", value, lambda v: lax.ppermute(v, "dp", self.ring))

    def along_z(self, value):
        send = lambda v: lax.all_to_all(v, "dp", 0, 0, axis_index_groups=self.lines, tiled=True)
        return self.queue("z", value, send)

    def behind(self, step):
        return lax.rem(self.z - step + 2 * self.z_count, self.z_count)

    def sum_dp(self, value):
        value = value + self.over_c(value)
        value = value + lax.ppermute(value, "dp", self.swap_y)
        for flip in self.flips:
            value = value + lax.ppermute(value, "dp", flip)
        return value


def pair(index, mine, other, axis):
    return jnp.where(
        index == 0, jnp.stack([mine, other], axis=axis), jnp.stack([other, mine], axis=axis)
    )


def take(value, index, axis):
    return lax.dynamic_index_in_dim(value, index, axis, keepdims=False)


def call(body, grid, in_specs, outs, out_specs, operands, scratch=(), aliases=None):
    return pl.pallas_call(
        body,
        out_shape=[jax.ShapeDtypeStruct(shape, dtype) for shape, dtype in outs],
        grid_spec=pltpu.PrefetchScalarGridSpec(
            num_scalar_prefetch=1,
            grid=grid,
            in_specs=in_specs,
            out_specs=out_specs,
            scratch_shapes=list(scratch),
        ),
        input_output_aliases=aliases or {},
        compiler_params=pltpu.CompilerParams(vmem_limit_bytes=VMEM),
    )(*operands)


def place_slot(ranks, pieces, wholes, z_count, cuts):
    rows, width = pieces[0].shape
    ends = list(cuts[1:]) + [width]
    given = len(wholes)

    def body(ranks_ref, *refs):
        sources, targets = refs[:4], refs[4 + given :]
        y, c = ranks_ref[1], ranks_ref[2]
        spots = [(y, c), (1 - y, c), (y, 1 - c), (1 - y, 1 - c)]
        for source, (at_y, at_c) in zip(sources, spots):
            for target, begin, end in zip(targets, cuts, ends):
                target[0, at_y, at_c] = source[:, begin:end]

    whole_spec = pl.BlockSpec(memory_space=pl.ANY)
    return call(
        body,
        (1,),
        [pl.BlockSpec((rows, width), lambda i, ranks: (0, 0))] * 4 + [whole_spec] * given,
        [((z_count, 2, 2, rows, end - begin), BF16) for begin, end in zip(cuts, ends)],
        [
            pl.BlockSpec((1, 2, 2, rows, end - begin), lambda i, ranks: (ranks[0], 0, 0, 0, 0))
            for begin, end in zip(cuts, ends)
        ],
        (ranks, *pieces, *wholes),
        aliases={5 + number: number for number in range(given)},
    )


def place_all(ranks, pieces):
    z_count, rows, width = pieces[0].shape

    def body(ranks_ref, own, side, core, both, target):
        y, c = ranks_ref[1], ranks_ref[2]
        target[0, y, c] = own[0]
        target[0, 1 - y, c] = side[0]
        target[0, y, 1 - c] = core[0]
        target[0, 1 - y, 1 - c] = both[0]

    whole = call(
        body,
        (z_count,),
        [pl.BlockSpec((1, rows, width), lambda i, ranks: (i, 0, 0))] * 4,
        [((z_count, 2, 2, rows, width), BF16)],
        [pl.BlockSpec((1, 2, 2, rows, width), lambda i, ranks: (i, 0, 0, 0, 0))],
        (ranks, *pieces),
    )[0]
    return whole.reshape(z_count * 4 * rows, width)


def product_rows(ranks, lefts, rights, z_count):
    features = lefts[0].shape[1]
    width = rights[0].shape[1]
    rows = features // (4 * z_count)
    block = math.lcm(4 * rows, 128)
    span = block // (4 * rows)

    def body(ranks_ref, *refs):
        left = [ref[...] for ref in refs[: len(lefts)]]
        right = [ref[...] for ref in refs[len(lefts) : -2]]
        keep, send = refs[-2:]
        left = left[0] if len(left) == 1 else jnp.concatenate(left, axis=0)
        right = right[0] if len(right) == 1 else jnp.concatenate(right, axis=0)
        whole = mm_tn(left, right)
        low = ranks_ref[2] == 0
        for place in range(span):
            for y in range(2):
                at = (place * 4 + y * 2) * rows
                first, second = whole[at : at + rows], whole[at + rows : at + 2 * rows]
                keep[place, y] = jnp.where(low, first, second).astype(BF16)
                send[place, y] = jnp.where(low, second, first).astype(BF16)

    out_spec = pl.BlockSpec((span, 2, rows, width), lambda i, ranks: (i, 0, 0, 0))
    return call(
        body,
        (features // block,),
        [pl.BlockSpec((left.shape[0], block), lambda i, ranks: (0, i)) for left in lefts]
        + [pl.BlockSpec(right.shape, lambda i, ranks: (0, 0)) for right in rights],
        [((z_count, 2, rows, width), BF16)] * 2,
        [out_spec] * 2,
        (ranks, *lefts, *rights),
    )


def reduce_rows(grid, ranks, lefts, rights):
    keep, send = product_rows(ranks, lefts, rights, grid.z_count)
    got = grid.over_c(send)
    pick = lambda value, y: take(value, y, 1).astype(F32)
    part = (pick(keep, 1 - grid.y) + pick(got, 1 - grid.y)).astype(BF16)
    across = grid.over_y(part)
    return (pick(keep, grid.y) + pick(got, grid.y) + across.astype(F32)).astype(BF16)


def mlp_slot(ranks, wg, wu, wd, bg, bu, own, other, dy_own, dy_other):
    features, hidden = wg.shape
    half = own.shape[0]
    block = features // 4 if (features // 4) % 128 == 0 else features

    def body(
        ranks_ref, wg_ref, wu_ref, wd_ref, bg_ref, bu_ref, own_ref, other_ref, dyo_ref, dyr_ref,
        hid_ref, dg_ref, du_ref, db_own, db_other, out_own, out_other, b_all, dy_all, sums,
    ):
        b_all[:half], b_all[half:] = own_ref[...], other_ref[...]
        dy_all[:half], dy_all[half:] = dyo_ref[...], dyr_ref[...]
        sums[...] = jnp.zeros_like(sums)

        @pl.loop(0, features // block)
        def _(step):
            at = pl.ds(pl.multiple_of(step * block, 128), block)
            sums[0] += mm(b_all[:, at], wg_ref[at, :])
            sums[1] += mm(b_all[:, at], wu_ref[at, :])
            sums[2] += mm(dy_all[:, at], wd_ref[at, :])

        gate, up, grad_inner = sums[0] + bg_ref[...], sums[1] + bu_ref[...], sums[2]
        inner = GELU_A * (gate + GELU_B * gate * gate * gate)
        bend = jnp.tanh(inner)
        gelu = 0.5 * gate * (1.0 + bend)
        slope = 0.5 * (1.0 + bend) + 0.5 * gate * (1.0 - bend * bend) * (
            GELU_A * (1.0 + 3.0 * GELU_B * gate * gate)
        )
        hid = (gelu * up).astype(BF16)
        grad_gate = (grad_inner * up * slope).astype(BF16)
        grad_up = (grad_inner * gelu).astype(BF16)
        hid_ref[...], dg_ref[...], du_ref[...] = hid, grad_gate, grad_up

        @pl.loop(0, features // block)
        def _(step):
            at = pl.ds(pl.multiple_of(step * block, 128), block)
            part = mm_nt(dg_ref[...], wg_ref[at, :]) + mm_nt(du_ref[...], wu_ref[at, :])
            db_own[:, at], db_other[:, at] = part[:half].astype(BF16), part[half:].astype(BF16)
            part = mm_nt(hid_ref[...], wd_ref[at, :])
            out_own[:, at], out_other[:, at] = part[:half].astype(BF16), part[half:].astype(BF16)

    full = lambda shape: pl.BlockSpec(shape, lambda i, ranks: (0, 0))
    operands = (wg, wu, wd, bg[None], bu[None], own, other, dy_own, dy_other)
    outs = [((2 * half, hidden), BF16)] * 3 + [((half, features), BF16)] * 4
    return call(
        body,
        (1,),
        [full(operand.shape) for operand in operands],
        outs,
        [full(shape) for shape, _ in outs],
        (ranks, *operands),
        scratch=[
            pltpu.VMEM((2 * half, features), BF16),
            pltpu.VMEM((2 * half, features), BF16),
            pltpu.VMEM((3, 2 * half, hidden), F32),
        ],
    )


def scatter_z(grid, parts):
    held = take(parts, grid.behind(1), 0)
    for step in range(2, grid.z_count + 1):
        got = grid.next_z(held)
        held = got.astype(F32) + take(parts, grid.behind(step), 0).astype(F32)
        held = held.astype(BF16) if step < grid.z_count else held
    return held


def split_columns(grid, shard):
    rows, width = shard.shape
    return shard.reshape(rows, grid.z_count, width // grid.z_count).transpose(1, 0, 2)


def collect_columns(grid, parts):
    parts = grid.along_z(parts)
    count, rows, width = parts.shape
    return parts.astype(F32).transpose(1, 0, 2).reshape(rows, count * width)


def turned(value, cosine, sine):
    first = value[:, : cosine.shape[1]]
    first = first * cosine + pltpu.roll(first, first.shape[1] // 2, 1) * sine
    return jnp.concatenate([first, value[:, cosine.shape[1] :]], axis=1)


def softmax(query, key, bias):
    scores = mm_nt(query, key) + bias
    expon = jnp.exp(scores - jnp.max(scores, axis=-1, keepdims=True))
    return expon / jnp.sum(expon, axis=-1, keepdims=True)


def attend(scale, q_ref, k_ref, v_ref, cos_ref, sin_ref, bias_ref, rq_ref, o_ref):
    size = k_ref.shape[1]
    for head in range(q_ref.shape[1] // size):
        at = pl.ds(head * size, size)
        query = (turned(q_ref[:, at], cos_ref[...], sin_ref[...]) * scale).astype(BF16)
        rq_ref[:, at] = query
        probs = softmax(query, k_ref[...], bias_ref[...]).astype(BF16)
        o_ref[:, at] = mm(probs, v_ref[...]).astype(BF16)


def attend_back(
    scale, do_ref, rq_ref, k_ref, v_ref, cos_ref, sin_ref, bias_ref, dq_ref, dk_ref, dv_ref
):
    size = k_ref.shape[1]
    cosine, sine = cos_ref[...], -sin_ref[...]
    grad_key = jnp.zeros(dk_ref.shape, F32)
    grad_value = jnp.zeros(dv_ref.shape, F32)
    for head in range(rq_ref.shape[1] // size):
        at = pl.ds(head * size, size)
        query, grad_out = rq_ref[:, at], do_ref[:, at]
        probs = softmax(query, k_ref[...], bias_ref[...])
        grad_value += mm_tn(probs.astype(BF16), grad_out)
        grad_probs = mm_nt(grad_out, v_ref[...])
        delta = jnp.sum(probs * grad_probs, axis=-1, keepdims=True)
        grad_scores = (probs * (grad_probs - delta)).astype(BF16)
        grad_query = mm(grad_scores, k_ref[...]) * scale
        dq_ref[:, at] = turned(grad_query, cosine, sine).astype(BF16)
        grad_key += mm_tn(grad_scores, query)
    dk_ref[...] = turned(grad_key, cosine, sine)
    dv_ref[...] = grad_value


def in_vmem(body, shapes, *operands):
    spec = pl.BlockSpec(memory_space=pltpu.VMEM)
    return pl.pallas_call(
        body,
        out_shape=[jax.ShapeDtypeStruct(shape, dtype) for shape, dtype in shapes],
        in_specs=[spec] * len(operands),
        out_specs=[spec] * len(shapes),
        compiler_params=pltpu.CompilerParams(vmem_limit_bytes=32 * 2**20),
    )(*operands)


def shards(
    inputs,
    gain_attn,
    w_query,
    w_keyval,
    w_output,
    gain_mlp,
    w_gate,
    b_gate,
    w_up,
    b_up,
    w_down,
    b_down,
    segment_ids,
    cotangent,
    total,
):
    grid = Grid(total)
    count = grid.z_count
    micro, length, width = inputs.shape
    tokens = micro * length
    head_dim = w_keyval.shape[1] // 2
    query_width = w_query.shape[1]
    scale = head_dim ** (-0.5)

    def halves(value):
        value = value.reshape(micro, 2, length // 2, value.shape[-1])
        return tuple(take(value, i, 1).reshape(tokens // 2, -1) for i in (grid.x, 1 - grid.x))

    def join(mine, other):
        shape = (micro, length // 2, mine.shape[-1])
        return pair(grid.x, mine.reshape(shape), other.reshape(shape), 1).reshape(tokens, -1)

    keyval_half = lax.dynamic_slice_in_dim(w_keyval, grid.x * head_dim, head_dim, 1)
    ranks = jnp.stack([grid.z, grid.y, grid.c]).astype(jnp.int32)
    slots = [jnp.concatenate([w_query, keyval_half, w_output.T], axis=1)]
    dy_half = halves(cotangent.reshape(tokens, width))[0]
    dy_slots, dy_others = [dy_half], []
    wholes = []
    for step in range(count):
        if step + 1 < count:
            slots.append(grid.next_z(slots[step]))
        across = grid.over_y(slots[step])
        if step + 1 < count:
            dy_slots.append(grid.next_z(dy_slots[step]))
        pieces = [slots[step], across, grid.over_c(slots[step]), grid.over_c(across)]
        spot = jnp.stack([grid.behind(step), grid.y, grid.c]).astype(jnp.int32)
        wholes = place_slot(spot, pieces, wholes, count, (0, query_width + head_dim))
        dy_others.append(grid.over_x(dy_slots[step]))
    w_qkv, w_out = [whole.reshape(width, -1) for whole in wholes]

    mlp = []
    for shard in (w_gate, w_up, w_down.T):
        mine = grid.along_z(split_columns(grid, shard))
        across = grid.over_y(mine)
        mlp.append(place_all(ranks, [mine, across, grid.over_c(mine), grid.over_c(across)]))
    wg, wu, wd = mlp
    hidden = wg.shape[1]
    place = grid.z * hidden
    bg = lax.dynamic_slice_in_dim(b_gate, place, hidden, 0)
    bu = lax.dynamic_slice_in_dim(b_up, place, hidden, 0)

    segment = segment_ids.reshape(micro, length)
    offsets = jax.vmap(positions)(segment).reshape(tokens)
    quarter = head_dim // 4
    freqs = 10000.0 ** (-jnp.arange(quarter, dtype=F32) / quarter)
    angle = offsets[:, None] * freqs[None, :]
    cosine, sine = jnp.cos(angle), jnp.sin(angle)
    cosine = jnp.concatenate([cosine, cosine], axis=1)
    sine = jnp.concatenate([-sine, sine], axis=1)
    index = jnp.arange(tokens, dtype=jnp.int32)
    seg = segment.reshape(tokens)
    allowed = (
        (seg[:, None] == seg[None, :])
        & (index[:, None] // length == index[None, :] // length)
        & (index[None, :] <= index[:, None])
    )
    bias = jnp.where(allowed, 0.0, -1e30).astype(F32)
    hidden_x = inputs.reshape(tokens, width).astype(F32)
    factor_one = inv_root(hidden_x)
    normed = (hidden_x * factor_one * gain_attn).astype(BF16)
    queries = mm(normed, w_qkv[:, :query_width])
    keyval = mm(normed, w_qkv[:, query_width:])
    front, back = keyval[:, :quarter], keyval[:, quarter : 2 * quarter]
    swapped = jnp.concatenate([back, front], axis=1)
    key = jnp.concatenate(
        [keyval[:, : 2 * quarter] * cosine + swapped * sine, keyval[:, 2 * quarter :]], axis=1
    )
    keyval = jnp.where(grid.x == 0, key, keyval).astype(BF16)
    keyval_other = grid.over_x(keyval)
    rot_key = jnp.where(grid.x == 0, keyval, keyval_other)
    values_in = jnp.where(grid.x == 0, keyval_other, keyval)
    shape = (tokens, query_width)
    rot_query, mixed_b = in_vmem(
        partial(attend, scale),
        [(shape, BF16), (shape, BF16)],
        *(queries, rot_key, values_in, cosine, sine, bias),
    )
    attended = mm_nt(mixed_b, w_out)
    mine, other = halves(attended)
    attended = mine + grid.over_x(other.astype(BF16)).astype(F32)
    x_half = halves(hidden_x)[0]
    residual = x_half + attended
    factor_two = inv_root(residual)
    normed_two = (residual * factor_two * gain_mlp).astype(BF16)

    b_slots, b_others, slot = [], [], normed_two
    for step in range(count):
        coming = grid.next_z(slot) if step + 1 < count else None
        b_slots.append(slot)
        b_others.append(grid.over_x(slot))
        slot = coming
    results = [
        mlp_slot(ranks, wg, wu, wd, bg, bu, *pieces)
        for pieces in zip(b_slots, b_others, dy_slots, dy_others)
    ]
    inner_slots, gate_slots, up_slots, db_own, db_other, out_own, out_other = zip(*results)

    def back_to_tokens(owns, others):
        held = None
        for step in list(range(1, count)) + [0]:
            part = owns[step].astype(F32) + grid.over_x(others[step]).astype(F32)
            held = part if held is None else part + held.astype(F32)
            if step > 0:
                held = grid.next_z(held.astype(BF16))
        return held

    grad_norm_two = back_to_tokens(db_own, db_other)
    grad_out = dy_half.astype(F32)
    gain_mlp_term = jnp.sum(grad_norm_two * residual * factor_two, axis=0)
    grad_resid = grad_out + norm_back(residual, factor_two, gain_mlp, grad_norm_two)
    grad_resid_b = grad_resid.astype(BF16)
    grad_resid_b = join(grad_resid_b, grid.over_x(grad_resid_b))

    dy_all = [piece for two in zip(dy_slots, dy_others) for piece in two]
    b_all = [piece for two in zip(b_slots, b_others) for piece in two]
    down_grad = collect_columns(grid, reduce_rows(grid, ranks, dy_all, inner_slots)).T
    gate_grad = collect_columns(grid, reduce_rows(grid, ranks, b_all, gate_slots))
    up_grad = collect_columns(grid, reduce_rows(grid, ranks, b_all, up_slots))

    out_grad = scatter_z(grid, reduce_rows(grid, ranks, [grad_resid_b], [mixed_b])).T
    grad_mixed = mm(grad_resid_b, w_out).astype(BF16)
    shape_kv = (tokens, head_dim)
    grad_query, grad_key, grad_values = in_vmem(
        partial(attend_back, scale),
        [(shape, BF16), (shape_kv, F32), (shape_kv, F32)],
        *(grad_mixed, rot_query, rot_key, values_in, cosine, sine, bias),
    )
    grad_own = jnp.where(grid.x == 0, grad_key, grad_values)
    grad_other = jnp.where(grid.x == 0, grad_values, grad_key)
    grad_keyval = (grad_own + grid.over_x(grad_other)).astype(BF16)
    grad_qkv = jnp.concatenate([grad_query, grad_keyval], axis=1)
    mine, other = halves(mm_nt(grad_qkv, w_qkv))
    grad_normed = mine + grid.over_x(other.astype(BF16)).astype(F32)
    factor_half = halves(factor_one)[0]
    gain_attn_term = jnp.sum(grad_normed * x_half * factor_half, axis=0)
    grad_input = grad_resid + norm_back(x_half, factor_half, gain_attn, grad_normed)
    grad_input = grad_input.astype(BF16)
    grad_input = join(grad_input, grid.over_x(grad_input))

    branch = back_to_tokens(out_own, out_other)
    outputs = (residual + branch + b_down).astype(BF16)
    outputs = join(outputs, grid.over_x(outputs))

    middle = (query_width + head_dim) // 2
    cuts = (grad_qkv[:, :middle], grad_qkv[:, middle:])
    cuts = [reduce_rows(grid, ranks, [normed], [cut]) for cut in cuts]
    qkv_grad = jnp.concatenate([scatter_z(grid, cut) for cut in cuts], axis=1)
    query_grad = qkv_grad[:, :query_width]
    keyval_grad = qkv_grad[:, query_width:]
    keyval_grad = pair(grid.x, keyval_grad, grid.over_x(keyval_grad), 1)
    keyval_grad = keyval_grad.reshape(keyval_grad.shape[0], 2 * head_dim)

    ffn = b_gate.shape[0]
    wide = jnp.zeros((2, ffn), F32)
    sums = [
        sum(jnp.sum(slot.astype(F32), axis=0) for slot in slots)
        for slots in (gate_slots, up_slots)
    ]
    wide = lax.dynamic_update_slice(wide, jnp.stack(sums), (0, place)).reshape(-1)
    narrow = jnp.stack([gain_attn_term, gain_mlp_term, jnp.sum(grad_out, axis=0)])
    narrow = (narrow + grid.over_x(narrow)).reshape(-1)
    small = grid.sum_dp(jnp.concatenate([narrow, wide]))
    return (
        outputs.reshape(inputs.shape),
        grad_input.reshape(inputs.shape),
        small[:width],
        query_grad,
        keyval_grad,
        out_grad,
        small[width : 2 * width],
        gate_grad,
        small[3 * width : 3 * width + ffn],
        up_grad,
        small[3 * width + ffn :],
        down_grad,
        small[2 * width : 3 * width],
    )


def solution(mesh):
    in_specs = (
        P(None, "dp", None),
        P(),
        P("dp", "mp"),
        P("dp", None),
        P("mp", "dp"),
        P(),
        P("dp", "mp"),
        P("mp"),
        P("dp", "mp"),
        P("mp"),
        P("mp", "dp"),
        P(),
        P(None, "dp", None),
        P(None, "dp", None),
    )
    out_specs = (
        P(None, "dp", None),
        P(None, "dp", None),
        P(),
        P("dp", "mp"),
        P("dp", None),
        P("mp", "dp"),
        P(),
        P("dp", "mp"),
        P("mp"),
        P("dp", "mp"),
        P("mp"),
        P("mp", "dp"),
        P(),
    )
    body = partial(shards, total=mesh.shape["dp"])
    return jax.shard_map(body, mesh=mesh, in_specs=in_specs, out_specs=out_specs, check_vma=False)
```

```python
import math
from functools import partial

import jax
import jax.numpy as jnp
from jax import lax
from jax.experimental import pallas as pl
from jax.experimental.pallas import tpu as pltpu
from jax.sharding import PartitionSpec as P

EPS = 1e-06
F32 = jnp.float32
BF16 = jnp.bfloat16
VMEM = 24 * 2**20
SCALE = 4.0
GELU_A, GELU_B = math.sqrt(2.0 / math.pi), 0.044715


def positions(segment):
    count = segment.shape[0]
    index = jnp.arange(count, dtype=jnp.int32)
    fresh = jnp.concatenate([jnp.ones((1,), jnp.bool_), segment[1:] != segment[:-1]])
    starts = lax.cummax(jnp.where(fresh, index, 0), axis=0)
    return (index - starts).astype(F32)


def inv_root(values):
    return lax.rsqrt(jnp.mean(values * values, axis=-1, keepdims=True) + EPS)


def norm_back(values, factor, gain, grad_norm):
    scaled = gain * grad_norm
    return factor * scaled - values * factor**3 * jnp.mean(scaled * values, axis=-1, keepdims=True)


def mm(left, right):
    return jnp.dot(left, right, preferred_element_type=F32)


def mm_nt(left, right):
    return lax.dot_general(left, right, (((1,), (1,)), ((), ())), preferred_element_type=F32)


def mm_tn(left, right):
    return lax.dot_general(left, right, (((0,), (0,)), ((), ())), preferred_element_type=F32)


class Grid:
    def __init__(self, total):
        self.z_count = total // 4
        spots = [(z, y, c) for z in range(self.z_count) for y in range(2) for c in range(2)]
        at = lambda z, y, c: (z * 2 + y) * 2 + c
        self.swap_y = [(at(z, y, c), at(z, 1 - y, c)) for z, y, c in spots]
        self.swap_c = [(at(z, y, c), at(z, y, 1 - c)) for z, y, c in spots]
        self.ring = lambda step: [
            (at(z, y, c), at((z + step) % self.z_count, y, c)) for z, y, c in spots
        ]
        self.flips = []
        step = 1
        while step < self.z_count:
            self.flips.append([(at(z, y, c), at(z ^ step, y, c)) for z, y, c in spots])
            step *= 2
        self.lines = [
            [at(z, y, c) for z in range(self.z_count)] for y in range(2) for c in range(2)
        ]
        index = lax.axis_index("dp")
        self.c = index % 2
        self.y = (index // 2) % 2
        self.z = index // 4
        self.x = lax.axis_index("mp")
        self.token = jnp.zeros((), F32)

    def wait(self, *values):
        self.token = lax.optimization_barrier((self.token, values))[0]

    def gate(self, value):
        return lax.optimization_barrier((value, self.token))[0]

    def over_y(self, value):
        return lax.ppermute(self.gate(value), "dp", self.swap_y)

    def over_c(self, value):
        return lax.ppermute(self.gate(value), "dp", self.swap_c)

    def over_x(self, value):
        return lax.ppermute(self.gate(value), "mp", [(0, 1), (1, 0)])

    def next_z(self, value, step=1):
        return lax.ppermute(self.gate(value), "dp", self.ring(step))

    def along_z(self, value):
        value = self.gate(value)
        return lax.all_to_all(value, "dp", 0, 0, axis_index_groups=self.lines, tiled=True)

    def behind(self, step):
        return lax.rem(self.z - step + 2 * self.z_count, self.z_count)


def pair(index, mine, other, axis):
    return jnp.where(
        index == 0, jnp.stack([mine, other], axis=axis), jnp.stack([other, mine], axis=axis)
    )


def take(value, index, axis):
    return lax.dynamic_index_in_dim(value, index, axis, keepdims=False)


def cost(micros):
    micros = micros / SCALE
    flops, moved = int(micros * 1.15e9), int(micros * 3.69e6)
    return pl.CostEstimate(flops=flops, bytes_accessed=moved, transcendentals=0)


def call(body, micros, grid, in_specs, outs, out_specs, operands, aliases=None, limit=VMEM):
    return pl.pallas_call(
        body,
        out_shape=[jax.ShapeDtypeStruct(shape, dtype) for shape, dtype in outs],
        grid_spec=pltpu.PrefetchScalarGridSpec(
            num_scalar_prefetch=1,
            grid=grid,
            in_specs=in_specs,
            out_specs=out_specs,
        ),
        input_output_aliases=aliases or {},
        cost_estimate=cost(micros),
        compiler_params=pltpu.CompilerParams(vmem_limit_bytes=limit),
    )(*operands)


def place_slot(ranks, pieces, wholes, z_count, cuts):
    rows, width = pieces[0].shape
    ends = list(cuts[1:]) + [width]
    given = len(wholes)

    def body(ranks_ref, *refs):
        sources, targets = refs[:4], refs[4 + given :]
        y, c = ranks_ref[1], ranks_ref[2]
        spots = [(y, c), (1 - y, c), (y, 1 - c), (1 - y, 1 - c)]
        for source, (at_y, at_c) in zip(sources, spots):
            for target, begin, end in zip(targets, cuts, ends):
                target[0, at_y, at_c] = source[:, begin:end]

    whole_spec = pl.BlockSpec(memory_space=pl.ANY)
    return call(
        body,
        4.0,
        (1,),
        [pl.BlockSpec((rows, width), lambda i, ranks: (0, 0))] * 4 + [whole_spec] * given,
        [((z_count, 2, 2, rows, end - begin), BF16) for begin, end in zip(cuts, ends)],
        [
            pl.BlockSpec((1, 2, 2, rows, end - begin), lambda i, ranks: (ranks[0], 0, 0, 0, 0))
            for begin, end in zip(cuts, ends)
        ],
        (ranks, *pieces, *wholes),
        aliases={5 + number: number for number in range(given)},
        limit=2 * VMEM,
    )


def place_all(ranks, pieces):
    z_count, rows, width = pieces[0].shape

    def body(ranks_ref, own, side, core, both, target):
        y, c = ranks_ref[1], ranks_ref[2]
        target[0, y, c] = own[0]
        target[0, 1 - y, c] = side[0]
        target[0, y, 1 - c] = core[0]
        target[0, 1 - y, 1 - c] = both[0]

    whole = call(
        body,
        4.0,
        (z_count,),
        [pl.BlockSpec((1, rows, width), lambda i, ranks: (i, 0, 0))] * 4,
        [((z_count, 2, 2, rows, width), BF16)],
        [pl.BlockSpec((1, 2, 2, rows, width), lambda i, ranks: (i, 0, 0, 0, 0))],
        (ranks, *pieces),
    )[0]
    return whole.reshape(z_count * 4 * rows, width)


def product(left, right, dtype):
    rows, depth = left.shape
    width = right.shape[1]
    block = 256 if width % 256 == 0 else width

    def body(ranks_ref, left_ref, right_ref, out_ref):
        out_ref[...] = mm(left_ref[...], right_ref[...]).astype(dtype)

    return call(
        body,
        4.5,
        (width // block,),
        [
            pl.BlockSpec((rows, depth), lambda i, ranks: (0, 0)),
            pl.BlockSpec((depth, block), lambda i, ranks: (0, i)),
        ],
        [((rows, width), dtype)],
        [pl.BlockSpec((rows, block), lambda i, ranks: (0, i))],
        (jnp.zeros((1,), jnp.int32), left, right),
    )[0]


def product_nt(ranks, left, right, groups):
    rows, depth = left.shape
    width = right.shape[0]
    block = 512 if width % 512 == 0 else width
    half = rows // groups // 2

    def body(ranks_ref, left_ref, right_ref, own_ref, other_ref):
        whole = mm_nt(left_ref[...], right_ref[...])
        low = ranks_ref[3] == 0
        for group in range(groups):
            at = group * 2 * half
            first, second = whole[at : at + half], whole[at + half : at + 2 * half]
            to = pl.ds(group * half, half)
            own_ref[to, :] = jnp.where(low, first, second)
            other_ref[to, :] = jnp.where(low, second, first).astype(BF16)

    out_spec = pl.BlockSpec((rows // 2, block), lambda i, ranks: (0, i))
    return call(
        body,
        4.0,
        (width // block,),
        [
            pl.BlockSpec((rows, depth), lambda i, ranks: (0, 0)),
            pl.BlockSpec((block, depth), lambda i, ranks: (i, 0)),
        ],
        [((rows // 2, width), F32), ((rows // 2, width), BF16)],
        [out_spec] * 2,
        (ranks, left, right),
    )


def second_norm(x_ref, mine_ref, got_ref, gain_ref, residual_ref, factor_ref, normed_ref):
    residual = x_ref[...].astype(F32) + mine_ref[...] + got_ref[...].astype(F32)
    factor = inv_root(residual)
    residual_ref[...], factor_ref[...] = residual, factor
    normed_ref[...] = (residual * factor * gain_ref[...]).astype(BF16)


def second_norm_back(
    own_ref, got_ref, held_ref, residual_ref, factor_ref, gain_ref, dy_ref,
    grad_ref, grad_b_ref, term_ref,
):
    grad = own_ref[...].astype(F32) + got_ref[...].astype(F32) + held_ref[...].astype(F32)
    residual, factor = residual_ref[...], factor_ref[...]
    term_ref[...] = jnp.sum(grad * residual * factor, axis=0, keepdims=True)
    grad = dy_ref[...].astype(F32) + norm_back(residual, factor, gain_ref[...], grad)
    grad_ref[...], grad_b_ref[...] = grad, grad.astype(BF16)


def first_norm_back(mine_ref, got_ref, x_ref, factor_ref, gain_ref, grad_ref, out_ref, term_ref):
    grad = mine_ref[...] + got_ref[...].astype(F32)
    values, factor = x_ref[...].astype(F32), factor_ref[...]
    term_ref[...] = jnp.sum(grad * values * factor, axis=0, keepdims=True)
    out_ref[...] = (grad_ref[...] + norm_back(values, factor, gain_ref[...], grad)).astype(BF16)


def product_rows(ranks, lefts, groups, z_count):
    features = lefts[0].shape[1]
    width = groups[0][0].shape[1]
    rows = features // (4 * z_count)
    block = math.lcm(4 * rows, 128)
    span = block // (4 * rows)
    rights = [right for group in groups for right in group]
    each = len(groups[0])
    join = lambda parts: parts[0] if len(parts) == 1 else jnp.concatenate(parts, axis=0)

    def body(ranks_ref, *refs):
        left = join([ref[...] for ref in refs[: len(lefts)]])
        right_refs, out_refs = refs[len(lefts) : -outs], refs[-outs:]
        low = ranks_ref[2] == 0
        here = pl.program_id(0)
        for number in range(len(groups)):
            right = join([ref[...] for ref in right_refs[number * each : (number + 1) * each]])
            keep, sends = out_refs[number], out_refs[len(groups) + number * z_count :]
            whole = mm_tn(left, right)
            for place in range(span):
                for y in range(2):
                    at = (place * 4 + y * 2) * rows
                    first, second = whole[at : at + rows], whole[at + rows : at + 2 * rows]
                    keep[place, y] = jnp.where(low, first, second).astype(BF16)
                    other = jnp.where(low, second, first).astype(BF16)
                    for z in range(place, z_count, span):

                        @pl.when(here == z // span)
                        def _(target=sends[z], y=y, other=other):
                            target[y] = other

    outs = len(groups) * (1 + z_count)
    keep_spec = pl.BlockSpec((span, 2, rows, width), lambda i, ranks: (i, 0, 0, 0))
    send_spec = pl.BlockSpec((2, rows, width), lambda i, ranks: (0, 0, 0))
    out = call(
        body,
        (7.0 if len(lefts) > 1 else 3.0) * len(groups),
        (features // block,),
        [pl.BlockSpec((left.shape[0], block), lambda i, ranks: (0, i)) for left in lefts]
        + [pl.BlockSpec(right.shape, lambda i, ranks: (0, 0)) for right in rights],
        [((z_count, 2, rows, width), BF16)] * len(groups)
        + [((2, rows, width), BF16)] * (len(groups) * z_count),
        [keep_spec] * len(groups) + [send_spec] * (len(groups) * z_count),
        (ranks, *lefts, *rights),
    )
    sends = out[len(groups) :]
    return [
        (out[number], sends[number * z_count : (number + 1) * z_count])
        for number in range(len(groups))
    ]


def mlp_slot(wg, wu, wd, bg, bu, own, other, dy_own, dy_other):
    features, hidden = wg.shape
    half = own.shape[0]
    block = features // 4 if (features // 4) % 128 == 0 else features

    def body(
        wg_ref, wu_ref, wd_ref, bg_ref, bu_ref, own_ref, other_ref, dyo_ref, dyr_ref,
        hid_ref, dg_ref, du_ref, db_own, db_other, out_own, out_other, b_all, dy_all,
    ):
        b_all[:half], b_all[half:] = own_ref[...], other_ref[...]
        dy_all[:half], dy_all[half:] = dyo_ref[...], dyr_ref[...]
        gate = mm(b_all[...], wg_ref[...]) + bg_ref[...]
        up = mm(b_all[...], wu_ref[...]) + bu_ref[...]
        grad_inner = mm(dy_all[...], wd_ref[...])
        bend = jnp.tanh(GELU_A * (gate + GELU_B * gate * gate * gate))
        gelu = 0.5 * gate * (1.0 + bend)
        slope = 0.5 * (1.0 + bend) + 0.5 * gate * (1.0 - bend * bend) * (
            GELU_A * (1.0 + 3.0 * GELU_B * gate * gate)
        )
        hid_ref[...] = (gelu * up).astype(BF16)
        dg_ref[...] = (grad_inner * up * slope).astype(BF16)
        du_ref[...] = (grad_inner * gelu).astype(BF16)
        for step in range(features // block):
            at = pl.ds(step * block, block)
            part = mm_nt(dg_ref[...], wg_ref[at, :]) + mm_nt(du_ref[...], wu_ref[at, :])
            db_own[:, at], db_other[:, at] = part[:half].astype(BF16), part[half:].astype(BF16)
            part = mm_nt(hid_ref[...], wd_ref[at, :])
            out_own[:, at], out_other[:, at] = part[:half].astype(BF16), part[half:].astype(BF16)

    weights = [pltpu.with_memory_space_constraint(w, pltpu.VMEM) for w in (wg, wu, wd)]
    return in_vmem(
        body,
        10.0,
        [((2 * half, hidden), BF16)] * 3 + [((half, features), BF16)] * 4,
        *(*weights, bg[None], bu[None], own, other, dy_own, dy_other),
        scratch=[pltpu.VMEM((2 * half, features), BF16)] * 2,
    )


def split_columns(grid, shard):
    rows, width = shard.shape
    return shard.reshape(rows, grid.z_count, width // grid.z_count).transpose(1, 0, 2)


def own_rows(ranks, keep, got):
    z_count, _, rows, width = keep.shape

    def body(ranks_ref, keep_ref, *refs):
        away_ref, stay_ref = refs[-2:]
        y = ranks_ref[1]
        for z in range(z_count):

            @pl.when(pl.program_id(0) == z)
            def _(got_ref=refs[z]):
                for at, target in ((1 - y, away_ref), (y, stay_ref)):
                    part = keep_ref[0, at].astype(F32) + got_ref[at].astype(F32)
                    target[0] = part.astype(BF16)

    block = pl.BlockSpec((1, 2, rows, width), lambda i, ranks: (i, 0, 0, 0))
    whole = pl.BlockSpec((2, rows, width), lambda i, ranks: (0, 0, 0))
    half = pl.BlockSpec((1, rows, width), lambda i, ranks: (i, 0, 0))
    shape = ((z_count, rows, width), BF16)
    specs = [block] + [whole] * z_count
    return call(body, 2.0, (z_count,), specs, [shape] * 2, [half] * 2, (ranks, keep, *got))


def plus(left, right):
    z_count, rows, width = left.shape

    def body(ranks_ref, left_ref, right_ref, out_ref):
        out_ref[...] = (left_ref[...].astype(F32) + right_ref[...].astype(F32)).astype(BF16)

    block = pl.BlockSpec((1, rows, width), lambda i, ranks: (i, 0, 0))
    operands = (jnp.zeros((1,), jnp.int32), left, right)
    return call(body, 2.0, (z_count,), [block] * 2, [(left.shape, BF16)], [block], operands)[0]


def ring_sum(grid, parts, held, step):
    _, rows, width = parts.shape
    dtype = BF16 if step < grid.z_count else F32
    given = [] if held is None else [held]

    def body(ranks_ref, part_ref, *refs):
        part = part_ref[0].astype(F32)
        refs[-1][...] = (part + refs[0][...].astype(F32) if given else part).astype(dtype)

    full = pl.BlockSpec((rows, width), lambda i, ranks: (0, 0))
    spot = grid.behind(step).astype(jnp.int32)[None]
    return call(
        body,
        1.0,
        (1,),
        [pl.BlockSpec((1, rows, width), lambda i, ranks: (ranks[0], 0, 0))] + [full] * len(given),
        [((rows, width), dtype)],
        [full],
        (spot, parts, *given),
    )[0]


def add(*values):
    def body(*refs):
        total = refs[0][...].astype(F32)
        for ref in refs[1:-1]:
            total += ref[...].astype(F32)
        refs[-1][...] = total.astype(BF16)

    values = [value for value in values if value is not None]
    return in_vmem(body, 1.0, [(values[0].shape, BF16)], *values)[0]


def collect_columns(parts, turn=False):
    count, rows, width = parts.shape

    def body(parts_ref, out_ref):
        if turn:
            for step in range(count):
                out_ref[step * width : (step + 1) * width, :] = parts_ref[step].astype(F32).T
        else:
            pieces = [parts_ref[step].astype(F32) for step in range(count)]
            out_ref[...] = jnp.concatenate(pieces, axis=1)

    shape = (count * width, rows) if turn else (rows, count * width)
    return in_vmem(body, 3.0, [(shape, F32)], parts)[0]


def turned(value, cosine, sine):
    first = value[:, : cosine.shape[1]]
    first = first * cosine + pltpu.roll(first, first.shape[1] // 2, 1) * sine
    return jnp.concatenate([first, value[:, cosine.shape[1] :]], axis=1)


def softmax(query, key, bias):
    scores = mm_nt(query, key) + bias
    expon = jnp.exp(scores - jnp.max(scores, axis=-1, keepdims=True))
    return expon / jnp.sum(expon, axis=-1, keepdims=True)


def attend(scale, q_ref, k_ref, v_ref, cos_ref, sin_ref, bias_ref, rq_ref, o_ref):
    size = k_ref.shape[1]
    for head in range(rq_ref.shape[1] // size):
        at = pl.ds(head * size, size)
        query = (turned(q_ref[:, at], cos_ref[...], sin_ref[...]) * scale).astype(BF16)
        rq_ref[:, at] = query
        probs = softmax(query, k_ref[...], bias_ref[...]).astype(BF16)
        o_ref[:, at] = mm(probs, v_ref[...]).astype(BF16)


def attend_back(
    scale, do_ref, rq_ref, k_ref, v_ref, cos_ref, sin_ref, bias_ref, dq_ref, dk_ref, dv_ref
):
    size = k_ref.shape[1]
    cosine, sine = cos_ref[...], -sin_ref[...]
    grad_key = jnp.zeros(dk_ref.shape, F32)
    grad_value = jnp.zeros(dv_ref.shape, F32)
    for head in range(rq_ref.shape[1] // size):
        at = pl.ds(head * size, size)
        query, grad_out = rq_ref[:, at], do_ref[:, at]
        probs = softmax(query, k_ref[...], bias_ref[...])
        grad_value += mm_tn(probs.astype(BF16), grad_out)
        grad_probs = mm_nt(grad_out, v_ref[...])
        delta = jnp.sum(probs * grad_probs, axis=-1, keepdims=True)
        grad_scores = (probs * (grad_probs - delta)).astype(BF16)
        grad_query = mm(grad_scores, k_ref[...]) * scale
        dq_ref[:, at] = turned(grad_query, cosine, sine).astype(BF16)
        grad_key += mm_tn(grad_scores, query)
    dk_ref[...] = turned(grad_key, cosine, sine)
    dv_ref[...] = grad_value


def in_vmem(body, micros, shapes, *operands, scratch=()):
    spec = pl.BlockSpec(memory_space=pltpu.VMEM)
    return pl.pallas_call(
        body,
        out_shape=[jax.ShapeDtypeStruct(shape, dtype) for shape, dtype in shapes],
        in_specs=[spec] * len(operands),
        out_specs=[spec] * len(shapes),
        scratch_shapes=list(scratch),
        cost_estimate=cost(micros),
        compiler_params=pltpu.CompilerParams(vmem_limit_bytes=VMEM),
    )(*operands)


def shards(
    inputs,
    gain_attn,
    w_query,
    w_keyval,
    w_output,
    gain_mlp,
    w_gate,
    b_gate,
    w_up,
    b_up,
    w_down,
    b_down,
    segment_ids,
    cotangent,
    total,
):
    grid = Grid(total)
    count = grid.z_count
    micro, length, width = inputs.shape
    tokens = micro * length
    head_dim = w_keyval.shape[1] // 2
    query_width = w_query.shape[1]
    scale = head_dim ** (-0.5)

    def halves(value):
        value = value.reshape(micro, 2, length // 2, value.shape[-1])
        return tuple(take(value, i, 1).reshape(tokens // 2, -1) for i in (grid.x, 1 - grid.x))

    def join(mine, other):
        shape = (micro, length // 2, mine.shape[-1])
        return pair(grid.x, mine.reshape(shape), other.reshape(shape), 1).reshape(tokens, -1)

    ranks = jnp.stack([grid.z, grid.y, grid.c, grid.x]).astype(jnp.int32)
    keyval_half = lax.dynamic_slice_in_dim(w_keyval, grid.x * head_dim, head_dim, 1)
    shards_of = [split_columns(grid, shard) for shard in (w_gate, w_up, w_down.T)]
    dy_half = halves(cotangent.reshape(tokens, width))[0]
    segment = segment_ids.reshape(micro, length)
    offsets = jax.vmap(positions)(segment).reshape(tokens)
    quarter = head_dim // 4
    freqs = 10000.0 ** (-jnp.arange(quarter, dtype=F32) / quarter)
    angle = offsets[:, None] * freqs[None, :]
    cosine, sine = jnp.cos(angle), jnp.sin(angle)
    cosine = jnp.concatenate([cosine, cosine], axis=1)
    sine = jnp.concatenate([-sine, sine], axis=1)
    index = jnp.arange(tokens, dtype=jnp.int32)
    seg = segment.reshape(tokens)
    allowed = (
        (seg[:, None] == seg[None, :])
        & (index[:, None] // length == index[None, :] // length)
        & (index[None, :] <= index[:, None])
    )
    bias = jnp.where(allowed, 0.0, -1e30).astype(F32)
    hidden_x = inputs.reshape(tokens, width).astype(F32)
    factor_one = inv_root(hidden_x)
    normed = (hidden_x * factor_one * gain_attn).astype(BF16)
    x_half, factor_half = halves(inputs.reshape(tokens, width))[0], halves(factor_one)[0]
    half_shape = (tokens // 2, width)

    def mlp(step):
        pieces = (b_slots[step], b_others[step], dy_slots[step], dy_others[step])
        results.append(mlp_slot(wg, wu, wd, bg, bu, *grid.gate(pieces)))
        grid.wait(*results[-1])

    slots = [jnp.concatenate([w_query, keyval_half, w_output.T], axis=1)]
    across, beside, both, wholes = [], [], [], []
    dy_slots, dy_others = [dy_half], []

    def place(step):
        pieces = [slots[step], across[step], beside[step], both[step]]
        spot = jnp.stack([grid.behind(step), grid.y, grid.c]).astype(jnp.int32)
        return place_slot(spot, pieces, wholes, count, (0, query_width + head_dim))

    for step in range(count):
        if step + 1 < count:
            slots.append(grid.next_z(slots[step]))
        else:
            gate_mine = grid.along_z(shards_of[0])
        if step > 0:
            grid.wait(across[step - 1])
        across.append(grid.over_y(slots[step]))
        beside.append(grid.over_c(slots[step]))
        if step == 0:
            dy_others.append(grid.over_x(dy_half))
            grid.wait(shards_of[0])
        else:
            both.append(grid.over_c(across[step - 1]))
            wholes = place(step - 1)
            grid.wait(*wholes, beside[step])
        if step == 1:
            grid.wait(shards_of[1], normed, x_half, dy_others[0])
        if step == 2:
            grid.wait(shards_of[2], cosine, sine, bias)
        if step + 1 < count:
            grid.wait(slots[step + 1])
    grid.wait(across[-1])
    grid.wait(gate_mine)

    up_mine = grid.along_z(shards_of[1])
    gate_across, gate_beside = grid.over_y(gate_mine), grid.over_c(gate_mine)
    both.append(grid.over_c(across[-1]))
    wholes = place(count - 1)
    w_qkv, w_out = [whole.reshape(width, -1) for whole in wholes]
    queries = product(normed, w_qkv, F32)
    keyval = queries[:, query_width:]
    front, back = keyval[:, :quarter], keyval[:, quarter : 2 * quarter]
    swapped = jnp.concatenate([back, front], axis=1)
    key = jnp.concatenate(
        [keyval[:, : 2 * quarter] * cosine + swapped * sine, keyval[:, 2 * quarter :]], axis=1
    )
    keyval = jnp.where(grid.x == 0, key, keyval).astype(BF16)
    keyval_other = grid.over_x(keyval)
    grid.wait(keyval_other)
    rot_key = jnp.where(grid.x == 0, keyval, keyval_other)
    values_in = jnp.where(grid.x == 0, keyval_other, keyval)
    shape = (tokens, query_width)
    rot_query, mixed_b = in_vmem(
        partial(attend, scale),
        1.2,
        [(shape, BF16), (shape, BF16)],
        *(queries, rot_key, values_in, cosine, sine, bias),
    )
    mine, other = product_nt(ranks, mixed_b, w_out, micro)
    grid.wait(mine)
    attended = grid.over_x(other)
    grid.wait(up_mine)
    down_mine = grid.along_z(shards_of[2])
    grid.wait(gate_across)
    up_across, up_beside = grid.over_y(up_mine), grid.over_c(up_mine)
    gate_both = grid.over_c(gate_across)
    grid.wait(attended)
    residual, factor_two, normed_two = in_vmem(
        second_norm,
        2.0,
        [(half_shape, F32), ((tokens // 2, 1), F32), (half_shape, BF16)],
        *(x_half, mine, attended, gain_mlp[None]),
    )
    grid.wait(normed_two)
    b_slots, b_others = [normed_two], [grid.over_x(normed_two)]
    b_slots.append(grid.next_z(normed_two))
    dy_slots.append(grid.next_z(dy_half))
    wg = place_all(ranks, [gate_mine, gate_across, gate_beside, gate_both])
    grid.wait(wg, b_others[0])
    grid.wait(down_mine)

    grid.wait(up_across)
    down_across, down_beside = grid.over_y(down_mine), grid.over_c(down_mine)
    grid.wait(b_slots[1], dy_slots[1])
    for step in range(1, count - 1):
        b_slots.append(grid.next_z(b_slots[step]))
        dy_slots.append(grid.next_z(dy_slots[step]))
        b_others.append(grid.over_x(b_slots[step]))
        dy_others.append(grid.over_x(dy_slots[step]))
        if step == 1:
            up_both = grid.over_c(up_across)
            wu = place_all(ranks, [up_mine, up_across, up_beside, up_both])
            grid.wait(wu)
        if step == 2:
            grid.wait(down_across)
            down_both = grid.over_c(down_across)
            wd = place_all(ranks, [down_mine, down_across, down_beside, down_both])
            hidden = wg.shape[1]
            spot = grid.z * hidden
            bg = lax.dynamic_slice_in_dim(b_gate, spot, hidden, 0)
            bu = lax.dynamic_slice_in_dim(b_up, spot, hidden, 0)
            grid.wait(wd, bg, bu)
            results = []
            mlp(0)
        grid.wait(b_slots[step + 1], dy_slots[step + 1])
        grid.wait(b_others[step], dy_others[step])
    b_others.append(grid.over_x(b_slots[-1]))
    dy_others.append(grid.over_x(dy_slots[-1]))
    mlp(1)

    db_got = [None, grid.over_x(results[1][4])]
    db_next = None
    for step in range(2, count):
        mlp(step)
        if step == 2:
            grid.wait(b_others[-1], dy_others[-1])
        grid.wait(db_got[step - 1], *([] if db_next is None else [db_next]))
        db_held = add(results[step - 1][3], db_got[step - 1], db_next)
        grid.wait(db_held)
        db_next = grid.next_z(db_held)
        db_got.append(grid.over_x(results[step][4]))
    inner_slots, gate_slots, up_slots, db_own, db_other, out_own, out_other = zip(*results)
    dy_all = [piece for two in zip(dy_slots, dy_others) for piece in two]
    b_all = [piece for two in zip(b_slots, b_others) for piece in two]
    down_keep, down_send = product_rows(ranks, grid.gate(dy_all), [inner_slots], count)[0]
    grid.wait(down_keep)
    down_got = [grid.over_c(send) for send in down_send]
    grid.wait(db_next, db_got[-1])
    db_held = add(db_own[-1], db_got[-1], db_next)
    grid.wait(db_held)
    db_next = grid.next_z(db_held)
    db_got[0] = grid.over_x(db_other[0])
    grid.wait(*down_got)
    down_away, down_stay = own_rows(ranks, down_keep, down_got)
    grid.wait(down_away)
    down_back = grid.over_y(down_away)
    out_got = [None] * count
    grid.wait(db_got[0], db_next)
    grad_resid, grad_resid_b, gain_mlp_term = in_vmem(
        second_norm_back,
        3.0,
        [(half_shape, F32), (half_shape, BF16), ((1, width), F32)],
        *(db_own[0], db_got[0], db_next, residual, factor_two, gain_mlp[None], dy_half),
    )
    grid.wait(grad_resid_b)
    grad_resid_other = grid.over_x(grad_resid_b)
    out_got[1] = grid.over_x(out_other[1])
    (gate_keep, gate_send), (up_keep, up_send) = product_rows(
        ranks, grid.gate(b_all), [gate_slots, up_slots], count
    )
    grid.wait(gate_keep)
    gate_got = [grid.over_c(send) for send in gate_send]
    up_got = [grid.over_c(send) for send in up_send]
    grid.wait(*gate_got, grad_resid_other)
    gate_away, gate_stay = own_rows(ranks, gate_keep, gate_got)
    grid.wait(gate_away)
    grid.wait(down_back)
    gate_back = grid.over_y(gate_away)

    grad_resid_b = join(grad_resid_b, grad_resid_other)
    grad_mixed = product(grid.gate(grad_resid_b), w_out, BF16)
    shape_kv = (tokens, head_dim)
    grad_query, grad_key, grad_values = in_vmem(
        partial(attend_back, scale),
        2.3,
        [(shape, BF16), (shape_kv, F32), (shape_kv, F32)],
        *(grad_mixed, rot_query, rot_key, values_in, cosine, sine, bias),
    )
    grid.wait(grad_query)
    grad_own = jnp.where(grid.x == 0, grad_key, grad_values)
    grad_other = grid.over_x(jnp.where(grid.x == 0, grad_values, grad_key))
    down_rows = plus(down_stay, down_back)
    grid.wait(down_rows)
    down_parts = grid.along_z(down_rows)
    grid.wait(grad_other, out_got[1])
    branch = add(out_own[1], out_got[1])
    grad_keyval = (grad_own + grad_other).astype(BF16)
    grad_qkv = jnp.concatenate([grad_query, grad_keyval], axis=1)
    mine, other = product_nt(ranks, grid.gate(grad_qkv), w_qkv, micro)
    grid.wait(mine, branch)
    grad_normed = grid.over_x(other)
    branch = grid.next_z(branch)
    out_keep, out_send = product_rows(ranks, [grid.gate(grad_resid_b)], [[mixed_b]], count)[0]
    grid.wait(out_keep)
    out_got_c = [grid.over_c(send) for send in out_send]
    grid.wait(*up_got)
    up_away, up_stay = own_rows(ranks, up_keep, up_got)
    grid.wait(up_away)
    grid.wait(gate_back, grad_normed)
    up_back = grid.over_y(up_away)
    out_got[2] = grid.over_x(out_other[2])
    gate_rows = plus(gate_stay, gate_back)
    grid.wait(gate_rows)
    grid.wait(down_parts, branch)
    gate_parts = grid.along_z(gate_rows)
    grad_input, gain_attn_term = in_vmem(
        first_norm_back,
        3.0,
        [(half_shape, BF16), ((1, width), F32)],
        *(mine, grad_normed, x_half, factor_half, gain_attn[None], grad_resid),
    )
    grid.wait(grad_input, *out_got_c)
    out_away, out_stay = own_rows(ranks, out_keep, out_got_c)
    middle = (query_width + head_dim) // 2
    cuts = (grad_qkv[:, :middle], grad_qkv[:, middle:])
    products = [product_rows(ranks, [grid.gate(normed)], [[cut]], count)[0] for cut in cuts]
    qkv_keep, qkv_send = zip(*products)
    grid.wait(out_away, *qkv_keep)
    qkv_got = [[grid.over_c(send) for send in sends] for sends in qkv_send]
    grid.wait(up_back, out_got[2])
    out_back = grid.over_y(out_away)
    out_got[3] = grid.over_x(out_other[3])
    branch = add(out_own[2], out_got[2], branch)
    grid.wait(branch)
    branch = grid.next_z(branch)
    up_rows = plus(up_stay, up_back)
    grid.wait(up_rows)
    narrow = jnp.concatenate(
        [gain_attn_term, gain_mlp_term, jnp.sum(dy_half.astype(F32), axis=0)[None]]
    )
    grid.wait(*qkv_got[0], *qkv_got[1])
    qkv_away, qkv_stay = zip(
        *[own_rows(ranks, keep, got) for keep, got in zip(qkv_keep, qkv_got)]
    )
    grid.wait(*qkv_away)
    grid.wait(gate_parts, branch, out_got[3])
    up_parts = grid.along_z(up_rows)
    branch = add(out_own[3], out_got[3], branch)
    grid.wait(branch)
    branch = grid.next_z(branch)
    for step in range(4, count):
        out_got[step] = grid.over_x(out_other[step])
        branch = grid.next_z(add(out_own[step], out_got[step], branch))
    out_got[0] = grid.over_x(out_other[0])
    down_grad = collect_columns(down_parts, True)
    gate_grad = collect_columns(gate_parts)
    grid.wait(down_grad, gate_grad)
    grid.wait(out_back, out_got[0])
    qkv_back = [grid.over_y(qkv_away[0])]
    narrow_other = grid.over_x(narrow)
    out_rows = plus(out_stay, out_back)
    out_held = ring_sum(grid, out_rows, None, 1)
    grid.wait(out_held)
    out_held = grid.next_z(out_held)
    grid.wait(branch, narrow_other)
    outputs = (residual + add(out_own[0], out_got[0], branch).astype(F32) + b_down).astype(BF16)
    grid.wait(outputs)
    outputs_other = grid.over_x(outputs)
    grid.wait(out_held)
    out_held = ring_sum(grid, out_rows, out_held, 2)
    grid.wait(out_held)
    out_held = grid.next_z(out_held)

    ffn = b_gate.shape[0]
    wide = jnp.zeros((2, ffn), F32)
    sums = [
        sum(jnp.sum(slot.astype(F32), axis=0) for slot in slots)
        for slots in (gate_slots, up_slots)
    ]
    wide = lax.dynamic_update_slice(wide, jnp.stack(sums), (0, spot)).reshape(-1)
    small = jnp.concatenate([(narrow + narrow_other).reshape(-1), wide])
    small_other = grid.over_c(small)
    grid.wait(small_other, outputs_other)
    small = small + small_other
    grad_input_other = grid.over_x(grad_input)
    grid.wait(qkv_back[0])
    qkv_back.append(grid.over_y(qkv_away[1]))
    small_other = grid.over_y(small)
    qkv_rows = [plus(qkv_stay[0], qkv_back[0])]
    qkv_held = ring_sum(grid, qkv_rows[0], None, 1)
    grid.wait(qkv_held)
    qkv_held = [grid.next_z(qkv_held), None]
    for step in range(3, count):
        grid.wait(out_held)
        out_held = ring_sum(grid, out_rows, out_held, step)
        grid.wait(out_held)
        out_held = grid.next_z(out_held)
    grid.wait(qkv_held[0], small_other)
    small = small + small_other
    qkv_held[0] = ring_sum(grid, qkv_rows[0], qkv_held[0], 2)
    grid.wait(qkv_held[0])
    qkv_held[0] = grid.next_z(qkv_held[0])
    grid.wait(up_parts, out_held)
    up_grad = collect_columns(up_parts)
    out_grad = ring_sum(grid, out_rows, out_held, count).T
    grid.wait(up_grad, out_grad)
    grid.wait(qkv_back[1])
    qkv_rows.append(plus(qkv_stay[1], qkv_back[1]))
    qkv_held[1] = ring_sum(grid, qkv_rows[1], None, 1)
    grid.wait(qkv_held[1])
    qkv_held[1] = grid.next_z(qkv_held[1])
    for step in range(3, count + 1):
        if step - 3 < len(grid.flips):
            small_other = lax.ppermute(grid.gate(small), "dp", grid.flips[step - 3])
        grid.wait(*qkv_held)
        qkv_held[1] = grid.next_z(ring_sum(grid, qkv_rows[1], qkv_held[1], step - 1))
        if step < count:
            qkv_held[0] = grid.next_z(ring_sum(grid, qkv_rows[0], qkv_held[0], step))
        if step - 3 < len(grid.flips):
            grid.wait(small_other)
            small = small + small_other
    grid.wait(grad_input_other)
    qkv_held = [ring_sum(grid, rows, held, count) for rows, held in zip(qkv_rows, qkv_held)]
    qkv_held = jnp.concatenate(qkv_held, axis=1)
    query_grad = qkv_held[:, :query_width]
    keyval_grad = qkv_held[:, query_width:]
    keyval_grad = pair(grid.x, keyval_grad, grid.over_x(keyval_grad), 1)
    keyval_grad = keyval_grad.reshape(keyval_grad.shape[0], 2 * head_dim)
    return (
        join(outputs, outputs_other).reshape(inputs.shape),
        join(grad_input, grad_input_other).reshape(inputs.shape),
        small[:width],
        query_grad,
        keyval_grad,
        out_grad,
        small[width : 2 * width],
        gate_grad,
        small[3 * width : 3 * width + ffn],
        up_grad,
        small[3 * width + ffn :],
        down_grad,
        small[2 * width : 3 * width],
    )


def solution(mesh):
    in_specs = (
        P(None, "dp", None),
        P(),
        P("dp", "mp"),
        P("dp", None),
        P("mp", "dp"),
        P(),
        P("dp", "mp"),
        P("mp"),
        P("dp", "mp"),
        P("mp"),
        P("mp", "dp"),
        P(),
        P(None, "dp", None),
        P(None, "dp", None),
    )
    out_specs = (
        P(None, "dp", None),
        P(None, "dp", None),
        P(),
        P("dp", "mp"),
        P("dp", None),
        P("mp", "dp"),
        P(),
        P("dp", "mp"),
        P("mp"),
        P("dp", "mp"),
        P("mp"),
        P("mp", "dp"),
        P(),
    )
    body = partial(shards, total=mesh.shape["dp"])
    return jax.shard_map(body, mesh=mesh, in_specs=in_specs, out_specs=out_specs, check_vma=False)
```

```python
import math
from functools import partial

import jax
import jax.numpy as jnp
from jax import lax
from jax.experimental import pallas as pl
from jax.experimental.pallas import tpu as pltpu
from jax.sharding import PartitionSpec as P

EPS = 1e-06
F32 = jnp.float32
BF16 = jnp.bfloat16
VMEM = 24 * 2**20
SCALE = 12.0
GELU_A, GELU_B = math.sqrt(2.0 / math.pi), 0.044715


def positions(segment):
    count = segment.shape[0]
    index = jnp.arange(count, dtype=jnp.int32)
    fresh = jnp.concatenate([jnp.ones((1,), jnp.bool_), segment[1:] != segment[:-1]])
    starts = lax.cummax(jnp.where(fresh, index, 0), axis=0)
    return (index - starts).astype(F32)


def inv_root(values):
    return lax.rsqrt(jnp.mean(values * values, axis=-1, keepdims=True) + EPS)


def norm_back(values, factor, gain, grad_norm):
    scaled = gain * grad_norm
    return factor * scaled - values * factor**3 * jnp.mean(scaled * values, axis=-1, keepdims=True)


def mm(left, right):
    return jnp.dot(left, right, preferred_element_type=F32)


def mm_nt(left, right):
    return lax.dot_general(left, right, (((1,), (1,)), ((), ())), preferred_element_type=F32)


def mm_tn(left, right):
    return lax.dot_general(left, right, (((0,), (0,)), ((), ())), preferred_element_type=F32)


class Grid:
    def __init__(self, total):
        self.z_count = total // 4
        spots = [(z, y, c) for z in range(self.z_count) for y in range(2) for c in range(2)]
        at = lambda z, y, c: (z * 2 + y) * 2 + c
        self.swap_y = [(at(z, y, c), at(z, 1 - y, c)) for z, y, c in spots]
        self.swap_c = [(at(z, y, c), at(z, y, 1 - c)) for z, y, c in spots]
        self.ring = lambda step: [
            (at(z, y, c), at((z + step) % self.z_count, y, c)) for z, y, c in spots
        ]
        self.flips = []
        step = 1
        while step < self.z_count:
            self.flips.append([(at(z, y, c), at(z ^ step, y, c)) for z, y, c in spots])
            step *= 2
        self.lines = [
            [at(z, y, c) for z in range(self.z_count)] for y in range(2) for c in range(2)
        ]
        index = lax.axis_index("dp")
        self.c = index % 2
        self.y = (index // 2) % 2
        self.z = index // 4
        self.x = lax.axis_index("mp")
        self.token = jnp.zeros((), F32)

    def wait(self, *values):
        self.token = lax.optimization_barrier((self.token, values))[0]

    def gate(self, value):
        return lax.optimization_barrier((value, self.token))[0]

    def over_y(self, value):
        return lax.ppermute(self.gate(value), "dp", self.swap_y)

    def over_c(self, value):
        return lax.ppermute(self.gate(value), "dp", self.swap_c)

    def over_x(self, value):
        return lax.ppermute(self.gate(value), "mp", [(0, 1), (1, 0)])

    def next_z(self, value, step=1):
        return lax.ppermute(self.gate(value), "dp", self.ring(step))

    def along_z(self, value):
        value = self.gate(value)
        return lax.all_to_all(value, "dp", 0, 0, axis_index_groups=self.lines, tiled=True)

    def behind(self, step):
        return lax.rem(self.z - step + 2 * self.z_count, self.z_count)


def pair(index, mine, other, axis):
    return jnp.where(
        index == 0, jnp.stack([mine, other], axis=axis), jnp.stack([other, mine], axis=axis)
    )


def take(value, index, axis):
    return lax.dynamic_index_in_dim(value, index, axis, keepdims=False)


def cost(micros):
    micros = micros / SCALE
    flops, moved = int(micros * 1.15e9), int(micros * 3.69e6)
    return pl.CostEstimate(flops=flops, bytes_accessed=moved, transcendentals=0)


def call(body, micros, grid, in_specs, outs, out_specs, operands, aliases=None, limit=VMEM):
    return pl.pallas_call(
        body,
        out_shape=[jax.ShapeDtypeStruct(shape, dtype) for shape, dtype in outs],
        grid_spec=pltpu.PrefetchScalarGridSpec(
            num_scalar_prefetch=1,
            grid=grid,
            in_specs=in_specs,
            out_specs=out_specs,
        ),
        input_output_aliases=aliases or {},
        cost_estimate=cost(micros),
        compiler_params=pltpu.CompilerParams(vmem_limit_bytes=limit),
    )(*operands)


def place_slot(ranks, pieces, wholes, z_count, cuts):
    rows, width = pieces[0].shape
    ends = list(cuts[1:]) + [width]
    given = len(wholes)

    def body(ranks_ref, *refs):
        sources, targets = refs[:4], refs[4 + given :]
        y, c = ranks_ref[1], ranks_ref[2]
        spots = [(y, c), (1 - y, c), (y, 1 - c), (1 - y, 1 - c)]
        for source, (at_y, at_c) in zip(sources, spots):
            for target, begin, end in zip(targets, cuts, ends):
                target[0, at_y, at_c] = source[:, begin:end]

    whole_spec = pl.BlockSpec(memory_space=pl.ANY)
    return call(
        body,
        1.0,
        (1,),
        [pl.BlockSpec((rows, width), lambda i, ranks: (0, 0))] * 4 + [whole_spec] * given,
        [((z_count, 2, 2, rows, end - begin), BF16) for begin, end in zip(cuts, ends)],
        [
            pl.BlockSpec((1, 2, 2, rows, end - begin), lambda i, ranks: (ranks[0], 0, 0, 0, 0))
            for begin, end in zip(cuts, ends)
        ],
        (ranks, *pieces, *wholes),
        aliases={5 + number: number for number in range(given)},
        limit=2 * VMEM,
    )


def place_all(ranks, pieces):
    z_count, rows, width = pieces[0].shape

    def body(ranks_ref, own, side, core, both, target):
        y, c = ranks_ref[1], ranks_ref[2]
        target[0, y, c] = own[0]
        target[0, 1 - y, c] = side[0]
        target[0, y, 1 - c] = core[0]
        target[0, 1 - y, 1 - c] = both[0]

    whole = call(
        body,
        1.0,
        (z_count,),
        [pl.BlockSpec((1, rows, width), lambda i, ranks: (i, 0, 0))] * 4,
        [((z_count, 2, 2, rows, width), BF16)],
        [pl.BlockSpec((1, 2, 2, rows, width), lambda i, ranks: (i, 0, 0, 0, 0))],
        (ranks, *pieces),
    )[0]
    return whole.reshape(z_count * 4 * rows, width)


def product(left, right, dtype):
    rows, depth = left.shape
    width = right.shape[1]
    block = 256 if width % 256 == 0 else width

    def body(ranks_ref, left_ref, right_ref, out_ref):
        out_ref[...] = mm(left_ref[...], right_ref[...]).astype(dtype)

    return call(
        body,
        1.0,
        (width // block,),
        [
            pl.BlockSpec((rows, depth), lambda i, ranks: (0, 0)),
            pl.BlockSpec((depth, block), lambda i, ranks: (0, i)),
        ],
        [((rows, width), dtype)],
        [pl.BlockSpec((rows, block), lambda i, ranks: (0, i))],
        (jnp.zeros((1,), jnp.int32), left, right),
    )[0]


def product_nt(ranks, left, right, groups):
    rows, depth = left.shape
    width = right.shape[0]
    block = 512 if width % 512 == 0 else width
    half = rows // groups // 2

    def body(ranks_ref, left_ref, right_ref, own_ref, other_ref):
        whole = mm_nt(left_ref[...], right_ref[...])
        low = ranks_ref[3] == 0
        for group in range(groups):
            at = group * 2 * half
            first, second = whole[at : at + half], whole[at + half : at + 2 * half]
            to = pl.ds(group * half, half)
            own_ref[to, :] = jnp.where(low, first, second)
            other_ref[to, :] = jnp.where(low, second, first).astype(BF16)

    out_spec = pl.BlockSpec((rows // 2, block), lambda i, ranks: (0, i))
    return call(
        body,
        1.0,
        (width // block,),
        [
            pl.BlockSpec((rows, depth), lambda i, ranks: (0, 0)),
            pl.BlockSpec((block, depth), lambda i, ranks: (i, 0)),
        ],
        [((rows // 2, width), F32), ((rows // 2, width), BF16)],
        [out_spec] * 2,
        (ranks, left, right),
    )


def second_norm(x_ref, mine_ref, got_ref, gain_ref, residual_ref, factor_ref, normed_ref):
    residual = x_ref[...].astype(F32) + mine_ref[...] + got_ref[...].astype(F32)
    factor = inv_root(residual)
    residual_ref[...], factor_ref[...] = residual, factor
    normed_ref[...] = (residual * factor * gain_ref[...]).astype(BF16)


def second_norm_back(
    own_ref, got_ref, held_ref, residual_ref, factor_ref, gain_ref, dy_ref,
    grad_ref, grad_b_ref, term_ref,
):
    grad = own_ref[...].astype(F32) + got_ref[...].astype(F32) + held_ref[...].astype(F32)
    residual, factor = residual_ref[...], factor_ref[...]
    term_ref[...] = jnp.sum(grad * residual * factor, axis=0, keepdims=True)
    grad = dy_ref[...].astype(F32) + norm_back(residual, factor, gain_ref[...], grad)
    grad_ref[...], grad_b_ref[...] = grad, grad.astype(BF16)


def first_norm_back(mine_ref, got_ref, x_ref, factor_ref, gain_ref, grad_ref, out_ref, term_ref):
    grad = mine_ref[...] + got_ref[...].astype(F32)
    values, factor = x_ref[...].astype(F32), factor_ref[...]
    term_ref[...] = jnp.sum(grad * values * factor, axis=0, keepdims=True)
    out_ref[...] = (grad_ref[...] + norm_back(values, factor, gain_ref[...], grad)).astype(BF16)


def product_rows(ranks, lefts, groups, z_count, cuts=1):
    features = lefts[0].shape[1]
    width = groups[0][0].shape[1]
    rows = features // (4 * z_count)
    block = math.lcm(4 * rows, 128)
    span = block // (4 * rows)
    rights = [right for group in groups for right in group]
    each = len(groups[0])
    join = lambda parts: parts[0] if len(parts) == 1 else jnp.concatenate(parts, axis=0)

    def body(ranks_ref, *refs):
        left = join([ref[...] for ref in refs[: len(lefts)]])
        right_refs, out_refs = refs[len(lefts) : -outs], refs[-outs:]
        low = ranks_ref[2] == 0
        here = pl.program_id(0)
        for number in range(len(groups)):
            right = join([ref[...] for ref in right_refs[number * each : (number + 1) * each]])
            keep, sends = out_refs[number], out_refs[len(groups) + number * cuts * z_count :]
            whole = mm_tn(left, right)
            for place in range(span):
                for y in range(2):
                    at = (place * 4 + y * 2) * rows
                    first, second = whole[at : at + rows], whole[at + rows : at + 2 * rows]
                    keep[place, y] = jnp.where(low, first, second).astype(BF16)
                    other = jnp.where(low, second, first).astype(BF16)
                    for z in range(place, z_count, span):

                        @pl.when(here == z // span)
                        def _(target=sends[cuts * z + (y if cuts == 2 else 0)], y=y, other=other):
                            target[y % (2 // cuts)] = other

    parts = cuts * z_count
    outs = len(groups) * (1 + parts)
    keep_spec = pl.BlockSpec((span, 2, rows, width), lambda i, ranks: (i, 0, 0, 0))
    send_spec = pl.BlockSpec((2 // cuts, rows, width), lambda i, ranks: (0, 0, 0))
    out = call(
        body,
        2.0 * len(groups),
        (features // block,),
        [pl.BlockSpec((left.shape[0], block), lambda i, ranks: (0, i)) for left in lefts]
        + [pl.BlockSpec(right.shape, lambda i, ranks: (0, 0)) for right in rights],
        [((z_count, 2, rows, width), BF16)] * len(groups)
        + [((2 // cuts, rows, width), BF16)] * (len(groups) * parts),
        [keep_spec] * len(groups) + [send_spec] * (len(groups) * parts),
        (ranks, *lefts, *rights),
    )
    sends = out[len(groups) :]
    return [
        (out[number], sends[number * parts : (number + 1) * parts])
        for number in range(len(groups))
    ]


def mlp_slot(wg, wu, wd, bg, bu, own, other, dy_own, dy_other):
    features, hidden = wg.shape
    half = own.shape[0]
    block = features // 4 if (features // 4) % 128 == 0 else features

    def body(
        wg_ref, wu_ref, wd_ref, bg_ref, bu_ref, own_ref, other_ref, dyo_ref, dyr_ref,
        hid_ref, dg_ref, du_ref, db_own, db_other, out_own, out_other, sum_ref, b_all, dy_all,
    ):
        b_all[:half], b_all[half:] = own_ref[...], other_ref[...]
        dy_all[:half], dy_all[half:] = dyo_ref[...], dyr_ref[...]
        gate = mm(b_all[...], wg_ref[...]) + bg_ref[...]
        up = mm(b_all[...], wu_ref[...]) + bu_ref[...]
        grad_inner = mm(dy_all[...], wd_ref[...])
        bend = jnp.tanh(GELU_A * (gate + GELU_B * gate * gate * gate))
        gelu = 0.5 * gate * (1.0 + bend)
        slope = 0.5 * (1.0 + bend) + 0.5 * gate * (1.0 - bend * bend) * (
            GELU_A * (1.0 + 3.0 * GELU_B * gate * gate)
        )
        hid_ref[...] = (gelu * up).astype(BF16)
        for row, target, value in (
            (0, dg_ref, grad_inner * up * slope),
            (1, du_ref, grad_inner * gelu),
        ):
            value = value.astype(BF16)
            target[...] = value
            sum_ref[row : row + 1] = jnp.sum(value.astype(F32), axis=0, keepdims=True)
        for step in range(features // block):
            at = pl.ds(step * block, block)
            part = mm_nt(dg_ref[...], wg_ref[at, :]) + mm_nt(du_ref[...], wu_ref[at, :])
            db_own[:, at], db_other[:, at] = part[:half].astype(BF16), part[half:].astype(BF16)
            part = mm_nt(hid_ref[...], wd_ref[at, :])
            out_own[:, at], out_other[:, at] = part[:half].astype(BF16), part[half:].astype(BF16)

    weights = [pltpu.with_memory_space_constraint(w, pltpu.VMEM) for w in (wg, wu, wd)]
    return in_vmem(
        body,
        4.0,
        [((2 * half, hidden), BF16)] * 3 + [((half, features), BF16)] * 4 + [((2, hidden), F32)],
        *(*weights, bg[None], bu[None], own, other, dy_own, dy_other),
        scratch=[pltpu.VMEM((2 * half, features), BF16)] * 2,
    )


def split_columns(grid, shard):
    rows, width = shard.shape
    return shard.reshape(rows, grid.z_count, width // grid.z_count).transpose(1, 0, 2)


def own_rows(ranks, keep, got):
    z_count, _, rows, width = keep.shape
    cuts = len(got) // z_count

    def body(ranks_ref, keep_ref, *refs):
        away_ref, stay_ref = refs[-2:]
        y = ranks_ref[1]
        for z in range(z_count):

            @pl.when(pl.program_id(0) == z)
            def _(got_refs=refs[cuts * z : cuts * z + cuts]):
                halves = [got_refs[at % cuts][at // cuts] for at in (0, 1)]
                sums = [keep_ref[0, at].astype(F32) + halves[at].astype(F32) for at in (0, 1)]
                away_ref[0] = jnp.where(y == 0, sums[1], sums[0]).astype(BF16)
                stay_ref[0] = jnp.where(y == 0, sums[0], sums[1]).astype(BF16)

    block = pl.BlockSpec((1, 2, rows, width), lambda i, ranks: (i, 0, 0, 0))
    whole = pl.BlockSpec((2 // cuts, rows, width), lambda i, ranks: (0, 0, 0))
    half = pl.BlockSpec((1, rows, width), lambda i, ranks: (i, 0, 0))
    shape = ((z_count, rows, width), BF16)
    specs = [block] + [whole] * (cuts * z_count)
    return call(body, 0.5, (z_count,), specs, [shape] * 2, [half] * 2, (ranks, keep, *got))


def plus(left, right):
    z_count, rows, width = left.shape

    def body(ranks_ref, left_ref, right_ref, out_ref):
        out_ref[...] = (left_ref[...].astype(F32) + right_ref[...].astype(F32)).astype(BF16)

    block = pl.BlockSpec((1, rows, width), lambda i, ranks: (i, 0, 0))
    operands = (jnp.zeros((1,), jnp.int32), left, right)
    return call(body, 0.5, (z_count,), [block] * 2, [(left.shape, BF16)], [block], operands)[0]


def ring_sum(grid, parts, held, step):
    _, rows, width = parts.shape
    dtype = BF16 if step < grid.z_count else F32
    given = [] if held is None else [held]

    def body(ranks_ref, part_ref, *refs):
        part = part_ref[0].astype(F32)
        refs[-1][...] = (part + refs[0][...].astype(F32) if given else part).astype(dtype)

    full = pl.BlockSpec((rows, width), lambda i, ranks: (0, 0))
    spot = grid.behind(step).astype(jnp.int32)[None]
    return call(
        body,
        1.0,
        (1,),
        [pl.BlockSpec((1, rows, width), lambda i, ranks: (ranks[0], 0, 0))] + [full] * len(given),
        [((rows, width), dtype)],
        [full],
        (spot, parts, *given),
    )[0]


def add(*values):
    def body(*refs):
        total = refs[0][...].astype(F32)
        for ref in refs[1:-1]:
            total += ref[...].astype(F32)
        refs[-1][...] = total.astype(BF16)

    values = [value for value in values if value is not None]
    return in_vmem(body, 1.0, [(values[0].shape, BF16)], *values)[0]


def collect_columns(parts, turn=False):
    count, rows, width = parts.shape

    def body(parts_ref, out_ref):
        if turn:
            for step in range(count):
                out_ref[step * width : (step + 1) * width, :] = parts_ref[step].astype(F32).T
        else:
            pieces = [parts_ref[step].astype(F32) for step in range(count)]
            out_ref[...] = jnp.concatenate(pieces, axis=1)

    shape = (count * width, rows) if turn else (rows, count * width)
    return in_vmem(body, 3.0, [(shape, F32)], parts)[0]


def turned(value, cosine, sine):
    first = value[:, : cosine.shape[1]]
    first = first * cosine + pltpu.roll(first, first.shape[1] // 2, 1) * sine
    return jnp.concatenate([first, value[:, cosine.shape[1] :]], axis=1)


def softmax(query, key, bias):
    scores = mm_nt(query, key) + bias
    expon = jnp.exp(scores - jnp.max(scores, axis=-1, keepdims=True))
    return expon / jnp.sum(expon, axis=-1, keepdims=True)


def attend(scale, q_ref, k_ref, v_ref, cos_ref, sin_ref, bias_ref, rq_ref, o_ref):
    size = k_ref.shape[1]
    for head in range(rq_ref.shape[1] // size):
        at = pl.ds(head * size, size)
        query = (turned(q_ref[:, at], cos_ref[...], sin_ref[...]) * scale).astype(BF16)
        rq_ref[:, at] = query
        probs = softmax(query, k_ref[...], bias_ref[...]).astype(BF16)
        o_ref[:, at] = mm(probs, v_ref[...]).astype(BF16)


def attend_back(
    scale, do_ref, rq_ref, k_ref, v_ref, cos_ref, sin_ref, bias_ref, dq_ref, dk_ref, dv_ref
):
    size = k_ref.shape[1]
    cosine, sine = cos_ref[...], -sin_ref[...]
    grad_key = jnp.zeros(dk_ref.shape, F32)
    grad_value = jnp.zeros(dv_ref.shape, F32)
    for head in range(rq_ref.shape[1] // size):
        at = pl.ds(head * size, size)
        query, grad_out = rq_ref[:, at], do_ref[:, at]
        probs = softmax(query, k_ref[...], bias_ref[...])
        grad_value += mm_tn(probs.astype(BF16), grad_out)
        grad_probs = mm_nt(grad_out, v_ref[...])
        delta = jnp.sum(probs * grad_probs, axis=-1, keepdims=True)
        grad_scores = (probs * (grad_probs - delta)).astype(BF16)
        grad_query = mm(grad_scores, k_ref[...]) * scale
        dq_ref[:, at] = turned(grad_query, cosine, sine).astype(BF16)
        grad_key += mm_tn(grad_scores, query)
    dk_ref[...] = turned(grad_key, cosine, sine)
    dv_ref[...] = grad_value


def in_vmem(body, micros, shapes, *operands, scratch=()):
    spec = pl.BlockSpec(memory_space=pltpu.VMEM)
    return pl.pallas_call(
        body,
        out_shape=[jax.ShapeDtypeStruct(shape, dtype) for shape, dtype in shapes],
        in_specs=[spec] * len(operands),
        out_specs=[spec] * len(shapes),
        scratch_shapes=list(scratch),
        cost_estimate=cost(micros),
        compiler_params=pltpu.CompilerParams(vmem_limit_bytes=VMEM),
    )(*operands)


def shards(
    inputs,
    gain_attn,
    w_query,
    w_keyval,
    w_output,
    gain_mlp,
    w_gate,
    b_gate,
    w_up,
    b_up,
    w_down,
    b_down,
    segment_ids,
    cotangent,
    total,
):
    grid = Grid(total)
    count = grid.z_count
    micro, length, width = inputs.shape
    tokens = micro * length
    head_dim = w_keyval.shape[1] // 2
    query_width = w_query.shape[1]
    scale = head_dim ** (-0.5)

    def halves(value):
        value = value.reshape(micro, 2, length // 2, value.shape[-1])
        return tuple(take(value, i, 1).reshape(tokens // 2, -1) for i in (grid.x, 1 - grid.x))

    def join(mine, other):
        shape = (micro, length // 2, mine.shape[-1])
        return pair(grid.x, mine.reshape(shape), other.reshape(shape), 1).reshape(tokens, -1)

    ranks = jnp.stack([grid.z, grid.y, grid.c, grid.x]).astype(jnp.int32)
    keyval_half = lax.dynamic_slice_in_dim(w_keyval, grid.x * head_dim, head_dim, 1)
    shards_of = [split_columns(grid, shard) for shard in (w_gate, w_up, w_down.T)]
    dy_half = halves(cotangent.reshape(tokens, width))[0]
    segment = segment_ids.reshape(micro, length)
    offsets = jax.vmap(positions)(segment).reshape(tokens)
    quarter = head_dim // 4
    freqs = 10000.0 ** (-jnp.arange(quarter, dtype=F32) / quarter)
    angle = offsets[:, None] * freqs[None, :]
    cosine, sine = jnp.cos(angle), jnp.sin(angle)
    cosine = jnp.concatenate([cosine, cosine], axis=1)
    sine = jnp.concatenate([-sine, sine], axis=1)
    index = jnp.arange(tokens, dtype=jnp.int32)
    seg = segment.reshape(tokens)
    allowed = (
        (seg[:, None] == seg[None, :])
        & (index[:, None] // length == index[None, :] // length)
        & (index[None, :] <= index[:, None])
    )
    bias = jnp.where(allowed, 0.0, -1e30).astype(F32)
    hidden_x = inputs.reshape(tokens, width).astype(F32)
    factor_one = inv_root(hidden_x)
    normed = (hidden_x * factor_one * gain_attn).astype(BF16)
    x_half, factor_half = halves(inputs.reshape(tokens, width))[0], halves(factor_one)[0]
    half_shape = (tokens // 2, width)

    def mlp(step):
        pieces = (b_slots[step], b_others[step], dy_slots[step], dy_others[step])
        results.append(mlp_slot(wg, wu, wd, bg, bu, *grid.gate(pieces)))
        grid.wait(*results[-1])

    slots = [jnp.concatenate([w_query, keyval_half, w_output.T], axis=1)]
    across, beside, both, wholes = [], [], [], []
    dy_slots, dy_others = [dy_half], []

    def place(step):
        pieces = [slots[step], across[step], beside[step], both[step]]
        spot = jnp.stack([grid.behind(step), grid.y, grid.c]).astype(jnp.int32)
        return place_slot(spot, pieces, wholes, count, (0, query_width + head_dim))

    for step in range(count):
        if step + 1 < count:
            slots.append(grid.next_z(slots[step]))
        else:
            gate_mine = grid.along_z(shards_of[0])
        across.append(grid.over_y(slots[step]))
        beside.append(grid.over_c(slots[step]))
        if step == 0:
            dy_others.append(grid.over_x(dy_half))
            grid.wait(shards_of[0])
        else:
            both.append(grid.over_c(across[step - 1]))
            wholes = place(step - 1)
            grid.wait(*wholes, beside[step])
        if step == 1:
            grid.wait(shards_of[1], normed, x_half, dy_others[0])
        if step == 2:
            grid.wait(shards_of[2], cosine, sine, bias)
        if step + 1 < count:
            grid.wait(slots[step + 1], across[step])
    grid.wait(across[-1])
    both.append(grid.over_c(across[-1]))
    grid.wait(gate_mine)

    up_mine = grid.along_z(shards_of[1])
    gate_across, gate_beside = grid.over_y(gate_mine), grid.over_c(gate_mine)
    wholes = place(count - 1)
    w_qkv, w_out = [whole.reshape(width, -1) for whole in wholes]
    queries = product(normed, w_qkv, F32)
    keyval = queries[:, query_width:]
    front, back = keyval[:, :quarter], keyval[:, quarter : 2 * quarter]
    swapped = jnp.concatenate([back, front], axis=1)
    key = jnp.concatenate(
        [keyval[:, : 2 * quarter] * cosine + swapped * sine, keyval[:, 2 * quarter :]], axis=1
    )
    keyval = jnp.where(grid.x == 0, key, keyval).astype(BF16)
    keyval_other = grid.over_x(keyval)
    grid.wait(keyval_other)
    rot_key = jnp.where(grid.x == 0, keyval, keyval_other)
    values_in = jnp.where(grid.x == 0, keyval_other, keyval)
    shape = (tokens, query_width)
    rot_query, mixed_b = in_vmem(
        partial(attend, scale),
        1.2,
        [(shape, BF16), (shape, BF16)],
        *(queries, rot_key, values_in, cosine, sine, bias),
    )
    mine, other = product_nt(ranks, mixed_b, w_out, micro)
    grid.wait(mine)
    attended = grid.over_x(other)
    grid.wait(up_mine)
    down_mine = grid.along_z(shards_of[2])
    grid.wait(gate_across)
    up_across, up_beside = grid.over_y(up_mine), grid.over_c(up_mine)
    gate_both = grid.over_c(gate_across)
    grid.wait(attended)
    residual, factor_two, normed_two = in_vmem(
        second_norm,
        0.5,
        [(half_shape, F32), ((tokens // 2, 1), F32), (half_shape, BF16)],
        *(x_half, mine, attended, gain_mlp[None]),
    )
    grid.wait(normed_two)
    b_slots, b_others = [normed_two], [grid.over_x(normed_two)]
    b_slots.append(grid.next_z(normed_two))
    dy_slots.append(grid.next_z(dy_half))
    wg = place_all(ranks, [gate_mine, gate_across, gate_beside, gate_both])
    grid.wait(wg, b_others[0])
    grid.wait(down_mine)

    grid.wait(up_across)
    down_across, down_beside = grid.over_y(down_mine), grid.over_c(down_mine)
    grid.wait(b_slots[1], dy_slots[1])
    for step in range(1, count - 1):
        b_slots.append(grid.next_z(b_slots[step]))
        dy_slots.append(grid.next_z(dy_slots[step]))
        b_others.append(grid.over_x(b_slots[step]))
        dy_others.append(grid.over_x(dy_slots[step]))
        if step == 1:
            up_both = grid.over_c(up_across)
            wu = place_all(ranks, [up_mine, up_across, up_beside, up_both])
            grid.wait(wu)
        if step == 2:
            grid.wait(down_across)
            down_both = grid.over_c(down_across)
            wd = place_all(ranks, [down_mine, down_across, down_beside, down_both])
            hidden = wg.shape[1]
            spot = grid.z * hidden
            bg = lax.dynamic_slice_in_dim(b_gate, spot, hidden, 0)
            bu = lax.dynamic_slice_in_dim(b_up, spot, hidden, 0)
            grid.wait(wd, bg, bu)
            results = []
            mlp(0)
        grid.wait(b_slots[step + 1], dy_slots[step + 1])
        grid.wait(b_others[step], dy_others[step])
    b_others.append(grid.over_x(b_slots[-1]))
    dy_others.append(grid.over_x(dy_slots[-1]))
    mlp(1)

    db_got = [None, grid.over_x(results[1][4])]
    for step in range(2, count):
        if step == count - 1:
            grid.wait(b_others[-1], dy_others[-1])
        mlp(step)
        db_got.append(grid.over_x(results[step][4]))
    inner_slots, gate_slots, up_slots, db_own, db_other, out_own, out_other, sums = zip(*results)
    dy_all = [piece for two in zip(dy_slots, dy_others) for piece in two]
    b_all = [piece for two in zip(b_slots, b_others) for piece in two]
    grid.wait(db_got[1])
    db_held = add(db_own[1], db_got[1])
    grid.wait(db_held)
    db_next = grid.next_z(db_held)
    out_got = [None, grid.over_x(out_other[1])] + [None] * (count - 2)
    down_keep, down_send = product_rows(ranks, grid.gate(dy_all), [inner_slots], count, 2)[0]
    grid.wait(down_keep)
    down_got = [grid.over_c(send) for send in down_send]
    for step in range(2, count):
        grid.wait(db_next, *db_got[step : count if step == 2 else step + 1])
        db_held = add(db_own[step], db_got[step], db_next)
        grid.wait(db_held)
        db_next = grid.next_z(db_held)
        if step == 2:
            db_got[0] = grid.over_x(db_other[0])
            grid.wait(*down_got)
            down_away, down_stay = own_rows(ranks, grid.gate(down_keep), down_got)
            grid.wait(down_away)
            down_back = grid.over_y(down_away)
            (gate_keep, gate_send), (up_keep, up_send) = product_rows(
                ranks, grid.gate(b_all), [gate_slots, up_slots], count
            )
            grid.wait(gate_keep)
            gate_got = [grid.over_c(send) for send in gate_send]
    grid.wait(db_got[0], out_got[1])
    grid.wait(*gate_got)
    up_got = [grid.over_c(send) for send in up_send]
    gate_away, gate_stay = own_rows(ranks, grid.gate(gate_keep), gate_got)
    branch = add(out_own[1], out_got[1])
    grid.wait(gate_away, branch)
    grid.wait(db_next, down_back)
    gate_back = grid.over_y(gate_away)
    grad_resid, grad_resid_b, gain_mlp_term = in_vmem(
        second_norm_back,
        0.5,
        [(half_shape, F32), (half_shape, BF16), ((1, width), F32)],
        *(db_own[0], db_got[0], grid.gate(db_next), residual, factor_two, gain_mlp[None], dy_half),
    )
    grid.wait(grad_resid_b)
    grad_resid_other = grid.over_x(grad_resid_b)
    branch = grid.next_z(branch)
    down_rows = plus(grid.gate(down_stay), down_back)
    grid.wait(down_rows, *up_got)
    down_parts = grid.along_z(down_rows)
    up_away, up_stay = own_rows(ranks, grid.gate(up_keep), up_got)
    grid.wait(up_away)
    grid.wait(grad_resid_other)

    grad_resid_b = join(grad_resid_b, grad_resid_other)
    grad_mixed = product(grid.gate(grad_resid_b), w_out, BF16)
    shape_kv = (tokens, head_dim)
    grad_query, grad_key, grad_values = in_vmem(
        partial(attend_back, scale),
        0.5,
        [(shape, BF16), (shape_kv, F32), (shape_kv, F32)],
        *(grad_mixed, rot_query, rot_key, values_in, cosine, sine, bias),
    )
    grid.wait(grad_query, gate_back)
    up_back = grid.over_y(up_away)
    grad_own = jnp.where(grid.x == 0, grad_key, grad_values)
    grad_other = grid.over_x(jnp.where(grid.x == 0, grad_values, grad_key))
    out_keep, out_send = product_rows(ranks, [grid.gate(grad_resid_b)], [[mixed_b]], count)[0]
    grid.wait(out_keep)
    out_got_c = [grid.over_c(send) for send in out_send]
    grid.wait(grad_other)
    out_got[2] = grid.over_x(out_other[2])
    gate_rows = plus(grid.gate(gate_stay), gate_back)
    grid.wait(gate_rows, *out_got_c)
    out_away, out_stay = own_rows(ranks, grid.gate(out_keep), out_got_c)
    grid.wait(out_away)
    grid.wait(down_parts)
    gate_parts = grid.along_z(gate_rows)
    grad_keyval = (grad_own + grad_other).astype(BF16)
    grad_qkv = jnp.concatenate([grad_query, grad_keyval], axis=1)
    mine, other = product_nt(ranks, grid.gate(grad_qkv), w_qkv, micro)
    grid.wait(mine, branch, out_got[2])
    grad_normed = grid.over_x(other)
    branch = add(out_own[2], out_got[2], branch)
    grid.wait(branch)
    branch = grid.next_z(branch)
    cuts = (
        jnp.concatenate([grad_keyval, grad_query[:, : 2 * head_dim]], axis=1),
        grad_query[:, 2 * head_dim :],
    )
    products = [product_rows(ranks, [grid.gate(normed)], [[cut]], count)[0] for cut in cuts]
    qkv_keep, qkv_send = zip(*products)
    grid.wait(*qkv_keep)
    grid.wait(up_back)
    out_back = grid.over_y(out_away)
    up_rows = plus(grid.gate(up_stay), up_back)
    qkv_got = [[grid.over_c(send) for send in sends] for sends in qkv_send]
    grid.wait(up_rows, grad_normed)
    out_got[3] = grid.over_x(out_other[3])
    grid.wait(gate_parts)
    up_parts = grid.along_z(up_rows)
    grid.wait(*qkv_got[0], *qkv_got[1])
    qkv_away, qkv_stay = zip(
        *[own_rows(ranks, grid.gate(keep), got) for keep, got in zip(qkv_keep, qkv_got)]
    )
    grid.wait(*qkv_away)
    grid.wait(branch, out_got[3])
    out_got[0] = grid.over_x(out_other[0])
    branch = add(out_own[3], out_got[3], branch)
    grid.wait(branch)
    branch = grid.next_z(branch)
    for step in range(4, count):
        out_got[step] = grid.over_x(out_other[step])
        branch = grid.next_z(add(out_own[step], out_got[step], branch))
    grad_input, gain_attn_term = in_vmem(
        first_norm_back,
        0.5,
        [(half_shape, BF16), ((1, width), F32)],
        *(mine, grad_normed, x_half, factor_half, gain_attn[None], grid.gate(grad_resid)),
    )
    grid.wait(grad_input)
    narrow = jnp.concatenate(
        [gain_attn_term, gain_mlp_term, jnp.sum(dy_half.astype(F32), axis=0)[None]]
    )
    grid.wait(narrow, out_got[0])
    narrow_other = grid.over_x(narrow)
    grid.wait(out_back)
    qkv_back = [grid.over_y(qkv_away[0])]
    out_rows = plus(grid.gate(out_stay), out_back)
    out_held = ring_sum(grid, out_rows, None, 1)
    grid.wait(out_held, narrow_other)
    grid.wait(up_parts)
    out_held = grid.next_z(out_held)

    ffn = b_gate.shape[0]
    wide = jnp.zeros((2, ffn), F32)
    wide = lax.dynamic_update_slice(wide, sum(sums), (0, spot)).reshape(-1)
    small = jnp.concatenate([(narrow + narrow_other).reshape(-1), wide])
    small_other = grid.over_c(small)
    grid.wait(small_other)
    small = small + small_other
    grid.wait(small)
    small_other = grid.over_y(small)
    grid.wait(branch)
    outputs = (residual + add(out_own[0], out_got[0], branch).astype(F32) + b_down).astype(BF16)
    grid.wait(outputs)
    outputs_other = grid.over_x(outputs)
    down_grad = collect_columns(grid.gate(down_parts), True)
    grid.wait(down_grad)
    grid.wait(qkv_back[0], small_other)
    qkv_back.append(grid.over_y(qkv_away[1]))
    qkv_rows = [plus(grid.gate(qkv_stay[0]), qkv_back[0])]
    qkv_held = ring_sum(grid, qkv_rows[0], None, 1)
    small = small + small_other
    grid.wait(qkv_held, small)
    qkv_held = [grid.next_z(qkv_held), None]
    small_other = lax.ppermute(grid.gate(small), "dp", grid.flips[0])
    for step in range(2, count):
        grid.wait(out_held)
        out_held = ring_sum(grid, out_rows, out_held, step)
        grid.wait(out_held)
        out_held = grid.next_z(out_held)
        if step == 2:
            grid.wait(qkv_held[0], small_other)
            small = small + small_other
            qkv_held[0] = ring_sum(grid, qkv_rows[0], qkv_held[0], 2)
            grid.wait(qkv_held[0], small)
            qkv_held[0] = grid.next_z(qkv_held[0])
    for number, flip in enumerate(grid.flips[1:]):
        small_other = lax.ppermute(grid.gate(small), "dp", flip)
        if number + 2 < len(grid.flips):
            grid.wait(small_other)
            small = small + small_other
    gate_grad = collect_columns(grid.gate(gate_parts))
    up_grad = collect_columns(grid.gate(up_parts))
    grid.wait(gate_grad, up_grad, outputs_other)
    grad_input_other = grid.over_x(grad_input)
    grid.wait(qkv_back[1])
    qkv_rows.append(plus(grid.gate(qkv_stay[1]), qkv_back[1]))
    qkv_held[1] = ring_sum(grid, qkv_rows[1], None, 1)
    grid.wait(qkv_held[1])
    qkv_held[1] = grid.next_z(qkv_held[1])
    grid.wait(out_held)
    out_grad = ring_sum(grid, out_rows, out_held, count).T
    for step in range(3, count + 1):
        grid.wait(qkv_held[0])
        qkv_held[0] = ring_sum(grid, qkv_rows[0], qkv_held[0], step)
        grid.wait(qkv_held[0])
        if step < count:
            qkv_held[0] = grid.next_z(qkv_held[0])
        else:
            keyval_grad = qkv_held[0][:, :head_dim]
            keyval_other = grid.over_x(keyval_grad)
        grid.wait(qkv_held[1])
        qkv_held[1] = ring_sum(grid, qkv_rows[1], qkv_held[1], step - 1)
        grid.wait(qkv_held[1])
        qkv_held[1] = grid.next_z(qkv_held[1])
    grid.wait(small_other)
    small = small + small_other
    grid.wait(grad_input_other, keyval_other)
    qkv_held[1] = ring_sum(grid, qkv_rows[1], qkv_held[1], count)
    query_grad = jnp.concatenate([qkv_held[0][:, head_dim:], qkv_held[1]], axis=1)
    keyval_grad = pair(grid.x, keyval_grad, keyval_other, 1)
    keyval_grad = keyval_grad.reshape(keyval_grad.shape[0], 2 * head_dim)
    return (
        join(outputs, outputs_other).reshape(inputs.shape),
        join(grad_input, grad_input_other).reshape(inputs.shape),
        small[:width],
        query_grad,
        keyval_grad,
        out_grad,
        small[width : 2 * width],
        gate_grad,
        small[3 * width : 3 * width + ffn],
        up_grad,
        small[3 * width + ffn :],
        down_grad,
        small[2 * width : 3 * width],
    )


def solution(mesh):
    in_specs = (
        P(None, "dp", None),
        P(),
        P("dp", "mp"),
        P("dp", None),
        P("mp", "dp"),
        P(),
        P("dp", "mp"),
        P("mp"),
        P("dp", "mp"),
        P("mp"),
        P("mp", "dp"),
        P(),
        P(None, "dp", None),
        P(None, "dp", None),
    )
    out_specs = (
        P(None, "dp", None),
        P(None, "dp", None),
        P(),
        P("dp", "mp"),
        P("dp", None),
        P("mp", "dp"),
        P(),
        P("dp", "mp"),
        P("mp"),
        P("dp", "mp"),
        P("mp"),
        P("mp", "dp"),
        P(),
    )
    body = partial(shards, total=mesh.shape["dp"])
    return jax.shard_map(body, mesh=mesh, in_specs=in_specs, out_specs=out_specs, check_vma=False)
```

```python
import math
from functools import partial

import jax
import jax.numpy as jnp
from jax import lax
from jax.experimental import pallas as pl
from jax.experimental.pallas import tpu as pltpu
from jax.sharding import PartitionSpec as P

EPS = 1e-06
F32 = jnp.float32
BF16 = jnp.bfloat16
VMEM = 24 * 2**20
SCALE = 12.0
GELU_A, GELU_B = math.sqrt(2.0 / math.pi), 0.044715


def positions(segment):
    count = segment.shape[0]
    index = jnp.arange(count, dtype=jnp.int32)
    fresh = jnp.concatenate([jnp.ones((1,), jnp.bool_), segment[1:] != segment[:-1]])
    starts = lax.cummax(jnp.where(fresh, index, 0), axis=0)
    return (index - starts).astype(F32)


def inv_root(values):
    return lax.rsqrt(jnp.mean(values * values, axis=-1, keepdims=True) + EPS)


def norm_back(values, factor, gain, grad_norm):
    scaled = gain * grad_norm
    return factor * scaled - values * factor**3 * jnp.mean(scaled * values, axis=-1, keepdims=True)


def mm(left, right):
    return jnp.dot(left, right, preferred_element_type=F32)


def mm_nt(left, right):
    return lax.dot_general(left, right, (((1,), (1,)), ((), ())), preferred_element_type=F32)


def mm_tn(left, right):
    return lax.dot_general(left, right, (((0,), (0,)), ((), ())), preferred_element_type=F32)


class Grid:
    def __init__(self, total):
        self.z_count = total // 4
        spots = [(z, y, c) for z in range(self.z_count) for y in range(2) for c in range(2)]
        at = lambda z, y, c: (z * 2 + y) * 2 + c
        self.swap_y = [(at(z, y, c), at(z, 1 - y, c)) for z, y, c in spots]
        self.swap_c = [(at(z, y, c), at(z, y, 1 - c)) for z, y, c in spots]
        self.ring = lambda step: [
            (at(z, y, c), at((z + step) % self.z_count, y, c)) for z, y, c in spots
        ]
        self.flips = []
        step = 1
        while step < self.z_count:
            self.flips.append([(at(z, y, c), at(z ^ step, y, c)) for z, y, c in spots])
            step *= 2
        self.lines = [
            [at(z, y, c) for z in range(self.z_count)] for y in range(2) for c in range(2)
        ]
        index = lax.axis_index("dp")
        self.c = index % 2
        self.y = (index // 2) % 2
        self.z = index // 4
        self.x = lax.axis_index("mp")
        self.token = jnp.zeros((), F32)

    def wait(self, *values):
        self.token = lax.optimization_barrier((self.token, values))[0]

    def gate(self, value):
        return lax.optimization_barrier((value, self.token))[0]

    def over_y(self, value):
        return lax.ppermute(self.gate(value), "dp", self.swap_y)

    def over_c(self, value):
        return lax.ppermute(self.gate(value), "dp", self.swap_c)

    def over_x(self, value):
        return lax.ppermute(self.gate(value), "mp", [(0, 1), (1, 0)])

    def next_z(self, value, step=1):
        return lax.ppermute(self.gate(value), "dp", self.ring(step))

    def along_z(self, value):
        value = self.gate(value)
        return lax.all_to_all(value, "dp", 0, 0, axis_index_groups=self.lines, tiled=True)

    def behind(self, step):
        return lax.rem(self.z - step + 2 * self.z_count, self.z_count)


def pair(index, mine, other, axis):
    return jnp.where(
        index == 0, jnp.stack([mine, other], axis=axis), jnp.stack([other, mine], axis=axis)
    )


def take(value, index, axis):
    return lax.dynamic_index_in_dim(value, index, axis, keepdims=False)


def cost(micros):
    micros = micros / SCALE
    flops, moved = int(micros * 1.15e9), int(micros * 3.69e6)
    return pl.CostEstimate(flops=flops, bytes_accessed=moved, transcendentals=0)


def call(body, micros, grid, in_specs, outs, out_specs, operands, aliases=None, limit=VMEM):
    return pl.pallas_call(
        body,
        out_shape=[jax.ShapeDtypeStruct(shape, dtype) for shape, dtype in outs],
        grid_spec=pltpu.PrefetchScalarGridSpec(
            num_scalar_prefetch=1,
            grid=grid,
            in_specs=in_specs,
            out_specs=out_specs,
        ),
        input_output_aliases=aliases or {},
        cost_estimate=cost(micros),
        compiler_params=pltpu.CompilerParams(vmem_limit_bytes=limit),
    )(*operands)


def place_slot(ranks, pieces, wholes, z_count, cuts):
    rows, width = pieces[0].shape
    ends = list(cuts[1:]) + [width]
    given = len(wholes)

    def body(ranks_ref, *refs):
        sources, targets = refs[:4], refs[4 + given :]
        y, c = ranks_ref[1], ranks_ref[2]
        spots = [(y, c), (1 - y, c), (y, 1 - c), (1 - y, 1 - c)]
        for source, (at_y, at_c) in zip(sources, spots):
            for target, begin, end in zip(targets, cuts, ends):
                target[0, at_y, at_c] = source[:, begin:end]

    whole_spec = pl.BlockSpec(memory_space=pl.ANY)
    return call(
        body,
        1.0,
        (1,),
        [pl.BlockSpec((rows, width), lambda i, ranks: (0, 0))] * 4 + [whole_spec] * given,
        [((z_count, 2, 2, rows, end - begin), BF16) for begin, end in zip(cuts, ends)],
        [
            pl.BlockSpec((1, 2, 2, rows, end - begin), lambda i, ranks: (ranks[0], 0, 0, 0, 0))
            for begin, end in zip(cuts, ends)
        ],
        (ranks, *pieces, *wholes),
        aliases={5 + number: number for number in range(given)},
        limit=2 * VMEM,
    )


def place_all(ranks, pieces):
    z_count, rows, width = pieces[0].shape

    def body(ranks_ref, own, side, core, both, target):
        y, c = ranks_ref[1], ranks_ref[2]
        target[0, y, c] = own[0]
        target[0, 1 - y, c] = side[0]
        target[0, y, 1 - c] = core[0]
        target[0, 1 - y, 1 - c] = both[0]

    whole = call(
        body,
        1.0,
        (z_count,),
        [pl.BlockSpec((1, rows, width), lambda i, ranks: (i, 0, 0))] * 4,
        [((z_count, 2, 2, rows, width), BF16)],
        [pl.BlockSpec((1, 2, 2, rows, width), lambda i, ranks: (i, 0, 0, 0, 0))],
        (ranks, *pieces),
    )[0]
    return whole.reshape(z_count * 4 * rows, width)


def product(left, right, dtype):
    rows, depth = left.shape
    width = right.shape[1]
    block = 256 if width % 256 == 0 else width

    def body(ranks_ref, left_ref, right_ref, out_ref):
        out_ref[...] = mm(left_ref[...], right_ref[...]).astype(dtype)

    return call(
        body,
        1.0,
        (width // block,),
        [
            pl.BlockSpec((rows, depth), lambda i, ranks: (0, 0)),
            pl.BlockSpec((depth, block), lambda i, ranks: (0, i)),
        ],
        [((rows, width), dtype)],
        [pl.BlockSpec((rows, block), lambda i, ranks: (0, i))],
        (jnp.zeros((1,), jnp.int32), left, right),
    )[0]


def product_nt(ranks, left, right, groups):
    rows, depth = left.shape
    width = right.shape[0]
    block = 512 if width % 512 == 0 else width
    half = rows // groups // 2

    def body(ranks_ref, left_ref, right_ref, own_ref, other_ref):
        whole = mm_nt(left_ref[...], right_ref[...])
        low = ranks_ref[3] == 0
        for group in range(groups):
            at = group * 2 * half
            first, second = whole[at : at + half], whole[at + half : at + 2 * half]
            to = pl.ds(group * half, half)
            own_ref[to, :] = jnp.where(low, first, second)
            other_ref[to, :] = jnp.where(low, second, first).astype(BF16)

    out_spec = pl.BlockSpec((rows // 2, block), lambda i, ranks: (0, i))
    return call(
        body,
        1.0,
        (width // block,),
        [
            pl.BlockSpec((rows, depth), lambda i, ranks: (0, 0)),
            pl.BlockSpec((block, depth), lambda i, ranks: (i, 0)),
        ],
        [((rows // 2, width), F32), ((rows // 2, width), BF16)],
        [out_spec] * 2,
        (ranks, left, right),
    )


def second_norm(x_ref, mine_ref, got_ref, gain_ref, residual_ref, factor_ref, normed_ref):
    residual = x_ref[...].astype(F32) + mine_ref[...] + got_ref[...].astype(F32)
    factor = inv_root(residual)
    residual_ref[...], factor_ref[...] = residual, factor
    normed_ref[...] = (residual * factor * gain_ref[...]).astype(BF16)


def second_norm_back(
    own_ref, got_ref, held_ref, residual_ref, factor_ref, gain_ref, bias_ref, dy_ref,
    grad_ref, grad_b_ref, term_ref, out_ref,
):
    both = [
        own_ref[at].astype(F32) + got_ref[at].astype(F32) + held_ref[at].astype(F32) for at in (0, 1)
    ]
    residual, factor = residual_ref[...], factor_ref[...]
    out_ref[...] = (residual + both[1] + bias_ref[...]).astype(BF16)
    term_ref[...] = jnp.sum(both[0] * residual * factor, axis=0, keepdims=True)
    grad = dy_ref[...].astype(F32) + norm_back(residual, factor, gain_ref[...], both[0])
    grad_ref[...], grad_b_ref[...] = grad, grad.astype(BF16)


def first_norm_back(mine_ref, got_ref, x_ref, factor_ref, gain_ref, grad_ref, out_ref, term_ref):
    grad = mine_ref[...] + got_ref[...].astype(F32)
    values, factor = x_ref[...].astype(F32), factor_ref[...]
    term_ref[...] = jnp.sum(grad * values * factor, axis=0, keepdims=True)
    out_ref[...] = (grad_ref[...] + norm_back(values, factor, gain_ref[...], grad)).astype(BF16)


def product_rows(ranks, lefts, groups, z_count, cuts=1, beside=False):
    features = lefts[0].shape[1]
    width = sum(right.shape[1] for right in groups[0]) if beside else groups[0][0].shape[1]
    rows = features // (4 * z_count)
    block = math.lcm(4 * rows, 128)
    span = block // (4 * rows)
    rights = [right for group in groups for right in group]
    each = len(groups[0])
    join = lambda parts: parts[0] if len(parts) == 1 else jnp.concatenate(parts, axis=0)

    def body(ranks_ref, *refs):
        left = [ref[...] for ref in refs[: len(lefts)]]
        left = left if beside else join(left)
        right_refs, out_refs = refs[len(lefts) : -outs], refs[-outs:]
        low = ranks_ref[2] == 0
        here = pl.program_id(0)
        for number in range(len(groups)):
            right = [ref[...] for ref in right_refs[number * each : (number + 1) * each]]
            keep, sends = out_refs[number], out_refs[len(groups) + number * cuts * z_count :]
            if beside:
                whole = jnp.concatenate([mm_tn(a, b) for a, b in zip(left, right)], axis=1)
            else:
                whole = mm_tn(left, join(right))
            for place in range(span):
                for y in range(2):
                    at = (place * 4 + y * 2) * rows
                    first, second = whole[at : at + rows], whole[at + rows : at + 2 * rows]
                    keep[place, y] = jnp.where(low, first, second).astype(BF16)
                    other = jnp.where(low, second, first).astype(BF16)
                    for z in range(place, z_count, span):

                        @pl.when(here == z // span)
                        def _(target=sends[cuts * z + (y if cuts == 2 else 0)], y=y, other=other):
                            target[y % (2 // cuts)] = other

    parts = cuts * z_count
    outs = len(groups) * (1 + parts)
    keep_spec = pl.BlockSpec((span, 2, rows, width), lambda i, ranks: (i, 0, 0, 0))
    send_spec = pl.BlockSpec((2 // cuts, rows, width), lambda i, ranks: (0, 0, 0))
    out = call(
        body,
        2.0 * len(groups),
        (features // block,),
        [pl.BlockSpec((left.shape[0], block), lambda i, ranks: (0, i)) for left in lefts]
        + [pl.BlockSpec(right.shape, lambda i, ranks: (0, 0)) for right in rights],
        [((z_count, 2, rows, width), BF16)] * len(groups)
        + [((2 // cuts, rows, width), BF16)] * (len(groups) * parts),
        [keep_spec] * len(groups) + [send_spec] * (len(groups) * parts),
        (ranks, *lefts, *rights),
    )
    sends = out[len(groups) :]
    return [
        (out[number], sends[number * parts : (number + 1) * parts])
        for number in range(len(groups))
    ]


def mlp_slot(wg, wu, wd, bg, bu, own, other, dy_own, dy_other):
    features, hidden = wg.shape
    half = own.shape[0]
    block = features // 4 if (features // 4) % 128 == 0 else features

    def body(
        wg_ref, wu_ref, wd_ref, bg_ref, bu_ref, own_ref, other_ref, dyo_ref, dyr_ref,
        hid_ref, dg_ref, du_ref, own_back, other_back, sum_ref, b_all, dy_all,
    ):
        b_all[:half], b_all[half:] = own_ref[...], other_ref[...]
        dy_all[:half], dy_all[half:] = dyo_ref[...], dyr_ref[...]
        gate = mm(b_all[...], wg_ref[...]) + bg_ref[...]
        up = mm(b_all[...], wu_ref[...]) + bu_ref[...]
        grad_inner = mm(dy_all[...], wd_ref[...])
        bend = jnp.tanh(GELU_A * (gate + GELU_B * gate * gate * gate))
        gelu = 0.5 * gate * (1.0 + bend)
        slope = 0.5 * (1.0 + bend) + 0.5 * gate * (1.0 - bend * bend) * (
            GELU_A * (1.0 + 3.0 * GELU_B * gate * gate)
        )
        hid_ref[...] = (gelu * up).astype(BF16)
        for row, target, value in (
            (0, dg_ref, grad_inner * up * slope),
            (1, du_ref, grad_inner * gelu),
        ):
            value = value.astype(BF16)
            target[...] = value
            sum_ref[row : row + 1] = jnp.sum(value.astype(F32), axis=0, keepdims=True)
        for step in range(features // block):
            at = pl.ds(step * block, block)
            part = mm_nt(dg_ref[...], wg_ref[at, :]) + mm_nt(du_ref[...], wu_ref[at, :])
            own_back[0, :, at], other_back[0, :, at] = part[:half].astype(BF16), part[half:].astype(BF16)
            part = mm_nt(hid_ref[...], wd_ref[at, :])
            own_back[1, :, at], other_back[1, :, at] = part[:half].astype(BF16), part[half:].astype(BF16)

    weights = [pltpu.with_memory_space_constraint(w, pltpu.VMEM) for w in (wg, wu, wd)]
    return in_vmem(
        body,
        4.0,
        [((2 * half, hidden), BF16)] * 3
        + [((2, half, features), BF16)] * 2
        + [((2, hidden), F32)],
        *(*weights, bg[None], bu[None], own, other, dy_own, dy_other),
        scratch=[pltpu.VMEM((2 * half, features), BF16)] * 2,
    )


def split_columns(grid, shard):
    rows, width = shard.shape
    return shard.reshape(rows, grid.z_count, width // grid.z_count).transpose(1, 0, 2)


def pick(values, index):
    chosen = values[0]
    for number in range(1, len(values)):
        chosen = jnp.where(index == number, values[number], chosen)
    return chosen


def own_rows(ranks, keep, got, parts=1):
    z_count, _, rows, width = keep.shape
    cuts, each = len(got) // z_count, z_count // parts

    def body(ranks_ref, keep_ref, *refs):
        y = ranks_ref[1]
        for z in range(z_count):

            @pl.when(pl.program_id(0) == z)
            def _(got_refs=refs[cuts * z : cuts * z + cuts], away=refs[cuts * z_count + z // each]):
                halves = [got_refs[at % cuts][at // cuts] for at in (0, 1)]
                sums = [keep_ref[0, at].astype(F32) + halves[at].astype(F32) for at in (0, 1)]
                away[0] = jnp.where(y == 0, sums[1], sums[0]).astype(BF16)
                refs[-1][0] = jnp.where(y == 0, sums[0], sums[1]).astype(BF16)

    block = pl.BlockSpec((1, 2, rows, width), lambda i, ranks: (i, 0, 0, 0))
    whole = pl.BlockSpec((2 // cuts, rows, width), lambda i, ranks: (0, 0, 0))
    outs = [((each, rows, width), BF16)] * parts + [((z_count, rows, width), BF16)]
    half = pl.BlockSpec((1, rows, width), lambda i, ranks: (i, 0, 0))
    specs = [block] + [whole] * (cuts * z_count)
    out_specs = [part_spec(rows, width, part, each) for part in range(parts)] + [half]
    out = call(body, 0.5, (z_count,), specs, outs, out_specs, (ranks, keep, *got))
    return (out[0] if parts == 1 else out[:-1]), out[-1]


def part_spec(rows, width, part, each):
    return pl.BlockSpec(
        (1, rows, width), lambda i, ranks: (jnp.clip(i - part * each, 0, each - 1), 0, 0)
    )


def plus(left, *rights):
    z_count, rows, width = left.shape
    each = z_count // len(rights)

    def body(ranks_ref, left_ref, *refs):
        for part, right_ref in enumerate(refs[:-1]):

            @pl.when(pl.program_id(0) // each == part)
            def _(right_ref=right_ref):
                refs[-1][...] = (left_ref[...].astype(F32) + right_ref[...].astype(F32)).astype(BF16)

    block = pl.BlockSpec((1, rows, width), lambda i, ranks: (i, 0, 0))
    specs = [block] + [part_spec(rows, width, part, each) for part in range(len(rights))]
    operands = (jnp.zeros((1,), jnp.int32), left, *rights)
    return call(body, 0.5, (z_count,), specs, [(left.shape, BF16)], [block], operands)[0]


def ring_sum(grid, parts, held, step):
    _, rows, width = parts.shape
    dtype = BF16 if step < grid.z_count else F32
    given = [] if held is None else [held]

    def body(ranks_ref, part_ref, *refs):
        part = part_ref[0].astype(F32)
        refs[-1][...] = (part + refs[0][...].astype(F32) if given else part).astype(dtype)

    full = pl.BlockSpec((rows, width), lambda i, ranks: (0, 0))
    spot = grid.behind(step).astype(jnp.int32)[None]
    return call(
        body,
        1.0,
        (1,),
        [pl.BlockSpec((1, rows, width), lambda i, ranks: (ranks[0], 0, 0))] + [full] * len(given),
        [((rows, width), dtype)],
        [full],
        (spot, parts, *given),
    )[0]


def add(*values):
    def body(*refs):
        total = refs[0][...].astype(F32)
        for ref in refs[1:-1]:
            total += ref[...].astype(F32)
        refs[-1][...] = total.astype(BF16)

    values = [value for value in values if value is not None]
    return in_vmem(body, 1.0, [(values[0].shape, BF16)], *values)[0]


def collect_columns(parts, turn=False):
    count, rows, width = parts.shape

    def body(parts_ref, out_ref):
        if turn:
            for step in range(count):
                out_ref[step * width : (step + 1) * width, :] = parts_ref[step].astype(F32).T
        else:
            pieces = [parts_ref[step].astype(F32) for step in range(count)]
            out_ref[...] = jnp.concatenate(pieces, axis=1)

    shape = (count * width, rows) if turn else (rows, count * width)
    return in_vmem(body, 3.0, [(shape, F32)], parts)[0]


def turned(value, cosine, sine):
    first = value[:, : cosine.shape[1]]
    first = first * cosine + pltpu.roll(first, first.shape[1] // 2, 1) * sine
    return jnp.concatenate([first, value[:, cosine.shape[1] :]], axis=1)


def softmax(query, key, bias):
    scores = mm_nt(query, key) + bias
    expon = jnp.exp(scores - jnp.max(scores, axis=-1, keepdims=True))
    return expon / jnp.sum(expon, axis=-1, keepdims=True)


def attend(scale, q_ref, k_ref, v_ref, cos_ref, sin_ref, bias_ref, rq_ref, o_ref):
    size = k_ref.shape[1]
    for head in range(rq_ref.shape[1] // size):
        at = pl.ds(head * size, size)
        query = (turned(q_ref[:, at], cos_ref[...], sin_ref[...]) * scale).astype(BF16)
        rq_ref[:, at] = query
        probs = softmax(query, k_ref[...], bias_ref[...]).astype(BF16)
        o_ref[:, at] = mm(probs, v_ref[...]).astype(BF16)


def attend_back(
    scale, do_ref, rq_ref, k_ref, v_ref, cos_ref, sin_ref, bias_ref, dq_ref, dk_ref, dv_ref
):
    size = k_ref.shape[1]
    cosine, sine = cos_ref[...], -sin_ref[...]
    grad_key = jnp.zeros(dk_ref.shape, F32)
    grad_value = jnp.zeros(dv_ref.shape, F32)
    for head in range(rq_ref.shape[1] // size):
        at = pl.ds(head * size, size)
        query, grad_out = rq_ref[:, at], do_ref[:, at]
        probs = softmax(query, k_ref[...], bias_ref[...])
        grad_value += mm_tn(probs.astype(BF16), grad_out)
        grad_probs = mm_nt(grad_out, v_ref[...])
        delta = jnp.sum(probs * grad_probs, axis=-1, keepdims=True)
        grad_scores = (probs * (grad_probs - delta)).astype(BF16)
        grad_query = mm(grad_scores, k_ref[...]) * scale
        dq_ref[:, at] = turned(grad_query, cosine, sine).astype(BF16)
        grad_key += mm_tn(grad_scores, query)
    dk_ref[...] = turned(grad_key, cosine, sine)
    dv_ref[...] = grad_value


def in_vmem(body, micros, shapes, *operands, scratch=()):
    spec = pl.BlockSpec(memory_space=pltpu.VMEM)
    return pl.pallas_call(
        body,
        out_shape=[jax.ShapeDtypeStruct(shape, dtype) for shape, dtype in shapes],
        in_specs=[spec] * len(operands),
        out_specs=[spec] * len(shapes),
        scratch_shapes=list(scratch),
        cost_estimate=cost(micros),
        compiler_params=pltpu.CompilerParams(vmem_limit_bytes=VMEM),
    )(*operands)


def shards(
    inputs,
    gain_attn,
    w_query,
    w_keyval,
    w_output,
    gain_mlp,
    w_gate,
    b_gate,
    w_up,
    b_up,
    w_down,
    b_down,
    segment_ids,
    cotangent,
    total,
):
    grid = Grid(total)
    count = grid.z_count
    micro, length, width = inputs.shape
    tokens = micro * length
    head_dim = w_keyval.shape[1] // 2
    query_width = w_query.shape[1]
    scale = head_dim ** (-0.5)

    def halves(value):
        value = value.reshape(micro, 2, length // 2, value.shape[-1])
        return tuple(take(value, i, 1).reshape(tokens // 2, -1) for i in (grid.x, 1 - grid.x))

    def join(mine, other):
        shape = (micro, length // 2, mine.shape[-1])
        return pair(grid.x, mine.reshape(shape), other.reshape(shape), 1).reshape(tokens, -1)

    ranks = jnp.stack([grid.z, grid.y, grid.c, grid.x]).astype(jnp.int32)
    keyval_half = lax.dynamic_slice_in_dim(w_keyval, grid.x * head_dim, head_dim, 1)
    shards_of = [split_columns(grid, shard) for shard in (w_gate, w_up, w_down.T)]
    dy_half = halves(cotangent.reshape(tokens, width))[0]
    segment = segment_ids.reshape(micro, length)
    offsets = jax.vmap(positions)(segment).reshape(tokens)
    quarter = head_dim // 4
    freqs = 10000.0 ** (-jnp.arange(quarter, dtype=F32) / quarter)
    angle = offsets[:, None] * freqs[None, :]
    cosine, sine = jnp.cos(angle), jnp.sin(angle)
    cosine = jnp.concatenate([cosine, cosine], axis=1)
    sine = jnp.concatenate([-sine, sine], axis=1)
    index = jnp.arange(tokens, dtype=jnp.int32)
    seg = segment.reshape(tokens)
    allowed = (
        (seg[:, None] == seg[None, :])
        & (index[:, None] // length == index[None, :] // length)
        & (index[None, :] <= index[:, None])
    )
    bias = jnp.where(allowed, 0.0, -1e30).astype(F32)
    hidden_x = inputs.reshape(tokens, width).astype(F32)
    factor_one = inv_root(hidden_x)
    normed = (hidden_x * factor_one * gain_attn).astype(BF16)
    x_half, factor_half = halves(inputs.reshape(tokens, width))[0], halves(factor_one)[0]
    half_shape = (tokens // 2, width)

    def mlp(step):
        pieces = (b_slots[step], b_others[step], dy_slots[step], dy_others[step])
        results.append(mlp_slot(wg, wu, wd, bg, bu, *grid.gate(pieces)))
        grid.wait(*results[-1])

    slots = [jnp.concatenate([w_query, keyval_half, w_output.T], axis=1)]
    across, beside, both, wholes = [], [], [], []
    dy_slots, dy_others = [dy_half], []

    def place(step):
        pieces = [slots[step], across[step], beside[step], both[step]]
        spot = jnp.stack([grid.behind(step), grid.y, grid.c]).astype(jnp.int32)
        return place_slot(spot, pieces, wholes, count, (0, query_width + head_dim))

    for step in range(count):
        if step + 1 < count:
            slots.append(grid.next_z(slots[step]))
        else:
            gate_mine = grid.along_z(shards_of[0])
        across.append(grid.over_y(slots[step]))
        beside.append(grid.over_c(slots[step]))
        if step == 0:
            dy_others.append(grid.over_x(dy_half))
            grid.wait(shards_of[0])
        else:
            both.append(grid.over_c(across[step - 1]))
            wholes = place(step - 1)
            grid.wait(*wholes, beside[step])
        if step == 1:
            grid.wait(shards_of[1], normed, x_half, dy_others[0])
        if step == 2:
            grid.wait(shards_of[2], cosine, sine, bias)
        if step + 1 < count:
            grid.wait(slots[step + 1], across[step])
    grid.wait(across[-1])
    both.append(grid.over_c(across[-1]))
    grid.wait(gate_mine)

    up_mine = grid.along_z(shards_of[1])
    gate_across, gate_beside = grid.over_y(gate_mine), grid.over_c(gate_mine)
    wholes = place(count - 1)
    w_qkv, w_out = [whole.reshape(width, -1) for whole in wholes]
    queries = product(normed, w_qkv, F32)
    keyval = queries[:, query_width:]
    front, back = keyval[:, :quarter], keyval[:, quarter : 2 * quarter]
    swapped = jnp.concatenate([back, front], axis=1)
    key = jnp.concatenate(
        [keyval[:, : 2 * quarter] * cosine + swapped * sine, keyval[:, 2 * quarter :]], axis=1
    )
    keyval = jnp.where(grid.x == 0, key, keyval).astype(BF16)
    keyval_other = grid.over_x(keyval)
    grid.wait(keyval_other)
    rot_key = jnp.where(grid.x == 0, keyval, keyval_other)
    values_in = jnp.where(grid.x == 0, keyval_other, keyval)
    shape = (tokens, query_width)
    rot_query, mixed_b = in_vmem(
        partial(attend, scale),
        1.2,
        [(shape, BF16), (shape, BF16)],
        *(queries, rot_key, values_in, cosine, sine, bias),
    )
    mine, other = product_nt(ranks, mixed_b, w_out, micro)
    grid.wait(mine)
    attended = grid.over_x(other)
    grid.wait(up_mine)
    down_mine = grid.along_z(shards_of[2])
    grid.wait(gate_across)
    up_across, up_beside = grid.over_y(up_mine), grid.over_c(up_mine)
    gate_both = grid.over_c(gate_across)
    grid.wait(attended)
    residual, factor_two, normed_two = in_vmem(
        second_norm,
        0.5,
        [(half_shape, F32), ((tokens // 2, 1), F32), (half_shape, BF16)],
        *(x_half, mine, attended, gain_mlp[None]),
    )
    grid.wait(normed_two)
    b_slots, b_others = [normed_two], [grid.over_x(normed_two)]
    b_slots.append(grid.next_z(normed_two))
    dy_slots.append(grid.next_z(dy_half))
    wg = place_all(ranks, [gate_mine, gate_across, gate_beside, gate_both])
    grid.wait(wg, b_others[0])
    grid.wait(down_mine)

    grid.wait(up_across)
    down_across, down_beside = grid.over_y(down_mine), grid.over_c(down_mine)
    grid.wait(b_slots[1], dy_slots[1])
    for step in range(1, count - 1):
        b_slots.append(grid.next_z(b_slots[step]))
        dy_slots.append(grid.next_z(dy_slots[step]))
        b_others.append(grid.over_x(b_slots[step]))
        dy_others.append(grid.over_x(dy_slots[step]))
        if step == 1:
            up_both = grid.over_c(up_across)
            wu = place_all(ranks, [up_mine, up_across, up_beside, up_both])
            grid.wait(wu)
        if step == 2:
            grid.wait(down_across)
            down_both = grid.over_c(down_across)
            wd = place_all(ranks, [down_mine, down_across, down_beside, down_both])
            hidden = wg.shape[1]
            spot = grid.z * hidden
            bg = lax.dynamic_slice_in_dim(b_gate, spot, hidden, 0)
            bu = lax.dynamic_slice_in_dim(b_up, spot, hidden, 0)
            grid.wait(wd, bg, bu)
            results = []
            mlp(0)
        grid.wait(b_slots[step + 1], dy_slots[step + 1])
        grid.wait(b_others[step], dy_others[step])
    b_others.append(grid.over_x(b_slots[-1]))
    dy_others.append(grid.over_x(dy_slots[-1]))
    mlp(1)

    for step in range(2, count - 1):
        mlp(step)
    grid.wait(b_others[-1], dy_others[-1])
    back_got = [None, grid.over_x(results[1][4])]
    mlp(count - 1)
    inner_slots, gate_slots, up_slots, back_own, back_other, sums = zip(*results)
    dy_all = [piece for two in zip(dy_slots, dy_others) for piece in two]
    b_all = [piece for two in zip(b_slots, b_others) for piece in two]
    down_keep, down_send = product_rows(ranks, grid.gate(dy_all), [inner_slots], count, 2)[0]
    grid.wait(down_keep, back_got[1])
    held = add(back_own[1], back_got[1])
    grid.wait(held)
    back_next = grid.next_z(held)
    back_got.append(grid.over_x(back_other[2]))
    down_got = [grid.over_c(send) for send in down_send]
    grid.wait(*down_got)
    down_away, down_stay = own_rows(ranks, grid.gate(down_keep), down_got)
    grid.wait(down_away)
    down_back = grid.over_y(down_away)
    (gate_keep, gate_send), (up_keep, up_send) = product_rows(
        ranks, grid.gate(b_all), [gate_slots, up_slots], count
    )
    grid.wait(gate_keep, back_got[2], back_next)
    held = add(back_own[2], back_got[2], back_next)
    grid.wait(held)
    back_next = grid.next_z(held)
    back_got.append(grid.over_x(back_other[3]))
    gate_got = [grid.over_c(send) for send in gate_send]
    grid.wait(*gate_got)
    gate_away, gate_stay = own_rows(ranks, grid.gate(gate_keep), gate_got)
    grid.wait(gate_away)
    for step in range(3, count):
        grid.wait(back_got[step], back_next)
        held = add(back_own[step], back_got[step], back_next)
        grid.wait(held)
        back_next = grid.next_z(held)
        back_got.append(grid.over_x(back_other[(step + 1) % count]))
    up_got = [grid.over_c(send) for send in up_send]
    grid.wait(down_back)
    gate_back = grid.over_y(gate_away)
    down_rows = plus(grid.gate(down_stay), down_back)
    grid.wait(down_rows)
    down_parts = grid.along_z(down_rows)
    grid.wait(*up_got)
    up_away, up_stay = own_rows(ranks, grid.gate(up_keep), up_got, 2)
    grid.wait(*up_away)
    grid.wait(back_got[-1], back_next)
    grad_resid, grad_resid_b, gain_mlp_term, outputs = in_vmem(
        second_norm_back,
        0.5,
        [(half_shape, F32), (half_shape, BF16), ((1, width), F32), (half_shape, BF16)],
        *(back_own[0], back_got[-1], back_next, residual, factor_two),
        *(gain_mlp[None], b_down[None], dy_half),
    )
    grid.wait(grad_resid_b)
    grad_resid_other = grid.over_x(grad_resid_b)
    grid.wait(gate_back)
    up_back = [grid.over_y(up_away[0])]
    gate_rows = plus(grid.gate(gate_stay), gate_back)
    grid.wait(gate_rows, grad_resid_other)

    grad_resid_b = join(grad_resid_b, grad_resid_other)
    grad_mixed = product(grid.gate(grad_resid_b), w_out, BF16)
    shape_kv = (tokens, head_dim)
    grad_query, grad_key, grad_values = in_vmem(
        partial(attend_back, scale),
        0.5,
        [(shape, BF16), (shape_kv, F32), (shape_kv, F32)],
        *(grad_mixed, rot_query, rot_key, values_in, cosine, sine, bias),
    )
    grid.wait(grad_query)
    grad_own = jnp.where(grid.x == 0, grad_key, grad_values)
    grad_other = grid.over_x(jnp.where(grid.x == 0, grad_values, grad_key))
    grid.wait(up_back[0])
    up_back.append(grid.over_y(up_away[1]))
    query_keep, query_send = product_rows(ranks, [grid.gate(normed)], [[grad_query]], count)[0]
    grid.wait(grad_other, query_keep, up_back[1])
    grid.wait(down_parts)
    gate_parts = grid.along_z(gate_rows)
    up_rows = plus(grid.gate(up_stay), *up_back)
    grid.wait(up_rows)
    grad_keyval = (grad_own + grad_other).astype(BF16)
    out_keep, out_send = product_rows(
        ranks, [grid.gate(grad_resid_b), normed], [[mixed_b, grad_keyval]], count, beside=True
    )[0]
    grid.wait(out_keep)
    out_got = [grid.over_c(send) for send in out_send]
    grid.wait(*out_got)
    out_away, out_stay = own_rows(ranks, grid.gate(out_keep), out_got, 2)
    grid.wait(*out_away)
    out_back = [grid.over_y(out_away[0])]
    grid.wait(gate_parts)
    up_parts = grid.along_z(up_rows)
    mine, other = product_nt(
        ranks, jnp.concatenate([grad_query, grid.gate(grad_keyval)], axis=1), w_qkv, micro
    )
    grid.wait(mine)
    grad_normed = grid.over_x(other)
    query_got = [grid.over_c(send) for send in query_send]
    grid.wait(out_back[0])
    out_back.append(grid.over_y(out_away[1]))
    grid.wait(*query_got)
    query_away, query_stay = own_rows(ranks, grid.gate(query_keep), query_got)
    grid.wait(query_away)
    grid.wait(grad_normed)
    grad_input, gain_attn_term = in_vmem(
        first_norm_back,
        0.5,
        [(half_shape, BF16), ((1, width), F32)],
        *(mine, grad_normed, x_half, factor_half, gain_attn[None], grid.gate(grad_resid)),
    )
    grid.wait(grad_input)
    narrow = jnp.concatenate(
        [gain_attn_term, gain_mlp_term, jnp.sum(dy_half.astype(F32), axis=0)[None]]
    )
    grid.wait(narrow)
    narrow_other = grid.over_x(narrow)
    outputs_other = grid.over_x(outputs)
    down_grad = collect_columns(grid.gate(down_parts), True)
    grid.wait(down_grad)
    grid.wait(out_back[1])
    query_back = grid.over_y(query_away)
    out_rows = plus(grid.gate(out_stay), *out_back)
    out_held = ring_sum(grid, out_rows, None, 1)
    grid.wait(out_held)
    out_held = grid.next_z(out_held)

    ffn = b_gate.shape[0]
    wide = jnp.zeros((2, ffn), F32)
    wide = lax.dynamic_update_slice(wide, sum(sums), (0, spot)).reshape(-1)
    grid.wait(narrow_other)
    small = jnp.concatenate([(narrow + narrow_other).reshape(-1), wide])
    small_other = grid.over_c(small)
    grid.wait(small_other)
    small = small + small_other
    grid.wait(small)
    small_all = [small] + [grid.next_z(small, step) for step in range(1, count)]
    grid.wait(out_held)
    out_held = ring_sum(grid, out_rows, out_held, 2)
    grid.wait(out_held)
    out_held = grid.next_z(out_held)
    grid.wait(up_parts)
    gate_grad = collect_columns(grid.gate(gate_parts))
    grid.wait(gate_grad)
    grid.wait(query_back)
    query_rows = plus(grid.gate(query_stay), query_back)
    query_held = ring_sum(grid, query_rows, None, 1)
    grid.wait(query_held)
    query_held = grid.next_z(query_held)
    grid.wait(outputs_other, *small_all)
    places = [lax.rem(grid.z - z + count, count) for z in range(count)]
    small = sum(pick(small_all, place) for place in places)
    grid.wait(small)
    small_other = grid.over_y(small)
    grad_input_other = grid.over_x(grad_input)
    for step in range(3, count):
        grid.wait(out_held)
        out_held = ring_sum(grid, out_rows, out_held, step)
        grid.wait(out_held)
        out_held = grid.next_z(out_held)
    grid.wait(query_held)
    query_held = ring_sum(grid, query_rows, query_held, 2)
    grid.wait(query_held)
    query_held = grid.next_z(query_held)
    up_grad = collect_columns(grid.gate(up_parts))
    grid.wait(up_grad)
    grid.wait(out_held)
    out_held = ring_sum(grid, out_rows, out_held, count)
    grid.wait(out_held)
    keyval_grad = out_held[:, query_width:]
    keyval_other = grid.over_x(keyval_grad)
    out_grad = out_held[:, :query_width].T
    for step in range(3, count):
        grid.wait(query_held)
        query_held = ring_sum(grid, query_rows, query_held, step)
        grid.wait(query_held)
        query_held = grid.next_z(query_held)
    grid.wait(out_grad, keyval_other, grad_input_other)
    small = small + small_other
    query_grad = ring_sum(grid, query_rows, grid.gate(query_held), count)
    keyval_grad = pair(grid.x, keyval_grad, keyval_other, 1)
    keyval_grad = keyval_grad.reshape(keyval_grad.shape[0], 2 * head_dim)
    return (
        join(outputs, outputs_other).reshape(inputs.shape),
        join(grad_input, grad_input_other).reshape(inputs.shape),
        small[:width],
        query_grad,
        keyval_grad,
        out_grad,
        small[width : 2 * width],
        gate_grad,
        small[3 * width : 3 * width + ffn],
        up_grad,
        small[3 * width + ffn :],
        down_grad,
        small[2 * width : 3 * width],
    )


def solution(mesh):
    in_specs = (
        P(None, "dp", None),
        P(),
        P("dp", "mp"),
        P("dp", None),
        P("mp", "dp"),
        P(),
        P("dp", "mp"),
        P("mp"),
        P("dp", "mp"),
        P("mp"),
        P("mp", "dp"),
        P(),
        P(None, "dp", None),
        P(None, "dp", None),
    )
    out_specs = (
        P(None, "dp", None),
        P(None, "dp", None),
        P(),
        P("dp", "mp"),
        P("dp", None),
        P("mp", "dp"),
        P(),
        P("dp", "mp"),
        P("mp"),
        P("dp", "mp"),
        P("mp"),
        P("mp", "dp"),
        P(),
    )
    body = partial(shards, total=mesh.shape["dp"])
    return jax.shard_map(body, mesh=mesh, in_specs=in_specs, out_specs=out_specs, check_vma=False)
```

```python
import math
from functools import partial

import jax
import jax.numpy as jnp
from jax import lax
from jax.experimental import pallas as pl
from jax.experimental.pallas import tpu as pltpu
from jax.sharding import PartitionSpec as P

EPS = 1e-06
F32 = jnp.float32
BF16 = jnp.bfloat16
VMEM = 24 * 2**20
SCALE = 12.0
GELU_A, GELU_B = math.sqrt(2.0 / math.pi), 0.044715


def positions(segment):
    count = segment.shape[0]
    index = jnp.arange(count, dtype=jnp.int32)
    fresh = jnp.concatenate([jnp.ones((1,), jnp.bool_), segment[1:] != segment[:-1]])
    starts = lax.cummax(jnp.where(fresh, index, 0), axis=0)
    return (index - starts).astype(F32)


def inv_root(values):
    return lax.rsqrt(jnp.mean(values * values, axis=-1, keepdims=True) + EPS)


def norm_back(values, factor, gain, grad_norm):
    scaled = gain * grad_norm
    return factor * scaled - values * factor**3 * jnp.mean(scaled * values, axis=-1, keepdims=True)


def mm(left, right):
    return jnp.dot(left, right, preferred_element_type=F32)


def mm_nt(left, right):
    return lax.dot_general(left, right, (((1,), (1,)), ((), ())), preferred_element_type=F32)


def mm_tn(left, right):
    return lax.dot_general(left, right, (((0,), (0,)), ((), ())), preferred_element_type=F32)


class Grid:
    def __init__(self, total):
        self.z_count = total // 4
        spots = [(z, y, c) for z in range(self.z_count) for y in range(2) for c in range(2)]
        at = lambda z, y, c: (z * 2 + y) * 2 + c
        self.swap_y = [(at(z, y, c), at(z, 1 - y, c)) for z, y, c in spots]
        self.swap_c = [(at(z, y, c), at(z, y, 1 - c)) for z, y, c in spots]
        self.ring = lambda step: [
            (at(z, y, c), at((z + step) % self.z_count, y, c)) for z, y, c in spots
        ]
        self.flips = []
        step = 1
        while step < self.z_count:
            self.flips.append([(at(z, y, c), at(z ^ step, y, c)) for z, y, c in spots])
            step *= 2
        self.lines = [
            [at(z, y, c) for z in range(self.z_count)] for y in range(2) for c in range(2)
        ]
        index = lax.axis_index("dp")
        self.c = index % 2
        self.y = (index // 2) % 2
        self.z = index // 4
        self.x = lax.axis_index("mp")
        self.token = jnp.zeros((), F32)

    def wait(self, *values):
        self.token = lax.optimization_barrier((self.token, values))[0]

    def gate(self, value):
        return lax.optimization_barrier((value, self.token))[0]

    def over_y(self, value):
        return lax.ppermute(self.gate(value), "dp", self.swap_y)

    def over_c(self, value):
        return lax.ppermute(self.gate(value), "dp", self.swap_c)

    def over_x(self, value):
        return lax.ppermute(self.gate(value), "mp", [(0, 1), (1, 0)])

    def next_z(self, value, step=1):
        return lax.ppermute(self.gate(value), "dp", self.ring(step))

    def along_z(self, value):
        value = self.gate(value)
        return lax.all_to_all(value, "dp", 0, 0, axis_index_groups=self.lines, tiled=True)

    def behind(self, step):
        return lax.rem(self.z - step + 2 * self.z_count, self.z_count)


def pair(index, mine, other, axis):
    return jnp.where(
        index == 0, jnp.stack([mine, other], axis=axis), jnp.stack([other, mine], axis=axis)
    )


def take(value, index, axis):
    return lax.dynamic_index_in_dim(value, index, axis, keepdims=False)


def cost(micros):
    micros = micros / SCALE
    flops, moved = int(micros * 1.15e9), int(micros * 3.69e6)
    return pl.CostEstimate(flops=flops, bytes_accessed=moved, transcendentals=0)


def call(body, micros, grid, in_specs, outs, out_specs, operands, aliases=None, limit=VMEM):
    return pl.pallas_call(
        body,
        out_shape=[jax.ShapeDtypeStruct(shape, dtype) for shape, dtype in outs],
        grid_spec=pltpu.PrefetchScalarGridSpec(
            num_scalar_prefetch=1,
            grid=grid,
            in_specs=in_specs,
            out_specs=out_specs,
        ),
        input_output_aliases=aliases or {},
        cost_estimate=cost(micros),
        compiler_params=pltpu.CompilerParams(vmem_limit_bytes=limit),
    )(*operands)


def place_slot(ranks, pieces, wholes, z_count, cuts):
    rows, width = pieces[0].shape
    ends = list(cuts[1:]) + [width]
    given = len(wholes)

    def body(ranks_ref, *refs):
        sources, targets = refs[:4], refs[4 + given :]
        y, c = ranks_ref[1], ranks_ref[2]
        spots = [(y, c), (1 - y, c), (y, 1 - c), (1 - y, 1 - c)]
        for source, (at_y, at_c) in zip(sources, spots):
            for target, begin, end in zip(targets, cuts, ends):
                target[0, at_y, at_c] = source[:, begin:end]

    whole_spec = pl.BlockSpec(memory_space=pl.ANY)
    return call(
        body,
        1.0,
        (1,),
        [pl.BlockSpec((rows, width), lambda i, ranks: (0, 0))] * 4 + [whole_spec] * given,
        [((z_count, 2, 2, rows, end - begin), BF16) for begin, end in zip(cuts, ends)],
        [
            pl.BlockSpec((1, 2, 2, rows, end - begin), lambda i, ranks: (ranks[0], 0, 0, 0, 0))
            for begin, end in zip(cuts, ends)
        ],
        (ranks, *pieces, *wholes),
        aliases={5 + number: number for number in range(given)},
        limit=2 * VMEM,
    )


def place_all(ranks, pieces):
    z_count, rows, width = pieces[0].shape

    def body(ranks_ref, own, side, core, both, target):
        y, c = ranks_ref[1], ranks_ref[2]
        target[0, y, c] = own[0]
        target[0, 1 - y, c] = side[0]
        target[0, y, 1 - c] = core[0]
        target[0, 1 - y, 1 - c] = both[0]

    whole = call(
        body,
        1.0,
        (z_count,),
        [pl.BlockSpec((1, rows, width), lambda i, ranks: (i, 0, 0))] * 4,
        [((z_count, 2, 2, rows, width), BF16)],
        [pl.BlockSpec((1, 2, 2, rows, width), lambda i, ranks: (i, 0, 0, 0, 0))],
        (ranks, *pieces),
    )[0]
    return whole.reshape(z_count * 4 * rows, width)


def product(left, right, dtype):
    rows, depth = left.shape
    width = right.shape[1]
    block = 256 if width % 256 == 0 else width

    def body(ranks_ref, left_ref, right_ref, out_ref):
        out_ref[...] = mm(left_ref[...], right_ref[...]).astype(dtype)

    return call(
        body,
        1.0,
        (width // block,),
        [
            pl.BlockSpec((rows, depth), lambda i, ranks: (0, 0)),
            pl.BlockSpec((depth, block), lambda i, ranks: (0, i)),
        ],
        [((rows, width), dtype)],
        [pl.BlockSpec((rows, block), lambda i, ranks: (0, i))],
        (jnp.zeros((1,), jnp.int32), left, right),
    )[0]


def product_nt(ranks, left, right, groups):
    rows, depth = left.shape
    width = right.shape[0]
    block = 512 if width % 512 == 0 else width
    half = rows // groups // 2

    def body(ranks_ref, left_ref, right_ref, own_ref, other_ref):
        whole = mm_nt(left_ref[...], right_ref[...])
        low = ranks_ref[3] == 0
        for group in range(groups):
            at = group * 2 * half
            first, second = whole[at : at + half], whole[at + half : at + 2 * half]
            to = pl.ds(group * half, half)
            own_ref[to, :] = jnp.where(low, first, second)
            other_ref[to, :] = jnp.where(low, second, first).astype(BF16)

    out_spec = pl.BlockSpec((rows // 2, block), lambda i, ranks: (0, i))
    return call(
        body,
        1.0,
        (width // block,),
        [
            pl.BlockSpec((rows, depth), lambda i, ranks: (0, 0)),
            pl.BlockSpec((block, depth), lambda i, ranks: (i, 0)),
        ],
        [((rows // 2, width), F32), ((rows // 2, width), BF16)],
        [out_spec] * 2,
        (ranks, left, right),
    )


def second_norm(x_ref, mine_ref, got_ref, gain_ref, residual_ref, factor_ref, normed_ref):
    residual = x_ref[...].astype(F32) + mine_ref[...] + got_ref[...].astype(F32)
    factor = inv_root(residual)
    residual_ref[...], factor_ref[...] = residual, factor
    normed_ref[...] = (residual * factor * gain_ref[...]).astype(BF16)


def second_norm_back(
    own_ref, got_ref, held_ref, residual_ref, factor_ref, gain_ref, bias_ref, dy_ref,
    grad_ref, grad_b_ref, term_ref, out_ref,
):
    both = [
        own_ref[at].astype(F32) + got_ref[at].astype(F32) + held_ref[at].astype(F32) for at in (0, 1)
    ]
    residual, factor = residual_ref[...], factor_ref[...]
    out_ref[...] = (residual + both[1] + bias_ref[...]).astype(BF16)
    term_ref[...] = jnp.sum(both[0] * residual * factor, axis=0, keepdims=True)
    grad = dy_ref[...].astype(F32) + norm_back(residual, factor, gain_ref[...], both[0])
    grad_ref[...], grad_b_ref[...] = grad, grad.astype(BF16)


def first_norm_back(mine_ref, got_ref, x_ref, factor_ref, gain_ref, grad_ref, out_ref, term_ref):
    grad = mine_ref[...] + got_ref[...].astype(F32)
    values, factor = x_ref[...].astype(F32), factor_ref[...]
    term_ref[...] = jnp.sum(grad * values * factor, axis=0, keepdims=True)
    out_ref[...] = (grad_ref[...] + norm_back(values, factor, gain_ref[...], grad)).astype(BF16)


def product_rows(ranks, lefts, groups, z_count, cuts=1, beside=False):
    features = lefts[0].shape[1]
    width = sum(right.shape[1] for right in groups[0]) if beside else groups[0][0].shape[1]
    rows = features // (4 * z_count)
    block = math.lcm(4 * rows, 128)
    span = block // (4 * rows)
    rights = [right for group in groups for right in group]
    each = len(groups[0])
    join = lambda parts: parts[0] if len(parts) == 1 else jnp.concatenate(parts, axis=0)

    def body(ranks_ref, *refs):
        left = [ref[...] for ref in refs[: len(lefts)]]
        left = left if beside else join(left)
        right_refs, out_refs = refs[len(lefts) : -outs], refs[-outs:]
        low = ranks_ref[2] == 0
        here = pl.program_id(0)
        for number in range(len(groups)):
            right = [ref[...] for ref in right_refs[number * each : (number + 1) * each]]
            keep, sends = out_refs[number], out_refs[len(groups) + number * cuts * z_count :]
            if beside:
                whole = jnp.concatenate([mm_tn(a, b) for a, b in zip(left, right)], axis=1)
            else:
                whole = mm_tn(left, join(right))
            for place in range(span):
                for y in range(2):
                    at = (place * 4 + y * 2) * rows
                    first, second = whole[at : at + rows], whole[at + rows : at + 2 * rows]
                    keep[place, y] = jnp.where(low, first, second).astype(BF16)
                    other = jnp.where(low, second, first).astype(BF16)
                    for z in range(place, z_count, span):

                        @pl.when(here == z // span)
                        def _(target=sends[cuts * z + (y if cuts == 2 else 0)], y=y, other=other):
                            target[y % (2 // cuts)] = other

    parts = cuts * z_count
    outs = len(groups) * (1 + parts)
    keep_spec = pl.BlockSpec((span, 2, rows, width), lambda i, ranks: (i, 0, 0, 0))
    send_spec = pl.BlockSpec((2 // cuts, rows, width), lambda i, ranks: (0, 0, 0))
    out = call(
        body,
        2.0 * len(groups),
        (features // block,),
        [pl.BlockSpec((left.shape[0], block), lambda i, ranks: (0, i)) for left in lefts]
        + [pl.BlockSpec(right.shape, lambda i, ranks: (0, 0)) for right in rights],
        [((z_count, 2, rows, width), BF16)] * len(groups)
        + [((2 // cuts, rows, width), BF16)] * (len(groups) * parts),
        [keep_spec] * len(groups) + [send_spec] * (len(groups) * parts),
        (ranks, *lefts, *rights),
    )
    sends = out[len(groups) :]
    return [
        (out[number], sends[number * parts : (number + 1) * parts])
        for number in range(len(groups))
    ]


def mlp_slot(wg, wu, wd, bg, bu, own, other, dy_own, dy_other):
    features, hidden = wg.shape
    half = own.shape[0]
    block = features // 4 if (features // 4) % 128 == 0 else features

    def body(
        wg_ref, wu_ref, wd_ref, bg_ref, bu_ref, own_ref, other_ref, dyo_ref, dyr_ref,
        hid_ref, dg_ref, du_ref, own_back, other_back, sum_ref, b_all, dy_all,
    ):
        b_all[:half], b_all[half:] = own_ref[...], other_ref[...]
        dy_all[:half], dy_all[half:] = dyo_ref[...], dyr_ref[...]
        gate = mm(b_all[...], wg_ref[...]) + bg_ref[...]
        up = mm(b_all[...], wu_ref[...]) + bu_ref[...]
        grad_inner = mm(dy_all[...], wd_ref[...])
        bend = jnp.tanh(GELU_A * (gate + GELU_B * gate * gate * gate))
        gelu = 0.5 * gate * (1.0 + bend)
        slope = 0.5 * (1.0 + bend) + 0.5 * gate * (1.0 - bend * bend) * (
            GELU_A * (1.0 + 3.0 * GELU_B * gate * gate)
        )
        hid_ref[...] = (gelu * up).astype(BF16)
        for row, target, value in (
            (0, dg_ref, grad_inner * up * slope),
            (1, du_ref, grad_inner * gelu),
        ):
            value = value.astype(BF16)
            target[...] = value
            sum_ref[row : row + 1] = jnp.sum(value.astype(F32), axis=0, keepdims=True)
        for step in range(features // block):
            at = pl.ds(step * block, block)
            part = mm_nt(dg_ref[...], wg_ref[at, :]) + mm_nt(du_ref[...], wu_ref[at, :])
            own_back[0, :, at], other_back[0, :, at] = part[:half].astype(BF16), part[half:].astype(BF16)
            part = mm_nt(hid_ref[...], wd_ref[at, :])
            own_back[1, :, at], other_back[1, :, at] = part[:half].astype(BF16), part[half:].astype(BF16)

    weights = [pltpu.with_memory_space_constraint(w, pltpu.VMEM) for w in (wg, wu, wd)]
    return in_vmem(
        body,
        4.0,
        [((2 * half, hidden), BF16)] * 3
        + [((2, half, features), BF16)] * 2
        + [((2, hidden), F32)],
        *(*weights, bg[None], bu[None], own, other, dy_own, dy_other),
        scratch=[pltpu.VMEM((2 * half, features), BF16)] * 2,
    )


def split_columns(grid, shard):
    rows, width = shard.shape
    return shard.reshape(rows, grid.z_count, width // grid.z_count).transpose(1, 0, 2)


def pick(values, index):
    chosen = values[0]
    for number in range(1, len(values)):
        chosen = jnp.where(index == number, values[number], chosen)
    return chosen


def own_rows(ranks, keep, got, parts=1):
    z_count, _, rows, width = keep.shape
    cuts, each = len(got) // z_count, z_count // parts

    def body(ranks_ref, keep_ref, *refs):
        y = ranks_ref[1]
        for z in range(z_count):

            @pl.when(pl.program_id(0) == z)
            def _(got_refs=refs[cuts * z : cuts * z + cuts], away=refs[cuts * z_count + z // each]):
                halves = [got_refs[at % cuts][at // cuts] for at in (0, 1)]
                sums = [keep_ref[0, at].astype(F32) + halves[at].astype(F32) for at in (0, 1)]
                away[0] = jnp.where(y == 0, sums[1], sums[0]).astype(BF16)
                refs[-1][0] = jnp.where(y == 0, sums[0], sums[1]).astype(BF16)

    block = pl.BlockSpec((1, 2, rows, width), lambda i, ranks: (i, 0, 0, 0))
    whole = pl.BlockSpec((2 // cuts, rows, width), lambda i, ranks: (0, 0, 0))
    outs = [((each, rows, width), BF16)] * parts + [((z_count, rows, width), BF16)]
    half = pl.BlockSpec((1, rows, width), lambda i, ranks: (i, 0, 0))
    specs = [block] + [whole] * (cuts * z_count)
    out_specs = [part_spec(rows, width, part, each) for part in range(parts)] + [half]
    out = call(body, 0.5, (z_count,), specs, outs, out_specs, (ranks, keep, *got))
    return (out[0] if parts == 1 else out[:-1]), out[-1]


def part_spec(rows, width, part, each):
    return pl.BlockSpec(
        (1, rows, width), lambda i, ranks: (jnp.clip(i - part * each, 0, each - 1), 0, 0)
    )


def plus(left, *rights):
    z_count, rows, width = left.shape
    each = z_count // len(rights)

    def body(ranks_ref, left_ref, *refs):
        for part, right_ref in enumerate(refs[:-1]):

            @pl.when(pl.program_id(0) // each == part)
            def _(right_ref=right_ref):
                refs[-1][...] = (left_ref[...].astype(F32) + right_ref[...].astype(F32)).astype(BF16)

    block = pl.BlockSpec((1, rows, width), lambda i, ranks: (i, 0, 0))
    specs = [block] + [part_spec(rows, width, part, each) for part in range(len(rights))]
    operands = (jnp.zeros((1,), jnp.int32), left, *rights)
    return call(body, 0.5, (z_count,), specs, [(left.shape, BF16)], [block], operands)[0]


def ring_sum(grid, parts, held, step):
    _, rows, width = parts.shape
    dtype = BF16 if step < grid.z_count else F32
    given = [] if held is None else [held]

    def body(ranks_ref, part_ref, *refs):
        part = part_ref[0].astype(F32)
        refs[-1][...] = (part + refs[0][...].astype(F32) if given else part).astype(dtype)

    full = pl.BlockSpec((rows, width), lambda i, ranks: (0, 0))
    spot = grid.behind(step).astype(jnp.int32)[None]
    return call(
        body,
        1.0,
        (1,),
        [pl.BlockSpec((1, rows, width), lambda i, ranks: (ranks[0], 0, 0))] + [full] * len(given),
        [((rows, width), dtype)],
        [full],
        (spot, parts, *given),
    )[0]


def add(*values):
    def body(*refs):
        total = refs[0][...].astype(F32)
        for ref in refs[1:-1]:
            total += ref[...].astype(F32)
        refs[-1][...] = total.astype(BF16)

    values = [value for value in values if value is not None]
    return in_vmem(body, 1.0, [(values[0].shape, BF16)], *values)[0]


def collect_columns(parts, turn=False):
    count, rows, width = parts.shape

    def body(parts_ref, out_ref):
        if turn:
            for step in range(count):
                out_ref[step * width : (step + 1) * width, :] = parts_ref[step].astype(F32).T
        else:
            pieces = [parts_ref[step].astype(F32) for step in range(count)]
            out_ref[...] = jnp.concatenate(pieces, axis=1)

    shape = (count * width, rows) if turn else (rows, count * width)
    return in_vmem(body, 3.0, [(shape, F32)], parts)[0]


def turned(value, cosine, sine):
    first = value[:, : cosine.shape[1]]
    first = first * cosine + pltpu.roll(first, first.shape[1] // 2, 1) * sine
    return jnp.concatenate([first, value[:, cosine.shape[1] :]], axis=1)


def softmax(query, key, bias):
    scores = mm_nt(query, key) + bias
    expon = jnp.exp(scores - jnp.max(scores, axis=-1, keepdims=True))
    return expon / jnp.sum(expon, axis=-1, keepdims=True)


def attend(scale, q_ref, k_ref, v_ref, cos_ref, sin_ref, bias_ref, rq_ref, o_ref):
    size = k_ref.shape[1]
    for head in range(rq_ref.shape[1] // size):
        at = pl.ds(head * size, size)
        query = (turned(q_ref[:, at], cos_ref[...], sin_ref[...]) * scale).astype(BF16)
        rq_ref[:, at] = query
        probs = softmax(query, k_ref[...], bias_ref[...]).astype(BF16)
        o_ref[:, at] = mm(probs, v_ref[...]).astype(BF16)


def attend_back(
    scale, do_ref, rq_ref, k_ref, v_ref, cos_ref, sin_ref, bias_ref, dq_ref, dk_ref, dv_ref
):
    size = k_ref.shape[1]
    cosine, sine = cos_ref[...], -sin_ref[...]
    grad_key = jnp.zeros(dk_ref.shape, F32)
    grad_value = jnp.zeros(dv_ref.shape, F32)
    for head in range(rq_ref.shape[1] // size):
        at = pl.ds(head * size, size)
        query, grad_out = rq_ref[:, at], do_ref[:, at]
        probs = softmax(query, k_ref[...], bias_ref[...])
        grad_value += mm_tn(probs.astype(BF16), grad_out)
        grad_probs = mm_nt(grad_out, v_ref[...])
        delta = jnp.sum(probs * grad_probs, axis=-1, keepdims=True)
        grad_scores = (probs * (grad_probs - delta)).astype(BF16)
        grad_query = mm(grad_scores, k_ref[...]) * scale
        dq_ref[:, at] = turned(grad_query, cosine, sine).astype(BF16)
        grad_key += mm_tn(grad_scores, query)
    dk_ref[...] = turned(grad_key, cosine, sine)
    dv_ref[...] = grad_value


def in_vmem(body, micros, shapes, *operands, scratch=()):
    spec = pl.BlockSpec(memory_space=pltpu.VMEM)
    return pl.pallas_call(
        body,
        out_shape=[jax.ShapeDtypeStruct(shape, dtype) for shape, dtype in shapes],
        in_specs=[spec] * len(operands),
        out_specs=[spec] * len(shapes),
        scratch_shapes=list(scratch),
        cost_estimate=cost(micros),
        compiler_params=pltpu.CompilerParams(vmem_limit_bytes=VMEM),
    )(*operands)


def shards(
    inputs,
    gain_attn,
    w_query,
    w_keyval,
    w_output,
    gain_mlp,
    w_gate,
    b_gate,
    w_up,
    b_up,
    w_down,
    b_down,
    segment_ids,
    cotangent,
    total,
):
    grid = Grid(total)
    count = grid.z_count
    micro, length, width = inputs.shape
    tokens = micro * length
    head_dim = w_keyval.shape[1] // 2
    query_width = w_query.shape[1]
    scale = head_dim ** (-0.5)

    def halves(value):
        value = value.reshape(micro, 2, length // 2, value.shape[-1])
        return tuple(take(value, i, 1).reshape(tokens // 2, -1) for i in (grid.x, 1 - grid.x))

    def join(mine, other):
        shape = (micro, length // 2, mine.shape[-1])
        return pair(grid.x, mine.reshape(shape), other.reshape(shape), 1).reshape(tokens, -1)

    ranks = jnp.stack([grid.z, grid.y, grid.c, grid.x]).astype(jnp.int32)
    keyval_half = lax.dynamic_slice_in_dim(w_keyval, grid.x * head_dim, head_dim, 1)
    shards_of = [split_columns(grid, shard) for shard in (w_gate, w_up, w_down.T)]
    dy_half = halves(cotangent.reshape(tokens, width))[0]
    segment = segment_ids.reshape(micro, length)
    offsets = jax.vmap(positions)(segment).reshape(tokens)
    quarter = head_dim // 4
    freqs = 10000.0 ** (-jnp.arange(quarter, dtype=F32) / quarter)
    angle = offsets[:, None] * freqs[None, :]
    cosine, sine = jnp.cos(angle), jnp.sin(angle)
    cosine = jnp.concatenate([cosine, cosine], axis=1)
    sine = jnp.concatenate([-sine, sine], axis=1)
    index = jnp.arange(tokens, dtype=jnp.int32)
    seg = segment.reshape(tokens)
    allowed = (
        (seg[:, None] == seg[None, :])
        & (index[:, None] // length == index[None, :] // length)
        & (index[None, :] <= index[:, None])
    )
    bias = jnp.where(allowed, 0.0, -1e30).astype(F32)
    hidden_x = inputs.reshape(tokens, width).astype(F32)
    factor_one = inv_root(hidden_x)
    normed = (hidden_x * factor_one * gain_attn).astype(BF16)
    x_half, factor_half = halves(inputs.reshape(tokens, width))[0], halves(factor_one)[0]
    half_shape = (tokens // 2, width)

    def mlp(step):
        pieces = (b_slots[step], b_others[step], dy_slots[step], dy_others[step])
        results.append(mlp_slot(wg, wu, wd, bg, bu, *grid.gate(pieces)))
        grid.wait(*results[-1])

    slots = [jnp.concatenate([w_query, keyval_half, w_output.T], axis=1)]
    across, beside, both, wholes = [], [], [], []
    dy_slots, dy_others = [dy_half], []

    def place(step):
        pieces = [slots[step], across[step], beside[step], both[step]]
        spot = jnp.stack([grid.behind(step), grid.y, grid.c]).astype(jnp.int32)
        return place_slot(spot, pieces, wholes, count, (0, query_width + head_dim))

    for step in range(count):
        if step + 1 < count:
            slots.append(grid.next_z(slots[step]))
        else:
            gate_mine = grid.along_z(shards_of[0])
        across.append(grid.over_y(slots[step]))
        beside.append(grid.over_c(slots[step]))
        if step == 0:
            dy_others.append(grid.over_x(dy_half))
            grid.wait(shards_of[0])
        else:
            both.append(grid.over_c(across[step - 1]))
            wholes = place(step - 1)
            grid.wait(*wholes, beside[step])
        if step == 1:
            grid.wait(shards_of[1], normed, x_half, dy_others[0])
        if step == 2:
            grid.wait(shards_of[2], cosine, sine, bias)
        if step + 1 < count:
            grid.wait(slots[step + 1], across[step])
    grid.wait(across[-1])
    both.append(grid.over_c(across[-1]))
    grid.wait(gate_mine)

    up_mine = grid.along_z(shards_of[1])
    gate_across, gate_beside = grid.over_y(gate_mine), grid.over_c(gate_mine)
    wholes = place(count - 1)
    w_qkv, w_out = [whole.reshape(width, -1) for whole in wholes]
    queries = product(normed, w_qkv, F32)
    keyval = queries[:, query_width:]
    front, back = keyval[:, :quarter], keyval[:, quarter : 2 * quarter]
    swapped = jnp.concatenate([back, front], axis=1)
    key = jnp.concatenate(
        [keyval[:, : 2 * quarter] * cosine + swapped * sine, keyval[:, 2 * quarter :]], axis=1
    )
    keyval = jnp.where(grid.x == 0, key, keyval).astype(BF16)
    keyval_other = grid.over_x(keyval)
    grid.wait(keyval_other)
    rot_key = jnp.where(grid.x == 0, keyval, keyval_other)
    values_in = jnp.where(grid.x == 0, keyval_other, keyval)
    shape = (tokens, query_width)
    rot_query, mixed_b = in_vmem(
        partial(attend, scale),
        1.2,
        [(shape, BF16), (shape, BF16)],
        *(queries, rot_key, values_in, cosine, sine, bias),
    )
    mine, other = product_nt(ranks, mixed_b, w_out, micro)
    grid.wait(mine)
    attended = grid.over_x(other)
    grid.wait(up_mine)
    down_mine = grid.along_z(shards_of[2])
    grid.wait(gate_across)
    up_across, up_beside = grid.over_y(up_mine), grid.over_c(up_mine)
    gate_both = grid.over_c(gate_across)
    grid.wait(attended)
    residual, factor_two, normed_two = in_vmem(
        second_norm,
        0.5,
        [(half_shape, F32), ((tokens // 2, 1), F32), (half_shape, BF16)],
        *(x_half, mine, attended, gain_mlp[None]),
    )
    grid.wait(normed_two)
    b_slots, b_others = [normed_two], [grid.over_x(normed_two)]
    b_slots.append(grid.next_z(normed_two))
    dy_slots.append(grid.next_z(dy_half))
    wg = place_all(ranks, [gate_mine, gate_across, gate_beside, gate_both])
    grid.wait(wg, b_others[0])
    grid.wait(down_mine)

    grid.wait(up_across)
    down_across, down_beside = grid.over_y(down_mine), grid.over_c(down_mine)
    grid.wait(b_slots[1], dy_slots[1])
    for step in range(1, count - 1):
        b_slots.append(grid.next_z(b_slots[step]))
        dy_slots.append(grid.next_z(dy_slots[step]))
        b_others.append(grid.over_x(b_slots[step]))
        dy_others.append(grid.over_x(dy_slots[step]))
        if step == 1:
            up_both = grid.over_c(up_across)
            wu = place_all(ranks, [up_mine, up_across, up_beside, up_both])
            grid.wait(wu)
        if step == 2:
            grid.wait(down_across)
            down_both = grid.over_c(down_across)
            wd = place_all(ranks, [down_mine, down_across, down_beside, down_both])
            hidden = wg.shape[1]
            spot = grid.z * hidden
            bg = lax.dynamic_slice_in_dim(b_gate, spot, hidden, 0)
            bu = lax.dynamic_slice_in_dim(b_up, spot, hidden, 0)
            grid.wait(wd, bg, bu)
            results = []
            mlp(0)
        grid.wait(b_slots[step + 1], dy_slots[step + 1])
        grid.wait(b_others[step], dy_others[step])
    b_others.append(grid.over_x(b_slots[-1]))
    dy_others.append(grid.over_x(dy_slots[-1]))
    mlp(1)

    for step in range(2, count - 1):
        mlp(step)
    grid.wait(b_others[-1], dy_others[-1])
    back_got = [None, grid.over_x(results[1][4])]
    mlp(count - 1)
    inner_slots, gate_slots, up_slots, back_own, back_other, sums = zip(*results)
    dy_all = [piece for two in zip(dy_slots, dy_others) for piece in two]
    b_all = [piece for two in zip(b_slots, b_others) for piece in two]
    down_keep, down_send = product_rows(ranks, grid.gate(dy_all), [inner_slots], count, 2)[0]
    grid.wait(down_keep, back_got[1])
    held = add(back_own[1], back_got[1])
    grid.wait(held)
    back_next = grid.next_z(held)
    back_got.append(grid.over_x(back_other[2]))
    down_got = [grid.over_c(send) for send in down_send]
    grid.wait(*down_got)
    down_away, down_stay = own_rows(ranks, grid.gate(down_keep), down_got)
    grid.wait(down_away)
    down_back = grid.over_y(down_away)
    (gate_keep, gate_send), (up_keep, up_send) = product_rows(
        ranks, grid.gate(b_all), [gate_slots, up_slots], count
    )
    grid.wait(gate_keep, back_got[2], back_next)
    held = add(back_own[2], back_got[2], back_next)
    grid.wait(held)
    back_next = grid.next_z(held)
    back_got.append(grid.over_x(back_other[3]))
    gate_got = [grid.over_c(send) for send in gate_send]
    grid.wait(*gate_got)
    gate_away, gate_stay = own_rows(ranks, grid.gate(gate_keep), gate_got)
    grid.wait(gate_away)
    for step in range(3, count):
        grid.wait(back_got[step], back_next)
        held = add(back_own[step], back_got[step], back_next)
        grid.wait(held)
        back_next = grid.next_z(held)
        back_got.append(grid.over_x(back_other[(step + 1) % count]))
    up_got = [grid.over_c(send) for send in up_send]
    grid.wait(down_back)
    gate_back = grid.over_y(gate_away)
    down_rows = plus(grid.gate(down_stay), down_back)
    grid.wait(down_rows)
    down_parts = grid.along_z(down_rows)
    grid.wait(*up_got)
    up_away, up_stay = own_rows(ranks, grid.gate(up_keep), up_got, 2)
    grid.wait(*up_away)
    grid.wait(back_got[-1], back_next)
    grad_resid, grad_resid_b, gain_mlp_term, outputs = in_vmem(
        second_norm_back,
        0.5,
        [(half_shape, F32), (half_shape, BF16), ((1, width), F32), (half_shape, BF16)],
        *(back_own[0], back_got[-1], back_next, residual, factor_two),
        *(gain_mlp[None], b_down[None], dy_half),
    )
    grid.wait(grad_resid_b)
    grad_resid_other = grid.over_x(grad_resid_b)
    grid.wait(gate_back)
    up_back = [grid.over_y(up_away[0])]
    gate_rows = plus(grid.gate(gate_stay), gate_back)
    grid.wait(gate_rows, grad_resid_other)

    grad_resid_b = join(grad_resid_b, grad_resid_other)
    grad_mixed = product(grid.gate(grad_resid_b), w_out, BF16)
    shape_kv = (tokens, head_dim)
    grad_query, grad_key, grad_values = in_vmem(
        partial(attend_back, scale),
        0.5,
        [(shape, BF16), (shape_kv, F32), (shape_kv, F32)],
        *(grad_mixed, rot_query, rot_key, values_in, cosine, sine, bias),
    )
    grid.wait(grad_query)
    grad_own = jnp.where(grid.x == 0, grad_key, grad_values)
    grad_other = grid.over_x(jnp.where(grid.x == 0, grad_values, grad_key))
    grid.wait(up_back[0])
    up_back.append(grid.over_y(up_away[1]))
    query_keep, query_send = product_rows(ranks, [grid.gate(normed)], [[grad_query]], count)[0]
    grid.wait(grad_other, query_keep, up_back[1])
    query_got = [grid.over_c(send) for send in query_send]
    grid.wait(down_parts)
    gate_parts = grid.along_z(gate_rows)
    grid.wait(*query_got)
    query_away, query_stay = own_rows(ranks, grid.gate(query_keep), query_got, 2)
    grid.wait(*query_away)
    query_back = [grid.over_y(query_away[0])]
    up_rows = plus(grid.gate(up_stay), *up_back)
    grid.wait(up_rows)
    grad_keyval = (grad_own + grad_other).astype(BF16)
    out_keep, out_send = product_rows(
        ranks, [grid.gate(grad_resid_b), normed], [[mixed_b, grad_keyval]], count, beside=True
    )[0]
    grid.wait(out_keep)
    mine, other = product_nt(
        ranks, jnp.concatenate([grad_query, grid.gate(grad_keyval)], axis=1), w_qkv, micro
    )
    grid.wait(mine)
    grad_normed = grid.over_x(other)
    out_got = [grid.over_c(send) for send in out_send]
    grid.wait(gate_parts)
    up_parts = grid.along_z(up_rows)
    grid.wait(query_back[0])
    query_back.append(grid.over_y(query_away[1]))
    grid.wait(*out_got)
    out_away, out_stay = own_rows(ranks, grid.gate(out_keep), out_got, 2)
    grid.wait(*out_away)
    grid.wait(query_back[1])
    out_back = [grid.over_y(out_away[0])]
    query_rows = plus(grid.gate(query_stay), *query_back)
    query_held = ring_sum(grid, query_rows, None, 1)
    grid.wait(query_held)
    query_held = grid.next_z(query_held)
    grid.wait(grad_normed)
    grad_input, gain_attn_term = in_vmem(
        first_norm_back,
        0.5,
        [(half_shape, BF16), ((1, width), F32)],
        *(mine, grad_normed, x_half, factor_half, gain_attn[None], grid.gate(grad_resid)),
    )
    grid.wait(grad_input)
    narrow = jnp.concatenate(
        [gain_attn_term, gain_mlp_term, jnp.sum(dy_half.astype(F32), axis=0)[None]]
    )
    grid.wait(narrow)
    narrow_other = grid.over_x(narrow)
    outputs_other = grid.over_x(outputs)

    ffn = b_gate.shape[0]
    wide = jnp.zeros((2, ffn), F32)
    wide = lax.dynamic_update_slice(wide, sum(sums), (0, spot)).reshape(-1)
    grid.wait(narrow_other)
    small = jnp.concatenate([(narrow + narrow_other).reshape(-1), wide])
    small_other = grid.over_c(small)
    down_grad = collect_columns(grid.gate(down_parts), True)
    grid.wait(down_grad, small_other)
    small = small + small_other
    grid.wait(small)
    grid.wait(up_parts)
    grid.wait(query_held)
    query_held = ring_sum(grid, query_rows, query_held, 2)
    grid.wait(query_held)
    query_held = grid.next_z(query_held)
    grid.wait(out_back[0])
    out_back.append(grid.over_y(out_away[1]))
    small_all = [small] + [grid.next_z(small, step) for step in range(1, count)]
    gate_grad = collect_columns(grid.gate(gate_parts))
    grid.wait(gate_grad)
    for step in range(3, count):
        grid.wait(query_held)
        query_held = ring_sum(grid, query_rows, query_held, step)
        grid.wait(query_held)
        query_held = grid.next_z(query_held)
    grid.wait(*out_back)
    out_rows = plus(grid.gate(out_stay), *out_back)
    out_held = ring_sum(grid, out_rows, None, 1)
    grid.wait(out_held)
    out_held = grid.next_z(out_held)
    grid.wait(outputs_other, *small_all)
    places = [lax.rem(grid.z - z + count, count) for z in range(count)]
    small = sum(pick(small_all, place) for place in places)
    grid.wait(small)
    small_other = grid.over_y(small)
    grad_input_other = grid.over_x(grad_input)
    for step in range(2, count):
        grid.wait(out_held)
        out_held = ring_sum(grid, out_rows, out_held, step)
        grid.wait(out_held)
        out_held = grid.next_z(out_held)
    query_grad = ring_sum(grid, query_rows, grid.gate(query_held), count)
    grid.wait(query_grad)
    up_grad = collect_columns(grid.gate(up_parts))
    grid.wait(up_grad, small_other)
    small = small + small_other
    grid.wait(out_held)
    out_held = ring_sum(grid, out_rows, out_held, count)
    grid.wait(out_held)
    keyval_grad = out_held[:, query_width:]
    keyval_other = grid.over_x(keyval_grad)
    out_grad = out_held[:, :query_width].T
    keyval_grad = pair(grid.x, keyval_grad, keyval_other, 1)
    keyval_grad = keyval_grad.reshape(keyval_grad.shape[0], 2 * head_dim)
    return (
        join(outputs, outputs_other).reshape(inputs.shape),
        join(grad_input, grad_input_other).reshape(inputs.shape),
        small[:width],
        query_grad,
        keyval_grad,
        out_grad,
        small[width : 2 * width],
        gate_grad,
        small[3 * width : 3 * width + ffn],
        up_grad,
        small[3 * width + ffn :],
        down_grad,
        small[2 * width : 3 * width],
    )


def solution(mesh):
    in_specs = (
        P(None, "dp", None),
        P(),
        P("dp", "mp"),
        P("dp", None),
        P("mp", "dp"),
        P(),
        P("dp", "mp"),
        P("mp"),
        P("dp", "mp"),
        P("mp"),
        P("mp", "dp"),
        P(),
        P(None, "dp", None),
        P(None, "dp", None),
    )
    out_specs = (
        P(None, "dp", None),
        P(None, "dp", None),
        P(),
        P("dp", "mp"),
        P("dp", None),
        P("mp", "dp"),
        P(),
        P("dp", "mp"),
        P("mp"),
        P("dp", "mp"),
        P("mp"),
        P("mp", "dp"),
        P(),
    )
    body = partial(shards, total=mesh.shape["dp"])
    return jax.shard_map(body, mesh=mesh, in_specs=in_specs, out_specs=out_specs, check_vma=False)
```
